32 devices in a mesh: groups: 2 (over y), tok: 2 (over x), kin: 2 (over core), nout: 4 (over z).
Axes of the slice: x: 2, y: 2, z: 4, core: 2. Of those that a mesh axis runs over, the one named last changes fastest.
Arguments:
- tokens: bfloat16 [64, 6144], P(('groups', 'tok', 'nout'), 'kin'), parts along dimension 0, may hold values from -6 to 6
- weight_in: bfloat16 [6144, 12288], P(('kin', 'tok'), 'nout'), may hold values from -0.078125 to 0.078125
- bias_in: float32 [12288], P('nout'), may hold values from -3 to 3
- weight_out: bfloat16 [12288, 6144], P('nout', ('kin', 'tok')), may hold values from -0.0546875 to 0.0546875
- bias_out: float32 [6144], P('kin'), may hold values from -3 to 3
- grad_out: bfloat16 [64, 6144], P(('groups', 'tok', 'nout'), 'kin'), parts along dimension 0, may hold values from -6 to 6
Outputs:
- output_rows: bfloat16 [64, 6144], P(('groups', 'tok', 'nout'), 'kin'), parts along dimension 0
- grad_tokens: bfloat16 [64, 6144], P(('groups', 'tok', 'nout'), 'kin'), parts along dimension 0
- weight_in_grad: bfloat16 [12288, 12288], P(('groups', 'kin', 'tok'), 'nout'), parts along dimension 0
- weight_out_grad: bfloat16 [24576, 6144], P(('groups', 'nout'), ('kin', 'tok')), parts along dimension 0
- bias_in_grad: float32 [24576], P(('groups', 'nout')), parts along dimension 0
- bias_out_grad: float32 [12288], P(('groups', 'kin')), parts along dimension 0
The draws below stay inside these ranges and needn't reach their ends.
There are 2 independent parts, one for each index of `groups`. The reference program is written for one: setup_inputs(seed, part) draws one part's arguments, and reference() takes and returns one part's arrays. A program takes and returns all parts, laid end to end along the dimension named above; an argument that names none is the same for every part. Nothing has to cross between parts.
All inputs are finite; a program needn't handle non-finite values.
Results may differ from the reference program's by a relative error of at most 0.018.
Values may be sent and summed in bfloat16 or wider, within the bound.
No kernel may reach another device: no remote copies, remote signals or barrier semaphores. Data moves between devices by JAX's collectives and lax.ppermute only.
A program may use at most 192 MiB of HBM per device.

```python
import jax
import jax.numpy as jnp
from jax import lax

D = 6144
FW = 12288
TOKENS = 32
N_NOUT = 4


def level_of(stream_key, extent, shards, smallest, largest):
    def one(axis_at, parts):
        heights = jax.random.uniform(jax.random.fold_in(jax.random.fold_in(stream_key, 6), axis_at), (parts,), jnp.float32, smallest / len(shards), largest / len(shards))
        return jnp.repeat(jnp.exp(heights), extent[axis_at] // parts).reshape((-1,) + (1,) * (len(extent) - axis_at - 1))

    level = one(*shards[0])
    for cut in shards[1:]:
        level = level * one(*cut)
    return level


def centred(key, extent, scale, limit, shards=(), kind=jnp.bfloat16):
    entries = scale * jax.random.normal(key, extent, jnp.float32)
    if shards:
        entries = entries * level_of(key, extent, shards, -0.22, 0.18)
    return jnp.clip(entries, -limit, limit).astype(kind)


def setup_inputs(seed: int = 0, part: int = 0) -> dict:
    key_of = jax.random.split(jax.random.key(seed), 7)
    own_keys = jax.random.split(jax.random.fold_in(key_of[6], part), 7)
    return {
        "tokens": centred(own_keys[0], (TOKENS, D), 1.0, 6.0, ((0, 8), (1, 2))),
        "weight_in": centred(key_of[1], (D, FW), D ** -0.5, 0.078125, ((0, 4), (1, 4))),
        "bias_in": centred(key_of[2], (FW,), 0.5, 3.0, ((0, 4),), jnp.float32),
        "weight_out": centred(key_of[3], (FW, D), FW ** -0.5, 0.0546875, ((0, 4), (1, 4))),
        "bias_out": centred(key_of[4], (D,), 0.5, 3.0, ((0, 2),), jnp.float32),
        "grad_out": centred(own_keys[5], (TOKENS, D), 1.0, 6.0, ((0, 8), (1, 2))),
    }


inv_root_two = 0.7071067811865476
inv_root_two_pi = 0.3989422804014327


def gelu_parts(hidden):
    normal_cdf = 0.5 * (1.0 + lax.erf(hidden * inv_root_two))
    density = jnp.exp(-0.5 * hidden * hidden) * inv_root_two_pi
    return hidden * normal_cdf, normal_cdf + hidden * density


def rounded(value):
    return lax.optimization_barrier(value.astype(jnp.bfloat16)).astype(jnp.float32)


def reference(tokens, weight_in, bias_in, weight_out, bias_out, grad_out):
    block_width = FW // N_NOUT
    pre_act = jnp.dot(tokens, weight_in, preferred_element_type=jnp.float32) + bias_in
    activated_full, slopes = gelu_parts(pre_act)
    activated = activated_full.astype(jnp.bfloat16)
    act_blocks = activated.reshape(TOKENS, N_NOUT, block_width).transpose(1, 0, 2)
    out_blocks = weight_out.reshape(N_NOUT, block_width, D)

    def add_out(running, pair):
        act_part, weight_part = pair
        term = jnp.dot(act_part, weight_part, preferred_element_type=jnp.float32)
        return running + rounded(term), None

    out_sum = lax.scan(add_out, jnp.zeros((TOKENS, D), jnp.float32), (act_blocks, out_blocks))[0]
    output_rows = (out_sum + bias_out).astype(jnp.bfloat16)
    grad_act = jnp.dot(grad_out, weight_out.T, preferred_element_type=jnp.float32)
    grad_pre = grad_act * slopes
    bias_in_grad = jnp.sum(grad_pre, axis=0)
    grad_half = grad_pre.astype(jnp.bfloat16)
    grad_blocks = grad_half.reshape(TOKENS, N_NOUT, block_width).transpose(1, 0, 2)
    in_blocks = weight_in.reshape(D, N_NOUT, block_width).transpose(1, 0, 2)

    def add_in(running, pair):
        grad_part, weight_part = pair
        term = jnp.dot(grad_part, weight_part.T, preferred_element_type=jnp.float32)
        return running + rounded(term), None

    in_sum = lax.scan(add_in, jnp.zeros((TOKENS, D), jnp.float32), (grad_blocks, in_blocks))[0]
    grad_tokens = in_sum.astype(jnp.bfloat16)
    weight_in_grad = jnp.dot(tokens.T, grad_half, preferred_element_type=jnp.float32).astype(jnp.bfloat16)
    weight_out_grad = jnp.dot(activated.T, grad_out, preferred_element_type=jnp.float32).astype(jnp.bfloat16)
    bias_out_grad = jnp.sum(grad_out.astype(jnp.float32), axis=0)
    return output_rows, grad_tokens, weight_in_grad, weight_out_grad, bias_in_grad, bias_out_grad
```

```python
import jax
import jax.numpy as jnp
from jax import lax
from jax.sharding import PartitionSpec as P

inv_root_two = 0.7071067811865476
inv_root_two_pi = 0.3989422804014327


def gelu_parts(hidden):
    normal_cdf = 0.5 * (1.0 + lax.erf(hidden * inv_root_two))
    density = jnp.exp(-0.5 * hidden * hidden) * inv_root_two_pi
    return (hidden * normal_cdf, normal_cdf + hidden * density)


def dot(left, right, left_dim, right_dim):
    return lax.dot_general(
        left, right, (((left_dim,), (right_dim,)), ((), ())), preferred_element_type=jnp.float32
    )


def exchange(chunks, axes):
    return lax.all_to_all(chunks, axes, split_axis=0, concat_axis=0, tiled=True)


def make(mesh):
    nt, nk, nn = mesh.shape["tok"], mesh.shape["kin"], mesh.shape["nout"]
    spread, square = nt * nn, nk * nt

    def on_device(tokens, weight_in, bias_in, weight_out, bias_out, grad_out):
        rows, cols = tokens.shape
        wide, hid = weight_in.shape
        part = hid // square
        pair = 2 * rows
        total = pair * spread

        mine = jnp.concatenate([tokens, grad_out], axis=0)
        by_owner = mine.reshape(pair, nt, wide).transpose(1, 0, 2)
        chunks = jnp.broadcast_to(by_owner[:, None], (nt, nn, pair, wide))
        mixed = exchange(chunks.reshape(spread, pair, wide), ("tok", "nout")).reshape(total, wide)
        is_fwd = (lax.broadcasted_iota(jnp.int32, (total, 1), 0) % pair) < rows

        col_sums = jnp.sum(jnp.where(is_fwd, 0.0, mixed.astype(jnp.float32)), axis=0)
        bias_out_grad = lax.all_gather(col_sums, "tok", axis=0, tiled=True)

        partial = jnp.where(is_fwd, dot(mixed, weight_in, 1, 0), dot(mixed, weight_out, 1, 1))
        partial = partial.astype(jnp.bfloat16).reshape(total, square, part).transpose(1, 0, 2)
        got = exchange(partial, ("kin", "tok"))
        summed = jnp.sum(got.astype(jnp.float32), axis=0).reshape(spread, 2, rows, part)
        at = lax.axis_index(("kin", "tok"))
        pre_act = summed[:, 0] + lax.dynamic_slice_in_dim(bias_in, at * part, part)
        activated, slopes = gelu_parts(pre_act)
        grad_pre = summed[:, 1] * slopes
        both = jnp.stack([activated, grad_pre], axis=1).astype(jnp.bfloat16).reshape(total, part)
        both = exchange(jnp.broadcast_to(both[None], (square, total, part)), ("kin", "tok"))
        both = both.transpose(1, 0, 2).reshape(total, hid)

        split = both.reshape(spread, 2, rows, hid)
        act = split[:, 0].reshape(spread * rows, hid)
        grad_half = split[:, 1].reshape(spread * rows, hid)
        split = mixed.reshape(spread, 2, rows, wide)
        x_cols = split[:, 0].reshape(spread * rows, wide)
        dy_cols = split[:, 1].reshape(spread * rows, wide)
        bias_in_grad = jnp.sum(grad_half.astype(jnp.float32), axis=0)

        block = jnp.stack(
            [
                dot(act, weight_out, 1, 0).reshape(spread, rows, wide),
                dot(grad_half, weight_in, 1, 1).reshape(spread, rows, wide),
            ],
            axis=1,
        )
        block = block.astype(jnp.bfloat16).reshape(spread, pair, wide)
        back = exchange(block, ("tok", "nout")).reshape(nt, nn, pair, wide)
        weight_in_grad = dot(x_cols, grad_half, 0, 0).astype(jnp.bfloat16)
        weight_out_grad = dot(act, dy_cols, 0, 0).astype(jnp.bfloat16)
        final = jnp.sum(back.astype(jnp.float32), axis=1).transpose(1, 0, 2).reshape(pair, cols)
        output_rows = (final[:rows] + bias_out).astype(jnp.bfloat16)
        grad_tokens = final[rows:].astype(jnp.bfloat16)
        return (output_rows, grad_tokens, weight_in_grad, weight_out_grad, bias_in_grad, bias_out_grad)

    return on_device


def solution(mesh):
    return jax.shard_map(
        make(mesh),
        mesh=mesh,
        in_specs=(
            P(("groups", "tok", "nout"), "kin"),
            P(("kin", "tok"), "nout"),
            P("nout"),
            P("nout", ("kin", "tok")),
            P("kin"),
            P(("groups", "tok", "nout"), "kin"),
        ),
        out_specs=(
            P(("groups", "tok", "nout"), "kin"),
            P(("groups", "tok", "nout"), "kin"),
            P(("groups", "kin", "tok"), "nout"),
            P(("groups", "nout"), ("kin", "tok")),
            P(("groups", "nout")),
            P(("groups", "kin")),
        ),
        check_vma=False,
    )
```

```python
import jax
import jax.numpy as jnp
from jax import lax
from jax.sharding import PartitionSpec as P

inv_root_two = 0.7071067811865476
inv_root_two_pi = 0.3989422804014327


def gelu_parts(hidden):
    normal_cdf = 0.5 * (1.0 + lax.erf(hidden * inv_root_two))
    density = jnp.exp(-0.5 * hidden * hidden) * inv_root_two_pi
    return (hidden * normal_cdf, normal_cdf + hidden * density)


def dot(left, right, left_dim, right_dim):
    return lax.dot_general(
        left, right, (((left_dim,), (right_dim,)), ((), ())), preferred_element_type=jnp.float32
    )


def exchange(chunks, axes, sizes):
    count = chunks.shape[0]
    if count > 8:
        return lax.all_to_all(chunks, axes, split_axis=0, concat_axis=0, tiled=True)
    me = lax.axis_index(axes)
    got = [lax.dynamic_index_in_dim(chunks, me, 0, keepdims=False)]
    in_order = tuple(name for name in ("tok", "kin", "nout") if name in axes)

    def place(i):
        low, high = i % sizes[1], i // sizes[1]
        return i if in_order == axes else low * sizes[0] + high

    for apart in range(1, count):
        sent = lax.dynamic_index_in_dim(chunks, me ^ apart, 0, keepdims=False)
        pairs = [(place(i), place(i ^ apart)) for i in range(count)]
        got.append(lax.ppermute(sent, in_order, pairs))
    return jnp.take(jnp.stack(got), me ^ jnp.arange(count), axis=0, mode="clip")


def make(mesh):
    nt, nk, nn = mesh.shape["tok"], mesh.shape["kin"], mesh.shape["nout"]
    spread, square = nt * nn, nk * nt

    def on_device(tokens, weight_in, bias_in, weight_out, bias_out, grad_out):
        rows, cols = tokens.shape
        wide, hid = weight_in.shape
        part = hid // square
        pair = 2 * rows
        total = pair * spread

        mine = jnp.concatenate([tokens, grad_out], axis=0)
        by_owner = mine.reshape(pair, nt, wide).transpose(1, 0, 2)
        chunks = jnp.broadcast_to(by_owner[:, None], (nt, nn, pair, wide))
        mixed = exchange(chunks.reshape(spread, pair, wide), ("tok", "nout"), (nt, nn)).reshape(total, wide)
        is_fwd = (lax.broadcasted_iota(jnp.int32, (total, 1), 0) % pair) < rows

        col_sums = jnp.sum(jnp.where(is_fwd, 0.0, mixed.astype(jnp.float32)), axis=0)
        bias_out_grad = lax.all_gather(col_sums, "tok", axis=0, tiled=True)

        partial = jnp.where(is_fwd, dot(mixed, weight_in, 1, 0), dot(mixed, weight_out, 1, 1))
        partial = partial.astype(jnp.bfloat16).reshape(total, square, part).transpose(1, 0, 2)
        got = exchange(partial, ("kin", "tok"), (nk, nt))
        summed = jnp.sum(got.astype(jnp.float32), axis=0).reshape(spread, 2, rows, part)
        at = lax.axis_index(("kin", "tok"))
        pre_act = summed[:, 0] + lax.dynamic_slice_in_dim(bias_in, at * part, part)
        activated, slopes = gelu_parts(pre_act)
        grad_pre = summed[:, 1] * slopes
        both = jnp.stack([activated, grad_pre], axis=1).astype(jnp.bfloat16).reshape(total, part)
        both = exchange(jnp.broadcast_to(both[None], (square, total, part)), ("kin", "tok"), (nk, nt))
        both = both.transpose(1, 0, 2).reshape(total, hid)

        split = both.reshape(spread, 2, rows, hid)
        act = split[:, 0].reshape(spread * rows, hid)
        grad_half = split[:, 1].reshape(spread * rows, hid)
        split = mixed.reshape(spread, 2, rows, wide)
        x_cols = split[:, 0].reshape(spread * rows, wide)
        dy_cols = split[:, 1].reshape(spread * rows, wide)
        bias_in_grad = jnp.sum(grad_half.astype(jnp.float32), axis=0)

        block = jnp.stack(
            [
                dot(act, weight_out, 1, 0).reshape(spread, rows, wide),
                dot(grad_half, weight_in, 1, 1).reshape(spread, rows, wide),
            ],
            axis=1,
        )
        block = block.astype(jnp.bfloat16).reshape(spread, pair, wide)
        back = exchange(block, ("tok", "nout"), (nt, nn)).reshape(nt, nn, pair, wide)
        weight_in_grad = dot(x_cols, grad_half, 0, 0).astype(jnp.bfloat16)
        weight_out_grad = dot(act, dy_cols, 0, 0).astype(jnp.bfloat16)
        final = jnp.sum(back.astype(jnp.float32), axis=1).transpose(1, 0, 2).reshape(pair, cols)
        output_rows = (final[:rows] + bias_out).astype(jnp.bfloat16)
        grad_tokens = final[rows:].astype(jnp.bfloat16)
        return (output_rows, grad_tokens, weight_in_grad, weight_out_grad, bias_in_grad, bias_out_grad)

    return on_device


def solution(mesh):
    return jax.shard_map(
        make(mesh),
        mesh=mesh,
        in_specs=(
            P(("groups", "tok", "nout"), "kin"),
            P(("kin", "tok"), "nout"),
            P("nout"),
            P("nout", ("kin", "tok")),
            P("kin"),
            P(("groups", "tok", "nout"), "kin"),
        ),
        out_specs=(
            P(("groups", "tok", "nout"), "kin"),
            P(("groups", "tok", "nout"), "kin"),
            P(("groups", "kin", "tok"), "nout"),
            P(("groups", "nout"), ("kin", "tok")),
            P(("groups", "nout")),
            P(("groups", "kin")),
        ),
        check_vma=False,
    )
```

```python
import jax
import jax.numpy as jnp
from jax import lax
from jax.experimental import pallas as pl
from jax.experimental.pallas import tpu as pltpu
from jax.sharding import PartitionSpec as P

inv_root_two = 0.7071067811865476
inv_root_two_pi = 0.3989422804014327


def gelu_parts(hidden):
    normal_cdf = 0.5 * (1.0 + lax.erf(hidden * inv_root_two))
    density = jnp.exp(-0.5 * hidden * hidden) * inv_root_two_pi
    return (hidden * normal_cdf, normal_cdf + hidden * density)


def dot(left, right, left_dim, right_dim):
    return lax.dot_general(
        left, right, (((left_dim,), (right_dim,)), ((), ())), preferred_element_type=jnp.float32
    )


def load_body(*refs):
    count = (len(refs) - 1) // 2
    sems = refs[-1]
    copies = [
        pltpu.make_async_copy(refs[i], refs[count + i], sems.at[i]) for i in range(count)
    ]
    for copy in copies:
        copy.start()
    for copy in copies:
        copy.wait()


def load_weights(*weights):
    size = sum(w.size * w.dtype.itemsize for w in weights)
    return pl.pallas_call(
        load_body,
        out_shape=[pltpu.VMEM(w.shape, w.dtype) for w in weights],
        in_specs=[pl.BlockSpec(memory_space=pl.ANY)] * len(weights),
        out_specs=[pl.BlockSpec(memory_space=pltpu.VMEM)] * len(weights),
        scratch_shapes=[pltpu.SemaphoreType.DMA((len(weights),))],
        cost_estimate=pl.CostEstimate(flops=0, bytes_accessed=2 * size, transcendentals=0),
        compiler_params=pltpu.CompilerParams(vmem_limit_bytes=1 << 20),
        name="load_weights",
    )(*weights)


def make(mesh):
    nt, nk, nn = mesh.shape["tok"], mesh.shape["kin"], mesh.shape["nout"]
    spread = nt * nn
    swap = [(0, 1), (1, 0)]

    def on_device(tokens, weight_in, bias_in, weight_out, bias_out, grad_out):
        rows, cols = tokens.shape
        wide, hid = weight_in.shape
        half = hid // nk
        pair = 2 * rows
        total = pair * spread
        core = lax.axis_index("kin")

        mine = jnp.concatenate([tokens, grad_out], axis=0)
        by_owner = mine.reshape(pair, nt, wide).transpose(1, 0, 2)
        chunks = jnp.broadcast_to(by_owner[:, None], (nt, nn, pair, wide))
        chunks = chunks.reshape(spread, pair, wide)
        mixed = lax.all_to_all(chunks, ("tok", "nout"), split_axis=0, concat_axis=0, tiled=True)
        mixed = mixed.reshape(total, wide)
        w_in, w_out = load_weights(weight_in, weight_out)
        is_fwd = (lax.broadcasted_iota(jnp.int32, (total, 1), 0) % pair) < rows

        col_sums = jnp.sum(jnp.where(is_fwd, 0.0, mixed.astype(jnp.float32)), axis=0)

        partial = jnp.where(is_fwd, dot(mixed, w_in, 1, 0), dot(mixed, w_out, 1, 1))
        partial = partial.astype(jnp.bfloat16)
        own = lax.dynamic_slice_in_dim(partial, core * half, half, 1)
        sent = lax.dynamic_slice_in_dim(partial, (1 - core) * half, half, 1)
        own = own.astype(jnp.float32) + lax.ppermute(sent, "kin", swap).astype(jnp.float32)
        own = own.astype(jnp.bfloat16)
        if nt == 2:
            other = lax.ppermute(own, "tok", swap)
            summed = own.astype(jnp.float32) + other.astype(jnp.float32)
            other_sums = lax.ppermute(col_sums, "tok", swap)
            first = lax.axis_index("tok") == 0
            bias_out_grad = jnp.concatenate(
                [jnp.where(first, col_sums, other_sums), jnp.where(first, other_sums, col_sums)]
            )
        else:
            summed = jnp.sum(lax.all_gather(own, "tok", axis=0).astype(jnp.float32), axis=0)
            bias_out_grad = lax.all_gather(col_sums, "tok", axis=0, tiled=True)
        summed = summed.reshape(spread, 2, rows, half)
        pre_act = summed[:, 0] + lax.dynamic_slice_in_dim(bias_in, core * half, half)
        activated, slopes = gelu_parts(pre_act)
        grad_pre = summed[:, 1] * slopes
        both = jnp.stack([activated, grad_pre], axis=1).astype(jnp.bfloat16).reshape(total, half)
        far = lax.ppermute(both, "kin", swap)
        low = jnp.where(core == 0, both, far)
        high = jnp.where(core == 0, far, both)
        both = jnp.concatenate([low, high], axis=1)

        split = both.reshape(spread, 2, rows, hid)
        act = split[:, 0].reshape(spread * rows, hid)
        grad_half = split[:, 1].reshape(spread * rows, hid)
        split = mixed.reshape(spread, 2, rows, wide)
        x_cols = split[:, 0].reshape(spread * rows, wide)
        dy_cols = split[:, 1].reshape(spread * rows, wide)
        bias_in_grad = jnp.sum(grad_half.astype(jnp.float32), axis=0)

        block = jnp.stack(
            [
                dot(act, w_out, 1, 0).reshape(spread, rows, wide),
                dot(grad_half, w_in, 1, 1).reshape(spread, rows, wide),
            ],
            axis=1,
        )
        block = block.astype(jnp.bfloat16).reshape(spread, pair, wide)
        back = lax.all_to_all(block, ("tok", "nout"), split_axis=0, concat_axis=0, tiled=True)
        back = back.reshape(nt, nn, pair, wide)
        weight_in_grad = dot(x_cols, grad_half, 0, 0).astype(jnp.bfloat16)
        weight_out_grad = dot(act, dy_cols, 0, 0).astype(jnp.bfloat16)
        final = jnp.sum(back.astype(jnp.float32), axis=1).transpose(1, 0, 2).reshape(pair, cols)
        output_rows = (final[:rows] + bias_out).astype(jnp.bfloat16)
        grad_tokens = final[rows:].astype(jnp.bfloat16)
        return (output_rows, grad_tokens, weight_in_grad, weight_out_grad, bias_in_grad, bias_out_grad)

    return on_device


def solution(mesh):
    return jax.shard_map(
        make(mesh),
        mesh=mesh,
        in_specs=(
            P(("groups", "tok", "nout"), "kin"),
            P(("kin", "tok"), "nout"),
            P("nout"),
            P("nout", ("kin", "tok")),
            P("kin"),
            P(("groups", "tok", "nout"), "kin"),
        ),
        out_specs=(
            P(("groups", "tok", "nout"), "kin"),
            P(("groups", "tok", "nout"), "kin"),
            P(("groups", "kin", "tok"), "nout"),
            P(("groups", "nout"), ("kin", "tok")),
            P(("groups", "nout")),
            P(("groups", "kin")),
        ),
        check_vma=False,
    )
```

```python
import functools

import jax
import jax.numpy as jnp
from jax import lax
from jax.experimental import pallas as pl
from jax.experimental.pallas import tpu as pltpu
from jax.sharding import PartitionSpec as P

inv_root_two = 0.7071067811865476
inv_root_two_pi = 0.3989422804014327

MIB = 1 << 20
whole = pl.BlockSpec(memory_space=pltpu.VMEM)


def gelu_parts(hidden):
    normal_cdf = 0.5 * (1.0 + lax.erf(hidden * inv_root_two))
    density = jnp.exp(-0.5 * hidden * hidden) * inv_root_two_pi
    return (hidden * normal_cdf, normal_cdf + hidden * density)


def dot(left, right, left_dim, right_dim):
    return lax.dot_general(
        left, right, (((left_dim,), (right_dim,)), ((), ())), preferred_element_type=jnp.float32
    )


def tile_of(size, most):
    return max(t for t in range(128, most + 1, 128) if size % t == 0)


def cost(flops, moved):
    return pl.CostEstimate(flops=flops, bytes_accessed=moved, transcendentals=0)


def call(body, name, outs, grant=4 * MIB, flops=0, moved=0, scratch=(), resident=True):
    shapes = [pltpu.VMEM(o.shape, o.dtype) if resident else o for o in outs]
    return functools.partial(
        pl.pallas_call,
        body,
        out_shape=shapes,
        out_specs=[whole] * len(outs),
        scratch_shapes=list(scratch),
        cost_estimate=cost(flops, moved),
        compiler_params=pltpu.CompilerParams(vmem_limit_bytes=grant),
        name=name,
    )


def kept(array):
    return pltpu.with_memory_space_constraint(array, pltpu.VMEM)


def in_hbm(array):
    return pltpu.with_memory_space_constraint(array, pltpu.HBM)


def forward_rows(shape, rows):
    return lax.rem(lax.broadcasted_iota(jnp.int32, shape, 0), 2 * rows) < rows


def ordered(core, own, far):
    return jnp.concatenate([jnp.where(core == 0, own, far), jnp.where(core == 0, far, own)], axis=0)


def load_body(in_hbm, out_hbm, after_ref, in_ref, out_ref, sems):
    first = pltpu.make_async_copy(in_hbm, in_ref, sems.at[0])
    second = pltpu.make_async_copy(out_hbm, out_ref, sems.at[1])
    first.start()
    second.start()
    first.wait()
    second.wait()


def pair_body(own_ref, got_ref, out_ref):
    out_ref[...] = ordered(lax.axis_index("tok"), own_ref[...], got_ref[...])


def partial_body(rows, tile, *refs):
    *piece_refs, w_in_ref, w_out_ref, own_ref, sent_ref, mixed_ref, sums_ref = refs
    mixed = jnp.concatenate([ref[...] for ref in piece_refs], axis=0)
    mixed_ref[...] = mixed
    total = mixed.shape[0]
    hid = w_in_ref.shape[1]
    core = lax.axis_index("kin")
    is_fwd = forward_rows((total, tile), rows)

    @pl.loop(0, hid // tile)
    def _(step):
        at = pl.ds(pl.multiple_of(step * tile, tile), tile)
        forward = dot(mixed, w_in_ref[:, at], 1, 0)
        backward = dot(mixed, w_out_ref[at, :], 1, 1)
        both = jnp.where(is_fwd, forward, backward)
        low, high = both[: total // 2], both[total // 2 :]
        own_ref[:, at] = jnp.where(core == 0, low, high).astype(jnp.bfloat16)
        sent_ref[:, at] = jnp.where(core == 0, high, low).astype(jnp.bfloat16)

    cotangents = jnp.where(forward_rows(mixed.shape, rows), 0.0, mixed.astype(jnp.float32))
    sums_ref[...] = jnp.sum(cotangents, axis=0, keepdims=True)


def add_body(left_ref, right_ref, out_ref):
    out_ref[...] = (
        left_ref[...].astype(jnp.float32) + right_ref[...].astype(jnp.float32)
    ).astype(jnp.bfloat16)


def gelu_body(rows, tile, bias_ref, *refs):
    *part_refs, out_ref = refs
    is_fwd = forward_rows((out_ref.shape[0], tile), rows)

    @pl.loop(0, out_ref.shape[1] // tile)
    def _(step):
        at = pl.ds(pl.multiple_of(step * tile, tile), tile)
        summed = sum(ref[:, at].astype(jnp.float32) for ref in part_refs)
        activated, slopes = gelu_parts(summed + bias_ref[:, at])
        grad_pre = summed * pltpu.roll(slopes, rows, 0)
        out_ref[:, at] = jnp.where(is_fwd, activated, grad_pre).astype(jnp.bfloat16)


def block_body(rows, tile, own_ref, far_ref, w_in_ref, w_out_ref, *out_refs):
    wide = w_in_ref.shape[0]
    both = ordered(lax.axis_index("kin"), own_ref[...], far_ref[...])
    is_fwd = forward_rows((both.shape[0], tile), rows)
    size = both.shape[0] // len(out_refs)

    @pl.loop(0, wide // tile)
    def _(step):
        at = pl.ds(pl.multiple_of(step * tile, tile), tile)
        forward = dot(both, w_out_ref[:, at], 1, 0)
        backward = dot(both, w_in_ref[at, :], 1, 1)
        terms = jnp.where(is_fwd, forward, backward).astype(jnp.bfloat16)
        for i, out_ref in enumerate(out_refs):
            out_ref[:, at] = terms[i * size : (i + 1) * size]


def split_body(rows, own_ref, far_ref, mixed_ref, act_ref, grad_ref, turned_ref, bias_ref):
    both = ordered(lax.axis_index("kin"), own_ref[...], far_ref[...]).astype(jnp.float32)
    is_fwd = forward_rows(both.shape, rows)
    zero = jnp.zeros_like(both)
    act_ref[...] = jnp.where(is_fwd, both, zero).astype(jnp.bfloat16)
    gradient = jnp.where(is_fwd, zero, both)
    grad_ref[...] = gradient.astype(jnp.bfloat16)
    bias_ref[...] = jnp.sum(gradient, axis=0, keepdims=True)
    mixed = mixed_ref[...].astype(jnp.float32)
    to_tokens = pltpu.roll(mixed, mixed.shape[0] - rows, 0)
    to_cotangents = pltpu.roll(mixed, rows, 0)
    is_fwd = forward_rows(mixed.shape, rows)
    turned_ref[...] = jnp.where(is_fwd, to_tokens, to_cotangents).astype(jnp.bfloat16)


def product_body(size, left_ref, right_ref, out_ref):
    at = pl.ds(pl.multiple_of(pl.program_id(0) * size, size), size)
    out_ref[...] = dot(left_ref[:, at], right_ref[...], 0, 0).astype(jnp.bfloat16)


def product(left, right, name, most):
    total, high = left.shape
    wide = right.shape[1]
    size = tile_of(high, most)
    return pl.pallas_call(
        functools.partial(product_body, size),
        grid=(high // size,),
        out_shape=jax.ShapeDtypeStruct((high, wide), jnp.bfloat16),
        in_specs=[whole] * 2,
        out_specs=pl.BlockSpec((size, wide), lambda i: (i, 0)),
        cost_estimate=cost(2 * total * wide * high, 2 * wide * high),
        compiler_params=pltpu.CompilerParams(vmem_limit_bytes=16 * MIB),
        name=name,
    )(kept(left), kept(right))


def sum_body(rows, bias_ref, *refs):
    *term_refs, own_ref, sent_ref = refs
    wide = own_ref.shape[1]
    me = lax.axis_index("tok")
    summed = sum(ref[...].astype(jnp.float32) for ref in term_refs)
    bias = jnp.where(me == 0, bias_ref[:, :wide], bias_ref[:, wide:])
    summed = summed + jnp.where(forward_rows(summed.shape, rows), bias, 0.0)
    low, high = summed[: 2 * rows], summed[2 * rows :]
    own_ref[...] = jnp.where(me == 0, low, high).astype(jnp.bfloat16)
    sent_ref[...] = jnp.where(me == 0, high, low).astype(jnp.bfloat16)


def final_body(rows, own_ref, got_ref, own_sums_ref, got_sums_ref, rows_ref, grad_ref, sums_ref):
    wide = own_ref.shape[1]
    me = lax.axis_index("tok")
    own, got = own_ref[...].astype(jnp.float32), got_ref[...].astype(jnp.float32)
    own_sums, got_sums = own_sums_ref[...], got_sums_ref[...]
    for i in range(2):
        at = pl.ds(i * wide, wide)
        part = jnp.where(me == i, own, got)
        rows_ref[:, at] = part[:rows].astype(jnp.bfloat16)
        grad_ref[:, at] = part[rows:].astype(jnp.bfloat16)
        sums_ref[:, at] = jnp.where(me == i, own_sums, got_sums)


def make(mesh):
    nt, nk, nn = mesh.shape["tok"], mesh.shape["kin"], mesh.shape["nout"]
    small = nt == 2 and nn <= 4
    spread = nt * nn
    swap = [(0, 1), (1, 0)]
    bf16, f32 = jnp.bfloat16, jnp.float32
    like = jax.ShapeDtypeStruct

    def across(array, shift):
        return lax.ppermute(array, "nout", [(i, i ^ shift) for i in range(nn)])

    def on_device(tokens, weight_in, bias_in, weight_out, bias_out, grad_out):
        rows, cols = tokens.shape
        wide, hid = weight_in.shape
        pair = 2 * rows
        total = pair * spread
        half = total // nk
        work = 4 * total * wide * hid

        mine = jnp.concatenate([tokens, grad_out], axis=0)
        if small:
            me = lax.axis_index("tok")
            own = lax.dynamic_slice_in_dim(mine, me * wide, wide, 1)
            sent = lax.dynamic_slice_in_dim(mine, (1 - me) * wide, wide, 1)
            got = lax.ppermute(sent, "tok", swap)
            (tiles,) = call(pair_body, "pair_tiles", [like((nt * pair, wide), bf16)])(
                in_specs=[whole] * 2
            )(kept(own), kept(got))
            pieces = [tiles] + [across(tiles, shift) for shift in range(1, nn)]
        else:
            chunks = mine.reshape(pair, nt, wide).transpose(1, 0, 2)
            tiles = lax.all_to_all(chunks, "tok", split_axis=0, concat_axis=0, tiled=True)
            tiles = tiles.reshape(nt * pair, wide)
            pieces = [lax.all_gather(tiles, "nout", axis=0, tiled=True)]

        w_in, w_out = call(
            load_body,
            "load_weights",
            [weight_in, weight_out],
            grant=MIB,
            moved=8 * wide * hid,
            scratch=[pltpu.SemaphoreType.DMA((2,))],
        )(in_specs=[pl.BlockSpec(memory_space=pltpu.HBM)] * 2 + [pl.BlockSpec(memory_space=pl.ANY)])(
            in_hbm(weight_in), in_hbm(weight_out), tiles
        )

        tile = tile_of(hid, 512)
        own, sent, mixed, sums = call(
            functools.partial(partial_body, rows, tile),
            "partial_sums",
            [like((half, hid), bf16)] * 2 + [like((total, wide), bf16), like((1, wide), f32)],
            grant=8 * MIB,
            flops=work,
        )(in_specs=[whole] * (len(pieces) + 2))(
            *[kept(piece) for piece in pieces], kept(w_in), kept(w_out)
        )
        got = lax.ppermute(sent, "kin", swap)
        (own,) = call(add_body, "add_cores", [like((half, hid), bf16)])(in_specs=[whole] * 2)(
            kept(own), kept(got)
        )
        if nt == 2:
            others = [lax.ppermute(own, "tok", swap)]
            own_others = [own] + others
        else:
            gathered = lax.all_gather(own, "tok", axis=0)
            own_others = [gathered[i] for i in range(nt)]
        (both,) = call(
            functools.partial(gelu_body, rows, tile), "gelu", [like((half, hid), bf16)]
        )(in_specs=[whole] * (nt + 1))(
            bias_in.reshape(1, hid), *[kept(part) for part in own_others]
        )
        far = lax.ppermute(both, "kin", swap)
        blocks = call(
            functools.partial(block_body, rows, tile_of(wide, 512)),
            "output_blocks",
            [like((total // len(pieces), wide), bf16)] * len(pieces),
            grant=8 * MIB,
            flops=work,
        )(in_specs=[whole] * 4)(kept(both), kept(far), kept(w_in), kept(w_out))

        act, grad, turned, bias_in_grad = call(
            functools.partial(split_body, rows),
            "split_rows",
            [like((total, hid), bf16)] * 2 + [like((total, wide), bf16), like((1, hid), f32)],
            grant=8 * MIB,
        )(in_specs=[whole] * 3)(kept(both), kept(far), kept(mixed))
        weight_in_grad = product(turned, grad, "weight_in_grad", 256)
        weight_out_grad = product(act, turned, "weight_out_grad", 512)

        if small:
            terms = [blocks[0]] + [across(blocks[shift], shift) for shift in range(1, nn)]
            own, sent = call(
                functools.partial(sum_body, rows), "sum_blocks", [like((pair, wide), bf16)] * 2
            )(in_specs=[whole] * (nn + 1))(
                bias_out.reshape(1, cols), *[kept(term) for term in terms]
            )
            got = lax.ppermute(sent, "tok", swap)
            got_sums = lax.ppermute(sums, "tok", swap)
            output_rows, grad_tokens, bias_out_grad = call(
                functools.partial(final_body, rows),
                "final_rows",
                [like((rows, cols), bf16)] * 2 + [like((1, cols), f32)],
                resident=False,
            )(in_specs=[whole] * 4)(kept(own), kept(got), kept(sums), kept(got_sums))
            bias_out_grad = bias_out_grad.reshape(cols)
        else:
            chunks = blocks[0].reshape(nn, nt * pair, wide)
            back = lax.all_to_all(chunks, "nout", split_axis=0, concat_axis=0, tiled=True)
            summed = jnp.sum(back.astype(f32), axis=0).reshape(nt, pair, wide)
            at = lax.axis_index("tok") * wide
            bias = lax.dynamic_slice_in_dim(bias_out, at, wide)
            summed = summed + jnp.where(jnp.arange(pair) < rows, 1.0, 0.0)[:, None] * bias
            summed = summed.astype(bf16)
            ends = lax.all_to_all(summed, "tok", split_axis=0, concat_axis=0, tiled=True)
            ends = ends.transpose(1, 0, 2).reshape(pair, cols)
            output_rows, grad_tokens = ends[:rows], ends[rows:]
            bias_out_grad = lax.all_gather(sums.reshape(wide), "tok", axis=0, tiled=True)
        return (
            output_rows,
            grad_tokens,
            weight_in_grad,
            weight_out_grad,
            bias_in_grad.reshape(hid),
            bias_out_grad,
        )

    return on_device


def solution(mesh):
    return jax.shard_map(
        make(mesh),
        mesh=mesh,
        in_specs=(
            P(("groups", "tok", "nout"), "kin"),
            P(("kin", "tok"), "nout"),
            P("nout"),
            P("nout", ("kin", "tok")),
            P("kin"),
            P(("groups", "tok", "nout"), "kin"),
        ),
        out_specs=(
            P(("groups", "tok", "nout"), "kin"),
            P(("groups", "tok", "nout"), "kin"),
            P(("groups", "kin", "tok"), "nout"),
            P(("groups", "nout"), ("kin", "tok")),
            P(("groups", "nout")),
            P(("groups", "kin")),
        ),
        check_vma=False,
    )
```

```python
import functools

import jax
import jax.numpy as jnp
from jax import lax
from jax.experimental import pallas as pl
from jax.experimental.pallas import tpu as pltpu
from jax.sharding import PartitionSpec as P

inv_root_two = 0.7071067811865476
inv_root_two_pi = 0.3989422804014327

MIB = 1 << 20
whole = pl.BlockSpec(memory_space=pltpu.VMEM)


def gelu_parts(hidden):
    normal_cdf = 0.5 * (1.0 + lax.erf(hidden * inv_root_two))
    density = jnp.exp(-0.5 * hidden * hidden) * inv_root_two_pi
    return (hidden * normal_cdf, normal_cdf + hidden * density)


def dot(left, right, left_dim, right_dim):
    return lax.dot_general(
        left, right, (((left_dim,), (right_dim,)), ((), ())), preferred_element_type=jnp.float32
    )


def tile_of(size, most):
    return max(t for t in range(128, most + 1, 128) if size % t == 0)


def cost(flops, moved):
    return pl.CostEstimate(flops=flops, bytes_accessed=moved, transcendentals=0)


def call(body, name, outs, grant=4 * MIB, flops=0, moved=0, scratch=(), resident=True):
    shapes = [pltpu.VMEM(o.shape, o.dtype) if resident else o for o in outs]
    return functools.partial(
        pl.pallas_call,
        body,
        out_shape=shapes,
        out_specs=[whole] * len(outs),
        scratch_shapes=list(scratch),
        cost_estimate=cost(flops, moved),
        compiler_params=pltpu.CompilerParams(vmem_limit_bytes=grant),
        name=name,
    )


def kept(array):
    return pltpu.with_memory_space_constraint(array, pltpu.VMEM)


def in_hbm(array):
    return pltpu.with_memory_space_constraint(array, pltpu.HBM)


def forward_rows(shape, rows):
    return lax.rem(lax.broadcasted_iota(jnp.int32, shape, 0), 2 * rows) < rows


def ordered(core, own, far):
    return jnp.concatenate([jnp.where(core == 0, own, far), jnp.where(core == 0, far, own)], axis=0)


def load_body(hbm_ref, after_ref, out_ref, sem):
    copy = pltpu.make_async_copy(hbm_ref, out_ref, sem.at[0])
    copy.start()
    copy.wait()


def pair_body(own_ref, got_ref, out_ref):
    out_ref[...] = ordered(lax.axis_index("tok"), own_ref[...], got_ref[...])


def partial_body(rows, tile, count, *refs):
    *piece_refs, w_in_ref, w_hbm = refs[: count + 2]
    w_out_ref, own_ref, sent_ref, mixed_ref, sums_ref, sems = refs[count + 2 :]
    hid = w_in_ref.shape[1]
    tiles = [pl.ds(i * tile, tile) for i in range(hid // tile)]
    copies = [
        pltpu.make_async_copy(w_hbm.at[at, :], w_out_ref.at[at, :], sems.at[i])
        for i, at in enumerate(tiles)
    ]
    for copy in copies:
        copy.start()
    mixed = jnp.concatenate([ref[...] for ref in piece_refs], axis=0)
    mixed_ref[...] = mixed
    total = mixed.shape[0]
    core = lax.axis_index("kin")
    is_fwd = forward_rows((total // 2, tile), rows)

    for at in tiles:
        forward = dot(mixed, w_in_ref[:, at], 1, 0)
        low, high = forward[: total // 2], forward[total // 2 :]
        own_ref[:, at] = jnp.where(core == 0, low, high).astype(jnp.bfloat16)
        sent_ref[:, at] = jnp.where(core == 0, high, low).astype(jnp.bfloat16)

    cotangents = jnp.where(forward_rows(mixed.shape, rows), 0.0, mixed.astype(jnp.float32))
    sums_ref[...] = jnp.sum(cotangents, axis=0, keepdims=True)

    for at, copy in zip(tiles, copies):
        copy.wait()
        backward = dot(mixed, w_out_ref[at, :], 1, 1)
        low, high = backward[: total // 2], backward[total // 2 :]
        for ref, part in (
            (own_ref, jnp.where(core == 0, low, high)),
            (sent_ref, jnp.where(core == 0, high, low)),
        ):
            forward = ref[:, at].astype(jnp.float32)
            ref[:, at] = jnp.where(is_fwd, forward, part).astype(jnp.bfloat16)


def add_body(left_ref, right_ref, out_ref):
    out_ref[...] = (
        left_ref[...].astype(jnp.float32) + right_ref[...].astype(jnp.float32)
    ).astype(jnp.bfloat16)


def gelu_body(rows, tile, bias_ref, after_ref, *refs):
    *part_refs, out_ref = refs
    is_fwd = forward_rows((out_ref.shape[0], tile), rows)

    @pl.loop(0, out_ref.shape[1] // tile)
    def _(step):
        at = pl.ds(pl.multiple_of(step * tile, tile), tile)
        summed = sum(ref[:, at].astype(jnp.float32) for ref in part_refs)
        activated, slopes = gelu_parts(summed + bias_ref[:, at])
        grad_pre = summed * pltpu.roll(slopes, rows, 0)
        out_ref[:, at] = jnp.where(is_fwd, activated, grad_pre).astype(jnp.bfloat16)


def block_body(rows, tile, own_ref, far_ref, w_in_ref, w_out_ref, *out_refs):
    wide = w_in_ref.shape[0]
    both = ordered(lax.axis_index("kin"), own_ref[...], far_ref[...])
    is_fwd = forward_rows((both.shape[0], tile), rows)
    size = both.shape[0] // len(out_refs)

    for i in range(wide // tile):
        at = pl.ds(i * tile, tile)
        forward = dot(both, w_out_ref[:, at], 1, 0)
        backward = dot(both, w_in_ref[at, :], 1, 1)
        terms = jnp.where(is_fwd, forward, backward).astype(jnp.bfloat16)
        for j, out_ref in enumerate(out_refs):
            out_ref[:, at] = terms[j * size : (j + 1) * size]


def split_body(rows, own_ref, far_ref, mixed_ref, act_ref, grad_ref, turned_ref):
    both = ordered(lax.axis_index("kin"), own_ref[...], far_ref[...]).astype(jnp.float32)
    is_fwd = forward_rows(both.shape, rows)
    zero = jnp.zeros_like(both)
    act_ref[...] = jnp.where(is_fwd, both, zero).astype(jnp.bfloat16)
    grad_ref[...] = jnp.where(is_fwd, zero, both).astype(jnp.bfloat16)
    mixed = mixed_ref[...].astype(jnp.float32)
    to_tokens = pltpu.roll(mixed, mixed.shape[0] - rows, 0)
    to_cotangents = pltpu.roll(mixed, rows, 0)
    is_fwd = forward_rows(mixed.shape, rows)
    turned_ref[...] = jnp.where(is_fwd, to_tokens, to_cotangents).astype(jnp.bfloat16)


def product_body(size, tile, left_ref, right_ref, out_ref, *sums_refs):
    at = pl.ds(pl.multiple_of(pl.program_id(0) * size, size), size)
    left = left_ref[:, at].T
    for i in range(out_ref.shape[1] // tile):
        part = pl.ds(i * tile, tile)
        out_ref[:, part] = dot(left, right_ref[:, part], 1, 0).astype(jnp.bfloat16)
    for sums_ref in sums_refs:

        @pl.when(pl.program_id(0) == 0)
        def _():
            right = right_ref[...].astype(jnp.float32)
            sums_ref[...] = jnp.sum(right, axis=0, keepdims=True)


def product(left, right, name, most, sums=False):
    total, high = left.shape
    wide = right.shape[1]
    size = tile_of(high, most)
    like = jax.ShapeDtypeStruct
    return pl.pallas_call(
        functools.partial(product_body, size, tile_of(wide, 512)),
        grid=(high // size,),
        out_shape=[like((high, wide), jnp.bfloat16)] + [like((1, wide), jnp.float32)] * sums,
        in_specs=[whole] * 2,
        out_specs=[pl.BlockSpec((size, wide), lambda i: (i, 0))] + [whole] * sums,
        cost_estimate=cost(2 * total * wide * high, 2 * wide * high),
        compiler_params=pltpu.CompilerParams(vmem_limit_bytes=16 * MIB),
        name=name,
    )(kept(left), kept(right))


def sum_body(rows, bias_ref, *refs):
    *term_refs, own_ref, sent_ref = refs
    wide = own_ref.shape[1]
    me = lax.axis_index("tok")
    summed = sum(ref[...].astype(jnp.float32) for ref in term_refs)
    bias = jnp.where(me == 0, bias_ref[:, :wide], bias_ref[:, wide:])
    summed = summed + jnp.where(forward_rows(summed.shape, rows), bias, 0.0)
    low, high = summed[: 2 * rows], summed[2 * rows :]
    own_ref[...] = jnp.where(me == 0, low, high).astype(jnp.bfloat16)
    sent_ref[...] = jnp.where(me == 0, high, low).astype(jnp.bfloat16)


def final_body(rows, own_ref, got_ref, own_sums_ref, got_sums_ref, rows_ref, grad_ref, sums_ref):
    wide = own_ref.shape[1]
    me = lax.axis_index("tok")
    own, got = own_ref[...].astype(jnp.float32), got_ref[...].astype(jnp.float32)
    own_sums, got_sums = own_sums_ref[...], got_sums_ref[...]
    for i in range(2):
        at = pl.ds(i * wide, wide)
        part = jnp.where(me == i, own, got)
        rows_ref[:, at] = part[:rows].astype(jnp.bfloat16)
        grad_ref[:, at] = part[rows:].astype(jnp.bfloat16)
        sums_ref[:, at] = jnp.where(me == i, own_sums, got_sums)


def make(mesh):
    nt, nk, nn = mesh.shape["tok"], mesh.shape["kin"], mesh.shape["nout"]
    small = nt == 2 and nn <= 4
    spread = nt * nn
    swap = [(0, 1), (1, 0)]
    bf16, f32 = jnp.bfloat16, jnp.float32
    like = jax.ShapeDtypeStruct

    def across(array, shift):
        return lax.ppermute(array, "nout", [(i, i ^ shift) for i in range(nn)])

    def on_device(tokens, weight_in, bias_in, weight_out, bias_out, grad_out):
        rows, cols = tokens.shape
        wide, hid = weight_in.shape
        pair = 2 * rows
        total = pair * spread
        half = total // nk
        work = 4 * total * wide * hid

        mine = jnp.concatenate([tokens, grad_out], axis=0)
        if small:
            me = lax.axis_index("tok")
            own = lax.dynamic_slice_in_dim(mine, me * wide, wide, 1)
            sent = lax.dynamic_slice_in_dim(mine, (1 - me) * wide, wide, 1)
            got = lax.ppermute(sent, "tok", swap)
            (tiles,) = call(pair_body, "pair_tiles", [like((nt * pair, wide), bf16)])(
                in_specs=[whole] * 2
            )(kept(own), kept(got))
            pieces = [tiles] + [across(tiles, shift) for shift in range(1, nn)]
        else:
            chunks = mine.reshape(pair, nt, wide).transpose(1, 0, 2)
            tiles = lax.all_to_all(chunks, "tok", split_axis=0, concat_axis=0, tiled=True)
            tiles = tiles.reshape(nt * pair, wide)
            pieces = [lax.all_gather(tiles, "nout", axis=0, tiled=True)]

        hbm = pl.BlockSpec(memory_space=pltpu.HBM)
        (w_in,) = call(
            load_body,
            "load_weight",
            [weight_in],
            grant=MIB,
            moved=4 * wide * hid,
            scratch=[pltpu.SemaphoreType.DMA((1,))],
        )(in_specs=[hbm, pl.BlockSpec(memory_space=pl.ANY)])(in_hbm(weight_in), tiles)

        tile = tile_of(hid, 512)
        w_out, own, sent, mixed, sums = call(
            functools.partial(partial_body, rows, tile, len(pieces)),
            "partial_sums",
            [weight_out]
            + [like((half, hid), bf16)] * 2
            + [like((total, wide), bf16), like((1, wide), f32)],
            grant=8 * MIB,
            flops=work,
            moved=4 * wide * hid,
            scratch=[pltpu.SemaphoreType.DMA((hid // tile,))],
        )(in_specs=[whole] * (len(pieces) + 1) + [hbm])(
            *[kept(piece) for piece in pieces], kept(w_in), in_hbm(weight_out)
        )
        got = lax.ppermute(sent, "kin", swap)
        (own,) = call(add_body, "add_cores", [like((half, hid), bf16)])(in_specs=[whole] * 2)(
            kept(own), kept(got)
        )
        if nt == 2:
            got_sums = lax.ppermute(sums, "tok", swap)
            own_others = [own, lax.ppermute(own, "tok", swap)]
        else:
            got_sums = sums
            gathered = lax.all_gather(own, "tok", axis=0)
            own_others = [gathered[i] for i in range(nt)]
        (both,) = call(
            functools.partial(gelu_body, rows, tile), "gelu", [like((half, hid), bf16)]
        )(in_specs=[whole] * (nt + 2))(
            bias_in.reshape(1, hid), got_sums, *[kept(part) for part in own_others]
        )
        far = lax.ppermute(both, "kin", swap)
        blocks = call(
            functools.partial(block_body, rows, tile_of(wide, 512)),
            "output_blocks",
            [like((total // len(pieces), wide), bf16)] * len(pieces),
            grant=8 * MIB,
            flops=work,
        )(in_specs=[whole] * 4)(kept(both), kept(far), kept(w_in), kept(w_out))

        act, grad, turned = call(
            functools.partial(split_body, rows),
            "split_rows",
            [like((total, hid), bf16)] * 2 + [like((total, wide), bf16)],
            grant=8 * MIB,
        )(in_specs=[whole] * 3)(kept(both), kept(far), kept(mixed))
        weight_in_grad, bias_in_grad = product(turned, grad, "weight_in_grad", 256, sums=True)
        (weight_out_grad,) = product(act, turned, "weight_out_grad", 512)

        if small:
            terms = [blocks[0]] + [across(blocks[shift], shift) for shift in range(1, nn)]
            own, sent = call(
                functools.partial(sum_body, rows), "sum_blocks", [like((pair, wide), bf16)] * 2
            )(in_specs=[whole] * (nn + 1))(
                bias_out.reshape(1, cols), *[kept(term) for term in terms]
            )
            got = lax.ppermute(sent, "tok", swap)
            output_rows, grad_tokens, bias_out_grad = call(
                functools.partial(final_body, rows),
                "final_rows",
                [like((rows, cols), bf16)] * 2 + [like((1, cols), f32)],
                resident=False,
            )(in_specs=[whole] * 4)(kept(own), kept(got), kept(sums), kept(got_sums))
            bias_out_grad = bias_out_grad.reshape(cols)
        else:
            chunks = blocks[0].reshape(nn, nt * pair, wide)
            back = lax.all_to_all(chunks, "nout", split_axis=0, concat_axis=0, tiled=True)
            summed = jnp.sum(back.astype(f32), axis=0).reshape(nt, pair, wide)
            at = lax.axis_index("tok") * wide
            bias = lax.dynamic_slice_in_dim(bias_out, at, wide)
            summed = summed + jnp.where(jnp.arange(pair) < rows, 1.0, 0.0)[:, None] * bias
            summed = summed.astype(bf16)
            ends = lax.all_to_all(summed, "tok", split_axis=0, concat_axis=0, tiled=True)
            ends = ends.transpose(1, 0, 2).reshape(pair, cols)
            output_rows, grad_tokens = ends[:rows], ends[rows:]
            bias_out_grad = lax.all_gather(sums.reshape(wide), "tok", axis=0, tiled=True)
        return (
            output_rows,
            grad_tokens,
            weight_in_grad,
            weight_out_grad,
            bias_in_grad.reshape(hid),
            bias_out_grad,
        )

    return on_device


def solution(mesh):
    return jax.shard_map(
        make(mesh),
        mesh=mesh,
        in_specs=(
            P(("groups", "tok", "nout"), "kin"),
            P(("kin", "tok"), "nout"),
            P("nout"),
            P("nout", ("kin", "tok")),
            P("kin"),
            P(("groups", "tok", "nout"), "kin"),
        ),
        out_specs=(
            P(("groups", "tok", "nout"), "kin"),
            P(("groups", "tok", "nout"), "kin"),
            P(("groups", "kin", "tok"), "nout"),
            P(("groups", "nout"), ("kin", "tok")),
            P(("groups", "nout")),
            P(("groups", "kin")),
        ),
        check_vma=False,
    )
```

```python
import functools

import jax
import jax.numpy as jnp
from jax import lax
from jax.experimental import pallas as pl
from jax.experimental.pallas import tpu as pltpu
from jax.sharding import PartitionSpec as P

inv_root_two = 0.7071067811865476
inv_root_two_pi = 0.3989422804014327

MIB = 1 << 20
whole = pl.BlockSpec(memory_space=pltpu.VMEM)


def gelu_parts(hidden):
    normal_cdf = 0.5 * (1.0 + lax.erf(hidden * inv_root_two))
    density = jnp.exp(-0.5 * hidden * hidden) * inv_root_two_pi
    return (hidden * normal_cdf, normal_cdf + hidden * density)


def dot(left, right, left_dim, right_dim):
    return lax.dot_general(
        left, right, (((left_dim,), (right_dim,)), ((), ())), preferred_element_type=jnp.float32
    )


def tile_of(size, most):
    return max(t for t in range(128, most + 1, 128) if size % t == 0)


def cost(flops, moved):
    return pl.CostEstimate(flops=flops, bytes_accessed=moved, transcendentals=0)


def call(body, name, outs, grant=4 * MIB, flops=0, moved=0, scratch=(), resident=True):
    shapes = [pltpu.VMEM(o.shape, o.dtype) if resident else o for o in outs]
    return functools.partial(
        pl.pallas_call,
        body,
        out_shape=shapes,
        out_specs=[whole] * len(outs),
        scratch_shapes=list(scratch),
        cost_estimate=cost(flops, moved),
        compiler_params=pltpu.CompilerParams(vmem_limit_bytes=grant),
        name=name,
    )


def kept(array):
    return pltpu.with_memory_space_constraint(array, pltpu.VMEM)


def in_hbm(array):
    return pltpu.with_memory_space_constraint(array, pltpu.HBM)


def apart(mixed, rows):
    total, wide = mixed.shape
    tiles = mixed.reshape(total // (4 * rows), 2, 2 * rows, wide)
    even, odd = tiles[:, 0], tiles[:, 1]
    is_low = lax.broadcasted_iota(jnp.int32, even.shape, 1) < rows
    first = jnp.where(is_low, even, pltpu.roll(odd, rows, 1))
    second = jnp.where(is_low, pltpu.roll(even, rows, 1), odd)
    return first.reshape(total // 2, wide), second.reshape(total // 2, wide)


def together(first, second, rows):
    total, wide = first.shape
    first = first.reshape(total // (2 * rows), 2 * rows, wide)
    second = second.reshape(total // (2 * rows), 2 * rows, wide)
    is_low = lax.broadcasted_iota(jnp.int32, first.shape, 1) < rows
    even = jnp.where(is_low, first, pltpu.roll(second, rows, 1))
    odd = jnp.where(is_low, pltpu.roll(first, rows, 1), second)
    return jnp.stack([even, odd], axis=1).reshape(2 * total, wide)


def ordered(core, own, far):
    return jnp.concatenate([jnp.where(core == 0, own, far), jnp.where(core == 0, far, own)], axis=0)


def load_body(hbm_ref, after_ref, out_ref, sem):
    copy = pltpu.make_async_copy(hbm_ref, out_ref, sem.at[0])
    copy.start()
    copy.wait()


def pair_body(own_ref, got_ref, out_ref):
    out_ref[...] = ordered(lax.axis_index("tok"), own_ref[...], got_ref[...])


def partial_body(rows, tile, count, *refs):
    *piece_refs, w_in_ref, w_hbm = refs[: count + 2]
    w_out_ref, own_ref, sent_ref, x_ref, dy_ref, sums_ref, sems = refs[count + 2 :]
    hid = w_in_ref.shape[1]
    tiles = [pl.ds(i * tile, tile) for i in range(hid // tile)]
    copies = [
        pltpu.make_async_copy(w_hbm.at[at, :], w_out_ref.at[at, :], sems.at[i])
        for i, at in enumerate(tiles)
    ]
    for copy in copies:
        copy.start()
    mixed = jnp.concatenate([ref[...] for ref in piece_refs], axis=0)
    x_cols, dy_cols = apart(mixed.astype(jnp.float32), rows)
    sums_ref[...] = jnp.sum(dy_cols, axis=0, keepdims=True)
    x_cols, dy_cols = x_cols.astype(jnp.bfloat16), dy_cols.astype(jnp.bfloat16)
    x_ref[...], dy_ref[...] = x_cols, dy_cols
    half = x_cols.shape[0] // 2
    core = lax.axis_index("kin")

    def store(terms, first, at):
        low, high = terms[:half], terms[half:]
        put = pl.ds(first, half)
        own_ref[put, at] = jnp.where(core == 0, low, high).astype(jnp.bfloat16)
        sent_ref[put, at] = jnp.where(core == 0, high, low).astype(jnp.bfloat16)

    for at in tiles:
        store(dot(x_cols, w_in_ref[:, at], 1, 0), 0, at)
    for at, copy in zip(tiles, copies):
        copy.wait()
        store(dot(dy_cols, w_out_ref[at, :], 1, 1), half, at)


def add_body(left_ref, right_ref, out_ref):
    out_ref[...] = (
        left_ref[...].astype(jnp.float32) + right_ref[...].astype(jnp.float32)
    ).astype(jnp.bfloat16)


def gelu_body(tile, bias_ref, after_ref, *refs):
    *part_refs, out_ref = refs
    half = out_ref.shape[0] // 2

    @pl.loop(0, out_ref.shape[1] // tile)
    def _(step):
        at = pl.ds(pl.multiple_of(step * tile, tile), tile)
        summed = sum(ref[:, at].astype(jnp.float32) for ref in part_refs)
        activated, slopes = gelu_parts(summed[:half] + bias_ref[:, at])
        out_ref[:half, at] = activated.astype(jnp.bfloat16)
        out_ref[half:, at] = (summed[half:] * slopes).astype(jnp.bfloat16)


def block_body(rows, tile, own_ref, far_ref, w_in_ref, w_out_ref, act_ref, grad_ref, *out_refs):
    wide = w_in_ref.shape[0]
    half = own_ref.shape[0] // 2
    core = lax.axis_index("kin")
    act = ordered(core, own_ref[:half], far_ref[:half])
    grad = ordered(core, own_ref[half:], far_ref[half:])
    act_ref[...], grad_ref[...] = act, grad
    size = out_refs[0].shape[0]
    for i in range(wide // tile):
        at = pl.ds(i * tile, tile)
        forward = dot(act, w_out_ref[:, at], 1, 0)
        backward = dot(grad, w_in_ref[at, :], 1, 1)
        terms = together(forward, backward, rows).astype(jnp.bfloat16)
        for j, out_ref in enumerate(out_refs):
            out_ref[:, at] = terms[j * size : (j + 1) * size]


def sum_body(rows, bias_ref, *refs):
    *term_refs, own_ref, sent_ref = refs
    wide = own_ref.shape[1]
    me = lax.axis_index("tok")
    summed = sum(ref[...].astype(jnp.float32) for ref in term_refs)
    bias = jnp.where(me == 0, bias_ref[:, :wide], bias_ref[:, wide:])
    is_fwd = lax.rem(lax.broadcasted_iota(jnp.int32, summed.shape, 0), 2 * rows) < rows
    summed = summed + jnp.where(is_fwd, bias, 0.0)
    low, high = summed[: 2 * rows], summed[2 * rows :]
    own_ref[...] = jnp.where(me == 0, low, high).astype(jnp.bfloat16)
    sent_ref[...] = jnp.where(me == 0, high, low).astype(jnp.bfloat16)


def final_body(
    rows, own_ref, got_ref, own_sums_ref, got_sums_ref, hidden_ref, rows_ref, grad_ref, sums_ref, bias_ref
):
    wide = own_ref.shape[1]
    me = lax.axis_index("tok")
    own, got = own_ref[...].astype(jnp.float32), got_ref[...].astype(jnp.float32)
    own_sums, got_sums = own_sums_ref[...], got_sums_ref[...]
    for i in range(2):
        at = pl.ds(i * wide, wide)
        part = jnp.where(me == i, own, got)
        rows_ref[:, at] = part[:rows].astype(jnp.bfloat16)
        grad_ref[:, at] = part[rows:].astype(jnp.bfloat16)
        sums_ref[:, at] = jnp.where(me == i, own_sums, got_sums)
    bias_ref[...] = jnp.sum(hidden_ref[...].astype(jnp.float32), axis=0, keepdims=True)


def make(mesh):
    nt, nk, nn = mesh.shape["tok"], mesh.shape["kin"], mesh.shape["nout"]
    small = nt == 2 and nn <= 4
    spread = nt * nn
    swap = [(0, 1), (1, 0)]
    bf16, f32 = jnp.bfloat16, jnp.float32
    like = jax.ShapeDtypeStruct

    def across(array, shift):
        return lax.ppermute(array, "nout", [(i, i ^ shift) for i in range(nn)])

    def on_device(tokens, weight_in, bias_in, weight_out, bias_out, grad_out):
        rows, cols = tokens.shape
        wide, hid = weight_in.shape
        pair = 2 * rows
        total = pair * spread
        half = total // nk
        work = 4 * total * wide * hid

        mine = jnp.concatenate([tokens, grad_out], axis=0)
        if small:
            me = lax.axis_index("tok")
            own = lax.dynamic_slice_in_dim(mine, me * wide, wide, 1)
            sent = lax.dynamic_slice_in_dim(mine, (1 - me) * wide, wide, 1)
            got = lax.ppermute(sent, "tok", swap)
            (tiles,) = call(pair_body, "pair_tiles", [like((nt * pair, wide), bf16)])(
                in_specs=[whole] * 2
            )(kept(own), kept(got))
            pieces = [tiles] + [across(tiles, shift) for shift in range(1, nn)]
        else:
            chunks = mine.reshape(pair, nt, wide).transpose(1, 0, 2)
            tiles = lax.all_to_all(chunks, "tok", split_axis=0, concat_axis=0, tiled=True)
            tiles = tiles.reshape(nt * pair, wide)
            pieces = [lax.all_gather(tiles, "nout", axis=0, tiled=True)]

        hbm = pl.BlockSpec(memory_space=pltpu.HBM)
        (w_in,) = call(
            load_body,
            "load_weight",
            [weight_in],
            grant=MIB,
            moved=4 * wide * hid,
            scratch=[pltpu.SemaphoreType.DMA((1,))],
        )(in_specs=[hbm, pl.BlockSpec(memory_space=pl.ANY)])(in_hbm(weight_in), tiles)

        tile = tile_of(hid, 512)
        w_out, own, sent, x_cols, dy_cols, sums = call(
            functools.partial(partial_body, rows, tile, len(pieces)),
            "partial_sums",
            [weight_out]
            + [like((half, hid), bf16)] * 2
            + [like((total // 2, wide), bf16)] * 2
            + [like((1, wide), f32)],
            grant=8 * MIB,
            flops=work,
            moved=4 * wide * hid,
            scratch=[pltpu.SemaphoreType.DMA((hid // tile,))],
        )(in_specs=[whole] * (len(pieces) + 1) + [hbm])(
            *[kept(piece) for piece in pieces], kept(w_in), in_hbm(weight_out)
        )
        got = lax.ppermute(sent, "kin", swap)
        (own,) = call(add_body, "add_cores", [like((half, hid), bf16)])(in_specs=[whole] * 2)(
            kept(own), kept(got)
        )
        if nt == 2:
            got_sums = lax.ppermute(sums, "tok", swap)
            own_others = [own, lax.ppermute(own, "tok", swap)]
        else:
            got_sums = sums
            gathered = lax.all_gather(own, "tok", axis=0)
            own_others = [gathered[i] for i in range(nt)]
        (both,) = call(
            functools.partial(gelu_body, tile), "gelu", [like((half, hid), bf16)]
        )(in_specs=[whole] * (nt + 2))(
            bias_in.reshape(1, hid), got_sums, *[kept(part) for part in own_others]
        )
        far = lax.ppermute(both, "kin", swap)
        act, grad, *blocks = call(
            functools.partial(block_body, rows, tile_of(wide, 512)),
            "output_blocks",
            [like((total // 2, hid), bf16)] * 2
            + [like((total // len(pieces), wide), bf16)] * len(pieces),
            grant=8 * MIB,
            flops=work,
        )(in_specs=[whole] * 4)(kept(both), kept(far), kept(w_in), kept(w_out))

        weight_in_grad = dot(x_cols, grad, 0, 0).astype(bf16)
        weight_out_grad = dot(act, dy_cols, 0, 0).astype(bf16)

        if small:
            terms = [blocks[0]] + [across(blocks[shift], shift) for shift in range(1, nn)]
            own, sent = call(
                functools.partial(sum_body, rows), "sum_blocks", [like((pair, wide), bf16)] * 2
            )(in_specs=[whole] * (nn + 1))(
                bias_out.reshape(1, cols), *[kept(term) for term in terms]
            )
            got = lax.ppermute(sent, "tok", swap)
            output_rows, grad_tokens, bias_out_grad, bias_in_grad = call(
                functools.partial(final_body, rows),
                "final_rows",
                [like((rows, cols), bf16)] * 2 + [like((1, cols), f32), like((1, hid), f32)],
                resident=False,
            )(in_specs=[whole] * 5)(kept(own), kept(got), kept(sums), kept(got_sums), kept(grad))
            bias_out_grad = bias_out_grad.reshape(cols)
        else:
            chunks = blocks[0].reshape(nn, nt * pair, wide)
            back = lax.all_to_all(chunks, "nout", split_axis=0, concat_axis=0, tiled=True)
            summed = jnp.sum(back.astype(f32), axis=0).reshape(nt, pair, wide)
            at = lax.axis_index("tok") * wide
            bias = lax.dynamic_slice_in_dim(bias_out, at, wide)
            summed = summed + jnp.where(jnp.arange(pair) < rows, 1.0, 0.0)[:, None] * bias
            summed = summed.astype(bf16)
            ends = lax.all_to_all(summed, "tok", split_axis=0, concat_axis=0, tiled=True)
            ends = ends.transpose(1, 0, 2).reshape(pair, cols)
            output_rows, grad_tokens = ends[:rows], ends[rows:]
            bias_out_grad = lax.all_gather(sums.reshape(wide), "tok", axis=0, tiled=True)
            bias_in_grad = jnp.sum(grad.astype(f32), axis=0)
        return (
            output_rows,
            grad_tokens,
            weight_in_grad,
            weight_out_grad,
            bias_in_grad.reshape(hid),
            bias_out_grad,
        )

    return on_device


def solution(mesh):
    return jax.shard_map(
        make(mesh),
        mesh=mesh,
        in_specs=(
            P(("groups", "tok", "nout"), "kin"),
            P(("kin", "tok"), "nout"),
            P("nout"),
            P("nout", ("kin", "tok")),
            P("kin"),
            P(("groups", "tok", "nout"), "kin"),
        ),
        out_specs=(
            P(("groups", "tok", "nout"), "kin"),
            P(("groups", "tok", "nout"), "kin"),
            P(("groups", "kin", "tok"), "nout"),
            P(("groups", "nout"), ("kin", "tok")),
            P(("groups", "nout")),
            P(("groups", "kin")),
        ),
        check_vma=False,
    )
```

```python
import functools

import jax
import jax.numpy as jnp
from jax import lax
from jax.experimental import pallas as pl
from jax.experimental.pallas import tpu as pltpu
from jax.sharding import PartitionSpec as P

inv_root_two = 0.7071067811865476
inv_root_two_pi = 0.3989422804014327

MIB = 1 << 20
bf16, f32 = jnp.bfloat16, jnp.float32
like = jax.ShapeDtypeStruct
whole = pl.BlockSpec(memory_space=pltpu.VMEM)
hbm = pl.BlockSpec(memory_space=pltpu.HBM)
swap = [(0, 1), (1, 0)]


def gelu_parts(hidden):
    normal_cdf = 0.5 * (1.0 + lax.erf(hidden * inv_root_two))
    density = jnp.exp(-0.5 * hidden * hidden) * inv_root_two_pi
    return (hidden * normal_cdf, normal_cdf + hidden * density)


def dot(left, right, left_dim, right_dim):
    return lax.dot_general(
        left, right, (((left_dim,), (right_dim,)), ((), ())), preferred_element_type=jnp.float32
    )


def exchange(chunks, axes):
    return lax.all_to_all(chunks, axes, split_axis=0, concat_axis=0, tiled=True)


def tile_of(size, most):
    return max(t for t in range(128, most + 1, 128) if size % t == 0)


def tiles_of(size, most=512):
    tile = tile_of(size, most)
    return [pl.ds(i * tile, tile) for i in range(size // tile)]


def call(body, name, outs, grant=4 * MIB, flops=0, moved=0, scratch=(), resident=True, specs=None):
    shapes = [pltpu.VMEM(o.shape, o.dtype) if resident else o for o in outs]

    def run(*args):
        cost = pl.CostEstimate(flops=flops, bytes_accessed=moved, transcendentals=0)
        return pl.pallas_call(
            body,
            out_shape=shapes,
            in_specs=specs or [whole] * len(args),
            out_specs=[whole] * len(outs),
            scratch_shapes=list(scratch),
            cost_estimate=cost,
            compiler_params=pltpu.CompilerParams(vmem_limit_bytes=grant),
            name=name,
        )(*args)

    return run


def kept(array):
    return pltpu.with_memory_space_constraint(array, pltpu.VMEM)


def in_hbm(array):
    return pltpu.with_memory_space_constraint(array, pltpu.HBM)


def apart(mixed, rows):
    total, wide = mixed.shape
    tiles = mixed.reshape(total // (4 * rows), 2, 2 * rows, wide)
    even, odd = tiles[:, 0], tiles[:, 1]
    is_low = lax.broadcasted_iota(jnp.int32, even.shape, 1) < rows
    first = jnp.where(is_low, even, pltpu.roll(odd, rows, 1))
    second = jnp.where(is_low, pltpu.roll(even, rows, 1), odd)
    return first.reshape(total // 2, wide), second.reshape(total // 2, wide)


def together(first, second, rows):
    total, wide = first.shape
    first = first.reshape(total // (2 * rows), 2 * rows, wide)
    second = second.reshape(total // (2 * rows), 2 * rows, wide)
    is_low = lax.broadcasted_iota(jnp.int32, first.shape, 1) < rows
    even = jnp.where(is_low, first, pltpu.roll(second, rows, 1))
    odd = jnp.where(is_low, pltpu.roll(first, rows, 1), second)
    return jnp.stack([even, odd], axis=1).reshape(2 * total, wide)


def ordered(me, own, far, axis=0):
    low, high = jnp.where(me == 0, own, far), jnp.where(me == 0, far, own)
    return jnp.concatenate([low, high], axis=axis)


def half_of(size, mine):
    core = lax.axis_index("kin")
    at = core if mine else 1 - core
    return pl.ds(pl.multiple_of(at * size, size), size)


def load_out_body(hbm_ref, after_ref, out_ref, sem):
    copy = pltpu.make_async_copy(hbm_ref.at[half_of(out_ref.shape[0], False), :], out_ref, sem.at[0])
    copy.start()
    copy.wait()


def load_in_body(hbm_ref, after_ref, own_ref, far_ref, sems):
    half = own_ref.shape[1]
    copies = [
        pltpu.make_async_copy(hbm_ref.at[:, half_of(half, mine)], ref, sems.at[i])
        for i, (ref, mine) in enumerate(((far_ref, False), (own_ref, True)))
    ]
    for copy in copies:
        copy.start()
    for copy in copies:
        copy.wait()


def pair_body(own_ref, got_ref, after_ref, out_ref):
    out_ref[...] = ordered(lax.axis_index("tok"), own_ref[...], got_ref[...])


def partial_sums(x_cols, dy_cols, w_in_ref, w_out_ref, out_ref):
    count = x_cols.shape[0]
    for at in tiles_of(out_ref.shape[1]):
        out_ref[:count, at] = dot(x_cols, w_in_ref[:, at], 1, 0).astype(bf16)
        out_ref[count:, at] = dot(dy_cols, w_out_ref[at, :], 1, 1).astype(bf16)


def far_half_body(rows, count, *refs):
    *piece_refs, w_in_ref, w_out_ref, w_hbm = refs[: count + 3]
    own_weight_ref, sent_ref, x_ref, dy_ref, sums_ref, sem = refs[count + 3 :]
    copy = pltpu.make_async_copy(
        w_hbm.at[half_of(own_weight_ref.shape[0], True), :], own_weight_ref, sem.at[0]
    )
    copy.start()
    mixed = jnp.concatenate([ref[...] for ref in piece_refs], axis=0)
    x_cols, dy_cols = apart(mixed.astype(f32), rows)
    sums_ref[...] = jnp.sum(dy_cols, axis=0, keepdims=True)
    x_cols, dy_cols = x_cols.astype(bf16), dy_cols.astype(bf16)
    x_ref[...], dy_ref[...] = x_cols, dy_cols
    partial_sums(x_cols, dy_cols, w_in_ref, w_out_ref, sent_ref)
    copy.wait()


def own_half_body(x_ref, dy_ref, w_in_ref, w_out_ref, own_ref):
    partial_sums(x_ref[...], dy_ref[...], w_in_ref, w_out_ref, own_ref)


def add_body(left_ref, right_ref, out_ref):
    out_ref[...] = (left_ref[...].astype(f32) + right_ref[...].astype(f32)).astype(bf16)


def gelu_body(bias_ref, after_ref, own_ref, other_ref, out_ref):
    count, half = out_ref.shape[0] // 2, out_ref.shape[1]
    bias = bias_ref[:, half_of(half, True)]
    tile = tile_of(half, 512)
    for i in range(half // tile):
        at = pl.ds(i * tile, tile)
        summed = own_ref[:, at].astype(f32) + other_ref[:, at].astype(f32)
        activated, slopes = gelu_parts(summed[:count] + bias[:, i * tile : (i + 1) * tile])
        out_ref[:count, at] = activated.astype(bf16)
        out_ref[count:, at] = (summed[count:] * slopes).astype(bf16)


def own_terms_body(both_ref, w_in_ref, w_out_ref, out_ref):
    count = both_ref.shape[0] // 2
    act, grad = both_ref[:count], both_ref[count:]
    for at in tiles_of(out_ref.shape[1]):
        out_ref[:count, at] = dot(act, w_out_ref[:, at], 1, 0)
        out_ref[count:, at] = dot(grad, w_in_ref[at, :], 1, 1)


def blocks_body(rows, own_ref, far_ref, terms_ref, w_in_ref, w_out_ref, act_ref, grad_ref, *out_refs):
    count = far_ref.shape[0] // 2
    core = lax.axis_index("kin")
    act, grad = far_ref[:count], far_ref[count:]
    act_ref[...] = ordered(core, own_ref[:count], act, 1)
    grad_ref[...] = ordered(core, own_ref[count:], grad, 1)
    size = out_refs[0].shape[0]
    for at in tiles_of(terms_ref.shape[1]):
        forward = terms_ref[:count, at] + dot(act, w_out_ref[:, at], 1, 0)
        backward = terms_ref[count:, at] + dot(grad, w_in_ref[at, :], 1, 1)
        terms = together(forward, backward, rows).astype(bf16)
        for i, out_ref in enumerate(out_refs):
            out_ref[:, at] = terms[i * size : (i + 1) * size]


def sum_body(rows, bias_ref, *refs):
    *term_refs, own_ref, sent_ref = refs
    wide = own_ref.shape[1]
    me = lax.axis_index("tok")
    summed = sum(ref[...].astype(f32) for ref in term_refs)
    bias = jnp.where(me == 0, bias_ref[:, :wide], bias_ref[:, wide:])
    is_fwd = lax.rem(lax.broadcasted_iota(jnp.int32, summed.shape, 0), 2 * rows) < rows
    summed = summed + jnp.where(is_fwd, bias, 0.0)
    low, high = summed[: 2 * rows], summed[2 * rows :]
    own_ref[...] = jnp.where(me == 0, low, high).astype(bf16)
    sent_ref[...] = jnp.where(me == 0, high, low).astype(bf16)


def final_body(
    rows, own_ref, got_ref, own_sums_ref, got_sums_ref, hidden_ref, rows_ref, grad_ref, sums_ref, bias_ref
):
    wide = own_ref.shape[1]
    me = lax.axis_index("tok")
    own, got = own_ref[...].astype(f32), got_ref[...].astype(f32)
    own_sums, got_sums = own_sums_ref[...], got_sums_ref[...]
    for i in range(2):
        at = pl.ds(i * wide, wide)
        part = jnp.where(me == i, own, got)
        rows_ref[:, at] = part[:rows].astype(bf16)
        grad_ref[:, at] = part[rows:].astype(bf16)
        sums_ref[:, at] = jnp.where(me == i, own_sums, got_sums)
    bias_ref[...] = jnp.sum(hidden_ref[...].astype(f32), axis=0, keepdims=True)


def make_small(nn):
    def across(array, shift):
        return lax.ppermute(array, "nout", [(i, i ^ shift) for i in range(nn)])

    def on_device(tokens, weight_in, bias_in, weight_out, bias_out, grad_out):
        rows, cols = tokens.shape
        wide, hid = weight_in.shape
        half = hid // 2
        pair = 2 * rows
        count = 2 * nn * rows
        work = 4 * count * wide * half
        piece = 2 * wide * half
        sem = pltpu.SemaphoreType.DMA

        mine = jnp.concatenate([tokens, grad_out], axis=0)
        me = lax.axis_index("tok")
        own = lax.dynamic_slice_in_dim(mine, me * wide, wide, 1)
        sent = lax.dynamic_slice_in_dim(mine, (1 - me) * wide, wide, 1)
        got = lax.ppermute(sent, "tok", swap)
        (out_far,) = call(
            load_out_body,
            "load_out",
            [like((half, wide), bf16)],
            grant=MIB,
            moved=piece,
            scratch=[sem((1,))],
            specs=[hbm, pl.BlockSpec(memory_space=pl.ANY)],
        )(in_hbm(weight_out), sent)
        (tiles,) = call(pair_body, "pair_tiles", [like((2 * pair, wide), bf16)])(
            kept(own), kept(got), kept(out_far)
        )
        pieces = [tiles] + [across(tiles, shift) for shift in range(1, nn)]
        in_own, in_far = call(
            load_in_body,
            "load_in",
            [like((wide, half), bf16)] * 2,
            grant=MIB,
            moved=2 * piece,
            scratch=[sem((2,))],
            specs=[hbm, pl.BlockSpec(memory_space=pl.ANY)],
        )(in_hbm(weight_in), tiles)

        out_own, sent, x_cols, dy_cols, sums = call(
            functools.partial(far_half_body, rows, nn),
            "far_half",
            [like((half, wide), bf16), like((2 * count, half), bf16)]
            + [like((count, wide), bf16)] * 2
            + [like((1, wide), f32)],
            grant=8 * MIB,
            flops=work,
            moved=piece,
            scratch=[sem((1,))],
            specs=[whole] * (nn + 2) + [hbm],
        )(*[kept(piece) for piece in pieces], kept(in_far), kept(out_far), in_hbm(weight_out))
        got = lax.ppermute(sent, "kin", swap)
        (own,) = call(
            own_half_body,
            "own_half",
            [like((2 * count, half), bf16)],
            grant=8 * MIB,
            flops=work,
            moved=2 * piece,
        )(kept(x_cols), kept(dy_cols), kept(in_own), kept(out_own))
        (own,) = call(add_body, "add_cores", [like((2 * count, half), bf16)])(kept(own), kept(got))
        other = lax.ppermute(own, "tok", swap)
        got_sums = lax.ppermute(sums, "tok", swap)
        (both,) = call(gelu_body, "gelu", [like((2 * count, half), bf16)])(
            bias_in.reshape(1, hid), got_sums, kept(own), kept(other)
        )
        far = lax.ppermute(both, "kin", swap)
        (terms,) = call(
            own_terms_body,
            "own_terms",
            [like((2 * count, wide), f32)],
            grant=8 * MIB,
            flops=work,
            moved=2 * piece,
        )(kept(both), kept(in_own), kept(out_own))
        act, grad, *blocks = call(
            functools.partial(blocks_body, rows),
            "output_blocks",
            [like((count, hid), bf16)] * 2 + [like((2 * pair, wide), bf16)] * nn,
            grant=8 * MIB,
            flops=work,
            moved=2 * piece,
        )(kept(both), kept(far), kept(terms), kept(in_far), kept(out_far))

        weight_in_grad = dot(x_cols, grad, 0, 0).astype(bf16)
        weight_out_grad = dot(act, dy_cols, 0, 0).astype(bf16)

        terms = [blocks[0]] + [across(blocks[shift], shift) for shift in range(1, nn)]
        own, sent = call(
            functools.partial(sum_body, rows), "sum_blocks", [like((pair, wide), bf16)] * 2
        )(bias_out.reshape(1, cols), *[kept(term) for term in terms])
        got = lax.ppermute(sent, "tok", swap)
        output_rows, grad_tokens, bias_out_grad, bias_in_grad = call(
            functools.partial(final_body, rows),
            "final_rows",
            [like((rows, cols), bf16)] * 2 + [like((1, cols), f32), like((1, hid), f32)],
            resident=False,
        )(kept(own), kept(got), kept(sums), kept(got_sums), kept(grad))
        return (
            output_rows,
            grad_tokens,
            weight_in_grad,
            weight_out_grad,
            bias_in_grad.reshape(hid),
            bias_out_grad.reshape(cols),
        )

    return on_device


def make_plain(nt, nk, nn):
    spread, square = nt * nn, nk * nt

    def on_device(tokens, weight_in, bias_in, weight_out, bias_out, grad_out):
        rows, cols = tokens.shape
        wide, hid = weight_in.shape
        part = hid // square
        pair = 2 * rows
        total = pair * spread

        mine = jnp.concatenate([tokens, grad_out], axis=0)
        by_owner = mine.reshape(pair, nt, wide).transpose(1, 0, 2)
        chunks = jnp.broadcast_to(by_owner[:, None], (nt, nn, pair, wide))
        mixed = exchange(chunks.reshape(spread, pair, wide), ("tok", "nout")).reshape(total, wide)
        is_fwd = (lax.broadcasted_iota(jnp.int32, (total, 1), 0) % pair) < rows

        col_sums = jnp.sum(jnp.where(is_fwd, 0.0, mixed.astype(jnp.float32)), axis=0)
        bias_out_grad = lax.all_gather(col_sums, "tok", axis=0, tiled=True)

        partial = jnp.where(is_fwd, dot(mixed, weight_in, 1, 0), dot(mixed, weight_out, 1, 1))
        partial = partial.astype(jnp.bfloat16).reshape(total, square, part).transpose(1, 0, 2)
        got = exchange(partial, ("kin", "tok"))
        summed = jnp.sum(got.astype(jnp.float32), axis=0).reshape(spread, 2, rows, part)
        at = lax.axis_index(("kin", "tok"))
        pre_act = summed[:, 0] + lax.dynamic_slice_in_dim(bias_in, at * part, part)
        activated, slopes = gelu_parts(pre_act)
        grad_pre = summed[:, 1] * slopes
        both = jnp.stack([activated, grad_pre], axis=1).astype(jnp.bfloat16).reshape(total, part)
        both = exchange(jnp.broadcast_to(both[None], (square, total, part)), ("kin", "tok"))
        both = both.transpose(1, 0, 2).reshape(total, hid)

        split = both.reshape(spread, 2, rows, hid)
        act = split[:, 0].reshape(spread * rows, hid)
        grad_half = split[:, 1].reshape(spread * rows, hid)
        split = mixed.reshape(spread, 2, rows, wide)
        x_cols = split[:, 0].reshape(spread * rows, wide)
        dy_cols = split[:, 1].reshape(spread * rows, wide)
        bias_in_grad = jnp.sum(grad_half.astype(jnp.float32), axis=0)

        block = jnp.stack(
            [
                dot(act, weight_out, 1, 0).reshape(spread, rows, wide),
                dot(grad_half, weight_in, 1, 1).reshape(spread, rows, wide),
            ],
            axis=1,
        )
        block = block.astype(jnp.bfloat16).reshape(spread, pair, wide)
        back = exchange(block, ("tok", "nout")).reshape(nt, nn, pair, wide)
        weight_in_grad = dot(x_cols, grad_half, 0, 0).astype(jnp.bfloat16)
        weight_out_grad = dot(act, dy_cols, 0, 0).astype(jnp.bfloat16)
        final = jnp.sum(back.astype(jnp.float32), axis=1).transpose(1, 0, 2).reshape(pair, cols)
        output_rows = (final[:rows] + bias_out).astype(jnp.bfloat16)
        grad_tokens = final[rows:].astype(jnp.bfloat16)
        return (output_rows, grad_tokens, weight_in_grad, weight_out_grad, bias_in_grad, bias_out_grad)

    return on_device


def solution(mesh):
    nt, nk, nn = mesh.shape["tok"], mesh.shape["kin"], mesh.shape["nout"]
    return jax.shard_map(
        make_small(nn) if (nt, nk) == (2, 2) and nn in (2, 4) else make_plain(nt, nk, nn),
        mesh=mesh,
        in_specs=(
            P(("groups", "tok", "nout"), "kin"),
            P(("kin", "tok"), "nout"),
            P("nout"),
            P("nout", ("kin", "tok")),
            P("kin"),
            P(("groups", "tok", "nout"), "kin"),
        ),
        out_specs=(
            P(("groups", "tok", "nout"), "kin"),
            P(("groups", "tok", "nout"), "kin"),
            P(("groups", "kin", "tok"), "nout"),
            P(("groups", "nout"), ("kin", "tok")),
            P(("groups", "nout")),
            P(("groups", "kin")),
        ),
        check_vma=False,
    )
```

```python
import functools

import jax
import jax.numpy as jnp
from jax import lax
from jax.experimental import pallas as pl
from jax.experimental.pallas import tpu as pltpu
from jax.sharding import PartitionSpec as P

inv_root_two = 0.7071067811865476
inv_root_two_pi = 0.3989422804014327

MIB = 1 << 20
bf16, f32 = jnp.bfloat16, jnp.float32
like = jax.ShapeDtypeStruct
whole = pl.BlockSpec(memory_space=pltpu.VMEM)
hbm = pl.BlockSpec(memory_space=pltpu.HBM)
swap = [(0, 1), (1, 0)]


def gelu_parts(hidden):
    normal_cdf = 0.5 * (1.0 + lax.erf(hidden * inv_root_two))
    density = jnp.exp(-0.5 * hidden * hidden) * inv_root_two_pi
    return (hidden * normal_cdf, normal_cdf + hidden * density)


def dot(left, right, left_dim, right_dim):
    return lax.dot_general(
        left, right, (((left_dim,), (right_dim,)), ((), ())), preferred_element_type=jnp.float32
    )


def exchange(chunks, axes):
    return lax.all_to_all(chunks, axes, split_axis=0, concat_axis=0, tiled=True)


def tile_of(size, most):
    return max(t for t in range(128, most + 1, 128) if size % t == 0)


def tiles_of(size, most=512):
    tile = tile_of(size, most)
    return [pl.ds(i * tile, tile) for i in range(size // tile)]


def call(body, name, outs, grant=4 * MIB, flops=0, moved=0, scratch=(), resident=True, specs=None):
    shapes = [pltpu.VMEM(o.shape, o.dtype) if resident else o for o in outs]

    def run(*args):
        cost = pl.CostEstimate(flops=flops, bytes_accessed=moved, transcendentals=0)
        return pl.pallas_call(
            body,
            out_shape=shapes,
            in_specs=specs or [whole] * len(args),
            out_specs=[whole] * len(outs),
            scratch_shapes=list(scratch),
            cost_estimate=cost,
            compiler_params=pltpu.CompilerParams(vmem_limit_bytes=grant),
            name=name,
        )(*args)

    return run


def kept(array):
    return pltpu.with_memory_space_constraint(array, pltpu.VMEM)


def in_hbm(array):
    return pltpu.with_memory_space_constraint(array, pltpu.HBM)


def apart(mixed, rows):
    total, wide = mixed.shape
    tiles = mixed.reshape(total // (4 * rows), 2, 2 * rows, wide)
    even, odd = tiles[:, 0], tiles[:, 1]
    is_low = lax.broadcasted_iota(jnp.int32, even.shape, 1) < rows
    first = jnp.where(is_low, even, pltpu.roll(odd, rows, 1))
    second = jnp.where(is_low, pltpu.roll(even, rows, 1), odd)
    return first.reshape(total // 2, wide), second.reshape(total // 2, wide)


def together(first, second, rows):
    total, wide = first.shape
    first = first.reshape(total // (2 * rows), 2 * rows, wide)
    second = second.reshape(total // (2 * rows), 2 * rows, wide)
    is_low = lax.broadcasted_iota(jnp.int32, first.shape, 1) < rows
    even = jnp.where(is_low, first, pltpu.roll(second, rows, 1))
    odd = jnp.where(is_low, pltpu.roll(first, rows, 1), second)
    return jnp.stack([even, odd], axis=1).reshape(2 * total, wide)


def ordered(me, own, far, axis=0):
    low, high = jnp.where(me == 0, own, far), jnp.where(me == 0, far, own)
    return jnp.concatenate([low, high], axis=axis)


def half_of(size, mine):
    core = lax.axis_index("kin")
    at = core if mine else 1 - core
    return pl.ds(pl.multiple_of(at * size, size), size)


def quarters(source, target, sems):
    size = target.shape[0] // 4
    return [
        pltpu.make_async_copy(source.at[part, :], target.at[part, :], sems.at[i])
        for i, part in enumerate(pl.ds(j * size, size) for j in range(4))
    ]


def load_far_body(hbm_ref, after_ref, out_ref, sems):
    copies = quarters(hbm_ref.at[half_of(out_ref.shape[0], False), :], out_ref, sems)
    for copy in copies:
        copy.start()
    for copy in copies:
        copy.wait()


def load_body(in_hbm_ref, out_hbm_ref, after_ref, far_ref, own_ref, out_ref, sems):
    half = own_ref.shape[1]
    copies = quarters(in_hbm_ref.at[:, half_of(half, False)], far_ref, sems.at[0])
    copies += quarters(in_hbm_ref.at[:, half_of(half, True)], own_ref, sems.at[1])
    copies += quarters(out_hbm_ref.at[half_of(half, True), :], out_ref, sems.at[2])
    for copy in copies:
        copy.start()
    for copy in copies:
        copy.wait()


def pair_body(own_ref, got_ref, after_ref, out_ref):
    out_ref[...] = ordered(lax.axis_index("tok"), own_ref[...], got_ref[...])


def partial_sums(x_cols, dy_cols, w_in_ref, w_out_ref, out_ref):
    count = x_cols.shape[0]
    for at in tiles_of(out_ref.shape[1]):
        out_ref[:count, at] = dot(x_cols, w_in_ref[:, at], 1, 0).astype(bf16)
        out_ref[count:, at] = dot(dy_cols, w_out_ref[at, :], 1, 1).astype(bf16)


def far_half_body(rows, count, *refs):
    *piece_refs, w_in_ref, w_out_ref = refs[: count + 2]
    sent_ref, x_ref, dy_ref, sums_ref = refs[count + 2 :]
    mixed = jnp.concatenate([ref[...] for ref in piece_refs], axis=0)
    x_cols, dy_cols = apart(mixed.astype(f32), rows)
    sums_ref[...] = jnp.sum(dy_cols, axis=0, keepdims=True)
    x_cols, dy_cols = x_cols.astype(bf16), dy_cols.astype(bf16)
    x_ref[...], dy_ref[...] = x_cols, dy_cols
    partial_sums(x_cols, dy_cols, w_in_ref, w_out_ref, sent_ref)


def own_half_body(x_ref, dy_ref, w_in_ref, w_out_ref, own_ref):
    partial_sums(x_ref[...], dy_ref[...], w_in_ref, w_out_ref, own_ref)


def add_body(left_ref, right_ref, out_ref):
    out_ref[...] = (left_ref[...].astype(f32) + right_ref[...].astype(f32)).astype(bf16)


def gelu_body(bias_ref, after_ref, own_ref, other_ref, out_ref):
    count, half = out_ref.shape[0] // 2, out_ref.shape[1]
    bias = bias_ref[:, half_of(half, True)]
    tile = tile_of(half, 512)
    for i in range(half // tile):
        at = pl.ds(i * tile, tile)
        summed = own_ref[:, at].astype(f32) + other_ref[:, at].astype(f32)
        activated, slopes = gelu_parts(summed[:count] + bias[:, i * tile : (i + 1) * tile])
        out_ref[:count, at] = activated.astype(bf16)
        out_ref[count:, at] = (summed[count:] * slopes).astype(bf16)


def own_terms_body(both_ref, w_in_ref, w_out_ref, out_ref):
    count = both_ref.shape[0] // 2
    act, grad = both_ref[:count], both_ref[count:]
    for at in tiles_of(out_ref.shape[1]):
        out_ref[:count, at] = dot(act, w_out_ref[:, at], 1, 0)
        out_ref[count:, at] = dot(grad, w_in_ref[at, :], 1, 1)


def blocks_body(rows, own_ref, far_ref, terms_ref, w_in_ref, w_out_ref, act_ref, grad_ref, *out_refs):
    count = far_ref.shape[0] // 2
    core = lax.axis_index("kin")
    act, grad = far_ref[:count], far_ref[count:]
    act_ref[...] = ordered(core, own_ref[:count], act, 1)
    grad_ref[...] = ordered(core, own_ref[count:], grad, 1)
    size = out_refs[0].shape[0]
    for at in tiles_of(terms_ref.shape[1]):
        forward = terms_ref[:count, at] + dot(act, w_out_ref[:, at], 1, 0)
        backward = terms_ref[count:, at] + dot(grad, w_in_ref[at, :], 1, 1)
        terms = together(forward, backward, rows).astype(bf16)
        for i, out_ref in enumerate(out_refs):
            out_ref[:, at] = terms[i * size : (i + 1) * size]


def outer_body(most, left_ref, right_ref, out_hbm, block_ref, sems):
    copies = []
    for i, at in enumerate(tiles_of(out_hbm.shape[0], 256)):
        left = left_ref[:, at].T
        for part in tiles_of(out_hbm.shape[1], most):
            block_ref[at, part] = dot(left, right_ref[:, part], 1, 0).astype(bf16)
        copies.append(
            pltpu.make_async_copy(block_ref.at[at, :], out_hbm.at[at, :], sems.at[i])
        )
        copies[-1].start()
    for copy in copies:
        copy.wait()


def outer(left, right, name, most):
    count, high = left.shape
    wide = right.shape[1]
    return pl.pallas_call(
        functools.partial(outer_body, most),
        out_shape=like((high, wide), bf16),
        in_specs=[whole] * 2,
        out_specs=pl.BlockSpec(memory_space=pl.ANY),
        scratch_shapes=[
            pltpu.VMEM((high, wide), bf16),
            pltpu.SemaphoreType.DMA((len(tiles_of(high, 256)),)),
        ],
        cost_estimate=pl.CostEstimate(
            flops=2 * count * wide * high, bytes_accessed=2 * wide * high, transcendentals=0
        ),
        compiler_params=pltpu.CompilerParams(vmem_limit_bytes=16 * MIB),
        name=name,
    )(kept(left), kept(right))


def sum_body(rows, bias_ref, *refs):
    *term_refs, own_ref, sent_ref = refs
    wide = own_ref.shape[1]
    me = lax.axis_index("tok")
    summed = sum(ref[...].astype(f32) for ref in term_refs)
    bias = jnp.where(me == 0, bias_ref[:, :wide], bias_ref[:, wide:])
    is_fwd = lax.rem(lax.broadcasted_iota(jnp.int32, summed.shape, 0), 2 * rows) < rows
    summed = summed + jnp.where(is_fwd, bias, 0.0)
    low, high = summed[: 2 * rows], summed[2 * rows :]
    own_ref[...] = jnp.where(me == 0, low, high).astype(bf16)
    sent_ref[...] = jnp.where(me == 0, high, low).astype(bf16)


def final_body(
    rows, own_ref, got_ref, own_sums_ref, got_sums_ref, hidden_ref, rows_ref, grad_ref, sums_ref, bias_ref
):
    wide = own_ref.shape[1]
    me = lax.axis_index("tok")
    own, got = own_ref[...].astype(f32), got_ref[...].astype(f32)
    own_sums, got_sums = own_sums_ref[...], got_sums_ref[...]
    for i in range(2):
        at = pl.ds(i * wide, wide)
        part = jnp.where(me == i, own, got)
        rows_ref[:, at] = part[:rows].astype(bf16)
        grad_ref[:, at] = part[rows:].astype(bf16)
        sums_ref[:, at] = jnp.where(me == i, own_sums, got_sums)
    bias_ref[...] = jnp.sum(hidden_ref[...].astype(f32), axis=0, keepdims=True)


def make_small(nn):
    def across(array, shift):
        return lax.ppermute(array, "nout", [(i, i ^ shift) for i in range(nn)])

    def on_device(tokens, weight_in, bias_in, weight_out, bias_out, grad_out):
        rows, cols = tokens.shape
        wide, hid = weight_in.shape
        half = hid // 2
        pair = 2 * rows
        count = 2 * nn * rows
        work = 4 * count * wide * half
        piece = 2 * wide * half
        sem = pltpu.SemaphoreType.DMA

        mine = jnp.concatenate([tokens, grad_out], axis=0)
        me = lax.axis_index("tok")
        own = lax.dynamic_slice_in_dim(mine, me * wide, wide, 1)
        sent = lax.dynamic_slice_in_dim(mine, (1 - me) * wide, wide, 1)
        got = lax.ppermute(sent, "tok", swap)
        (out_far,) = call(
            load_far_body,
            "load_far",
            [like((half, wide), bf16)],
            grant=MIB,
            moved=piece,
            scratch=[sem((4,))],
            specs=[hbm, pl.BlockSpec(memory_space=pl.ANY)],
        )(in_hbm(weight_out), sent)
        (tiles,) = call(pair_body, "pair_tiles", [like((2 * pair, wide), bf16)])(
            kept(own), kept(got), kept(out_far)
        )
        pieces = [across(tiles, shift) for shift in reversed(range(1, nn))] + [tiles]
        in_far, in_own, out_own = call(
            load_body,
            "load_rest",
            [like((wide, half), bf16)] * 2 + [like((half, wide), bf16)],
            grant=MIB,
            moved=3 * piece,
            scratch=[sem((3, 4))],
            specs=[hbm] * 2 + [pl.BlockSpec(memory_space=pl.ANY)],
        )(in_hbm(weight_in), in_hbm(weight_out), tiles)

        sent, x_cols, dy_cols, sums = call(
            functools.partial(far_half_body, rows, nn),
            "far_half",
            [like((2 * count, half), bf16)]
            + [like((count, wide), bf16)] * 2
            + [like((1, wide), f32)],
            grant=8 * MIB,
            flops=work,
            moved=2 * piece,
        )(*[kept(piece) for piece in pieces], kept(in_far), kept(out_far))
        got = lax.ppermute(sent, "kin", swap)
        (own,) = call(
            own_half_body,
            "own_half",
            [like((2 * count, half), bf16)],
            grant=8 * MIB,
            flops=work,
            moved=2 * piece,
        )(kept(x_cols), kept(dy_cols), kept(in_own), kept(out_own))
        (own,) = call(add_body, "add_cores", [like((2 * count, half), bf16)])(kept(own), kept(got))
        other = lax.ppermute(own, "tok", swap)
        got_sums = lax.ppermute(sums, "tok", swap)
        (both,) = call(gelu_body, "gelu", [like((2 * count, half), bf16)])(
            bias_in.reshape(1, hid), got_sums, kept(own), kept(other)
        )
        far = lax.ppermute(both, "kin", swap)
        (terms,) = call(
            own_terms_body,
            "own_terms",
            [like((2 * count, wide), f32)],
            grant=8 * MIB,
            flops=work,
            moved=2 * piece,
        )(kept(both), kept(in_own), kept(out_own))
        act, grad, *blocks = call(
            functools.partial(blocks_body, rows),
            "output_blocks",
            [like((count, hid), bf16)] * 2 + [like((2 * pair, wide), bf16)] * nn,
            grant=8 * MIB,
            flops=work,
            moved=2 * piece,
        )(kept(both), kept(far), kept(terms), kept(in_far), kept(out_far))

        weight_in_grad = outer(x_cols, grad, "weight_in_grad", 256)
        weight_out_grad = outer(act, dy_cols, "weight_out_grad", 1536)

        terms = [across(blocks[i], nn - 1 - i) for i in range(nn - 1)] + [blocks[-1]]
        own, sent = call(
            functools.partial(sum_body, rows), "sum_blocks", [like((pair, wide), bf16)] * 2
        )(bias_out.reshape(1, cols), *[kept(term) for term in terms])
        got = lax.ppermute(sent, "tok", swap)
        output_rows, grad_tokens, bias_out_grad, bias_in_grad = call(
            functools.partial(final_body, rows),
            "final_rows",
            [like((rows, cols), bf16)] * 2 + [like((1, cols), f32), like((1, hid), f32)],
            resident=False,
        )(kept(own), kept(got), kept(sums), kept(got_sums), kept(grad))
        return (
            output_rows,
            grad_tokens,
            weight_in_grad,
            weight_out_grad,
            bias_in_grad.reshape(hid),
            bias_out_grad.reshape(cols),
        )

    return on_device


def make_plain(nt, nk, nn):
    spread, square = nt * nn, nk * nt

    def on_device(tokens, weight_in, bias_in, weight_out, bias_out, grad_out):
        rows, cols = tokens.shape
        wide, hid = weight_in.shape
        part = hid // square
        pair = 2 * rows
        total = pair * spread

        mine = jnp.concatenate([tokens, grad_out], axis=0)
        by_owner = mine.reshape(pair, nt, wide).transpose(1, 0, 2)
        chunks = jnp.broadcast_to(by_owner[:, None], (nt, nn, pair, wide))
        mixed = exchange(chunks.reshape(spread, pair, wide), ("tok", "nout")).reshape(total, wide)
        is_fwd = (lax.broadcasted_iota(jnp.int32, (total, 1), 0) % pair) < rows

        col_sums = jnp.sum(jnp.where(is_fwd, 0.0, mixed.astype(jnp.float32)), axis=0)
        bias_out_grad = lax.all_gather(col_sums, "tok", axis=0, tiled=True)

        partial = jnp.where(is_fwd, dot(mixed, weight_in, 1, 0), dot(mixed, weight_out, 1, 1))
        partial = partial.astype(jnp.bfloat16).reshape(total, square, part).transpose(1, 0, 2)
        got = exchange(partial, ("kin", "tok"))
        summed = jnp.sum(got.astype(jnp.float32), axis=0).reshape(spread, 2, rows, part)
        at = lax.axis_index(("kin", "tok"))
        pre_act = summed[:, 0] + lax.dynamic_slice_in_dim(bias_in, at * part, part)
        activated, slopes = gelu_parts(pre_act)
        grad_pre = summed[:, 1] * slopes
        both = jnp.stack([activated, grad_pre], axis=1).astype(jnp.bfloat16).reshape(total, part)
        both = exchange(jnp.broadcast_to(both[None], (square, total, part)), ("kin", "tok"))
        both = both.transpose(1, 0, 2).reshape(total, hid)

        split = both.reshape(spread, 2, rows, hid)
        act = split[:, 0].reshape(spread * rows, hid)
        grad_half = split[:, 1].reshape(spread * rows, hid)
        split = mixed.reshape(spread, 2, rows, wide)
        x_cols = split[:, 0].reshape(spread * rows, wide)
        dy_cols = split[:, 1].reshape(spread * rows, wide)
        bias_in_grad = jnp.sum(grad_half.astype(jnp.float32), axis=0)

        block = jnp.stack(
            [
                dot(act, weight_out, 1, 0).reshape(spread, rows, wide),
                dot(grad_half, weight_in, 1, 1).reshape(spread, rows, wide),
            ],
            axis=1,
        )
        block = block.astype(jnp.bfloat16).reshape(spread, pair, wide)
        back = exchange(block, ("tok", "nout")).reshape(nt, nn, pair, wide)
        weight_in_grad = dot(x_cols, grad_half, 0, 0).astype(jnp.bfloat16)
        weight_out_grad = dot(act, dy_cols, 0, 0).astype(jnp.bfloat16)
        final = jnp.sum(back.astype(jnp.float32), axis=1).transpose(1, 0, 2).reshape(pair, cols)
        output_rows = (final[:rows] + bias_out).astype(jnp.bfloat16)
        grad_tokens = final[rows:].astype(jnp.bfloat16)
        return (output_rows, grad_tokens, weight_in_grad, weight_out_grad, bias_in_grad, bias_out_grad)

    return on_device


def solution(mesh):
    nt, nk, nn = mesh.shape["tok"], mesh.shape["kin"], mesh.shape["nout"]
    return jax.shard_map(
        make_small(nn) if (nt, nk) == (2, 2) and nn in (2, 4) else make_plain(nt, nk, nn),
        mesh=mesh,
        in_specs=(
            P(("groups", "tok", "nout"), "kin"),
            P(("kin", "tok"), "nout"),
            P("nout"),
            P("nout", ("kin", "tok")),
            P("kin"),
            P(("groups", "tok", "nout"), "kin"),
        ),
        out_specs=(
            P(("groups", "tok", "nout"), "kin"),
            P(("groups", "tok", "nout"), "kin"),
            P(("groups", "kin", "tok"), "nout"),
            P(("groups", "nout"), ("kin", "tok")),
            P(("groups", "nout")),
            P(("groups", "kin")),
        ),
        check_vma=False,
    )
```

```python
import functools

import jax
import jax.numpy as jnp
from jax import lax
from jax.experimental import pallas as pl
from jax.experimental.pallas import tpu as pltpu
from jax.sharding import PartitionSpec as P

inv_root_two = 0.7071067811865476
inv_root_two_pi = 0.3989422804014327

MIB = 1 << 20
bf16, f32 = jnp.bfloat16, jnp.float32
like = jax.ShapeDtypeStruct
whole = pl.BlockSpec(memory_space=pltpu.VMEM)
hbm = pl.BlockSpec(memory_space=pltpu.HBM)
swap = [(0, 1), (1, 0)]


def gelu_parts(hidden):
    normal_cdf = 0.5 * (1.0 + lax.erf(hidden * inv_root_two))
    density = jnp.exp(-0.5 * hidden * hidden) * inv_root_two_pi
    return (hidden * normal_cdf, normal_cdf + hidden * density)


def dot(left, right, left_dim, right_dim):
    return lax.dot_general(
        left, right, (((left_dim,), (right_dim,)), ((), ())), preferred_element_type=jnp.float32
    )


def exchange(chunks, axes):
    return lax.all_to_all(chunks, axes, split_axis=0, concat_axis=0, tiled=True)


def tile_of(size, most):
    return max(t for t in range(128, most + 1, 128) if size % t == 0)


def tiles_of(size, most=512):
    tile = tile_of(size, most)
    return [pl.ds(i * tile, tile) for i in range(size // tile)]


def call(body, name, outs, grant=4 * MIB, flops=0, moved=0, scratch=(), resident=True, specs=None):
    shapes = [pltpu.VMEM(o.shape, o.dtype) if resident else o for o in outs]

    def run(*args):
        cost = pl.CostEstimate(flops=flops, bytes_accessed=moved, transcendentals=0)
        return pl.pallas_call(
            body,
            out_shape=shapes,
            in_specs=specs or [whole] * len(args),
            out_specs=[whole] * len(outs),
            scratch_shapes=list(scratch),
            cost_estimate=cost,
            compiler_params=pltpu.CompilerParams(vmem_limit_bytes=grant),
            name=name,
        )(*args)

    return run


def kept(array):
    return pltpu.with_memory_space_constraint(array, pltpu.VMEM)


def in_hbm(array):
    return pltpu.with_memory_space_constraint(array, pltpu.HBM)


def apart(mixed, rows):
    total, wide = mixed.shape
    tiles = mixed.reshape(total // (4 * rows), 2, 2 * rows, wide)
    even, odd = tiles[:, 0], tiles[:, 1]
    is_low = lax.broadcasted_iota(jnp.int32, even.shape, 1) < rows
    first = jnp.where(is_low, even, pltpu.roll(odd, rows, 1))
    second = jnp.where(is_low, pltpu.roll(even, rows, 1), odd)
    return first.reshape(total // 2, wide), second.reshape(total // 2, wide)


def together(first, second, rows):
    total, wide = first.shape
    first = first.reshape(total // (2 * rows), 2 * rows, wide)
    second = second.reshape(total // (2 * rows), 2 * rows, wide)
    is_low = lax.broadcasted_iota(jnp.int32, first.shape, 1) < rows
    even = jnp.where(is_low, first, pltpu.roll(second, rows, 1))
    odd = jnp.where(is_low, pltpu.roll(first, rows, 1), second)
    return jnp.stack([even, odd], axis=1).reshape(2 * total, wide)


def ordered(me, own, far, axis=0):
    low, high = jnp.where(me == 0, own, far), jnp.where(me == 0, far, own)
    return jnp.concatenate([low, high], axis=axis)


def half_of(size, mine):
    core = lax.axis_index("kin")
    at = core if mine else 1 - core
    return pl.ds(pl.multiple_of(at * size, size), size)


def quarters(source, target, sems):
    size = target.shape[0] // 4
    return [
        pltpu.make_async_copy(source.at[part, :], target.at[part, :], sems.at[i])
        for i, part in enumerate(pl.ds(j * size, size) for j in range(4))
    ]


def load_far_body(hbm_ref, after_ref, out_ref, sems):
    copies = quarters(hbm_ref.at[half_of(out_ref.shape[0], False), :], out_ref, sems)
    for copy in copies:
        copy.start()
    for copy in copies:
        copy.wait()


def load_body(in_hbm_ref, out_hbm_ref, after_ref, far_ref, own_ref, out_ref, sems):
    half = own_ref.shape[1]
    copies = quarters(in_hbm_ref.at[:, half_of(half, False)], far_ref, sems.at[0])
    copies += quarters(in_hbm_ref.at[:, half_of(half, True)], own_ref, sems.at[1])
    copies += quarters(out_hbm_ref.at[half_of(half, True), :], out_ref, sems.at[2])
    for copy in copies:
        copy.start()
    for copy in copies:
        copy.wait()


def pair_body(own_ref, got_ref, after_ref, out_ref):
    out_ref[...] = ordered(lax.axis_index("tok"), own_ref[...], got_ref[...])


def far_pre_body(rows, count, *refs):
    *piece_refs, w_in_ref = refs[: count + 1]
    sent_ref, x_ref, dy_ref, sums_ref = refs[count + 1 :]
    mixed = jnp.concatenate([ref[...] for ref in piece_refs], axis=0)
    x_cols, dy_cols = apart(mixed.astype(f32), rows)
    sums_ref[...] = jnp.sum(dy_cols, axis=0, keepdims=True)
    x_cols, dy_cols = x_cols.astype(bf16), dy_cols.astype(bf16)
    x_ref[...], dy_ref[...] = x_cols, dy_cols
    for at in tiles_of(sent_ref.shape[1]):
        sent_ref[:, at] = dot(x_cols, w_in_ref[:, at], 1, 0).astype(bf16)


def far_grad_body(dy_ref, w_out_ref, sent_ref):
    dy_cols = dy_ref[...]
    for at in tiles_of(sent_ref.shape[1]):
        sent_ref[:, at] = dot(dy_cols, w_out_ref[at, :], 1, 1).astype(bf16)


def own_pre_body(x_ref, w_in_ref, got_ref, after_ref, own_ref):
    x_cols = x_ref[...]
    for at in tiles_of(own_ref.shape[1]):
        own = dot(x_cols, w_in_ref[:, at], 1, 0) + got_ref[:, at].astype(f32)
        own_ref[:, at] = own.astype(bf16)


def own_grad_body(dy_ref, w_out_ref, got_ref, after_ref, own_ref):
    dy_cols = dy_ref[...]
    for at in tiles_of(own_ref.shape[1]):
        own = dot(dy_cols, w_out_ref[at, :], 1, 1) + got_ref[:, at].astype(f32)
        own_ref[:, at] = own.astype(bf16)


def gelu_body(bias_ref, own_ref, other_ref, after_ref, act_ref, slopes_ref):
    half = act_ref.shape[1]
    bias = bias_ref[:, half_of(half, True)]
    tile = tile_of(half, 512)
    for i in range(half // tile):
        at = pl.ds(i * tile, tile)
        pre_act = own_ref[:, at].astype(f32) + other_ref[:, at].astype(f32)
        activated, slopes = gelu_parts(pre_act + bias[:, i * tile : (i + 1) * tile])
        act_ref[:, at] = activated.astype(bf16)
        slopes_ref[:, at] = slopes


def grad_pre_body(slopes_ref, own_ref, other_ref, after_ref, sums_ref, grad_ref):
    grad_act = own_ref[...].astype(f32) + other_ref[...].astype(f32)
    grad_ref[...] = (grad_act * slopes_ref[...]).astype(bf16)


def own_forward_body(act_ref, w_out_ref, out_ref):
    act = act_ref[...]
    for at in tiles_of(out_ref.shape[1]):
        out_ref[:, at] = dot(act, w_out_ref[:, at], 1, 0)


def far_forward_body(own_ref, far_ref, w_out_ref, terms_ref, act_ref, out_ref):
    act = far_ref[...]
    act_ref[...] = ordered(lax.axis_index("kin"), own_ref[...], act, 1)
    for at in tiles_of(out_ref.shape[1]):
        out_ref[:, at] = terms_ref[:, at] + dot(act, w_out_ref[:, at], 1, 0)


def own_backward_body(grad_ref, w_in_ref, out_ref):
    grad = grad_ref[...]
    for at in tiles_of(out_ref.shape[1]):
        out_ref[:, at] = dot(grad, w_in_ref[at, :], 1, 1)


def blocks_body(rows, own_ref, far_ref, forward_ref, backward_ref, w_in_ref, grad_ref, *out_refs):
    grad = far_ref[...]
    grad_ref[...] = ordered(lax.axis_index("kin"), own_ref[...], grad, 1)
    size = out_refs[0].shape[0]
    for at in tiles_of(forward_ref.shape[1]):
        backward = backward_ref[:, at] + dot(grad, w_in_ref[at, :], 1, 1)
        terms = together(forward_ref[:, at], backward, rows).astype(bf16)
        for i, out_ref in enumerate(out_refs):
            out_ref[:, at] = terms[i * size : (i + 1) * size]


def outer_body(most, left_ref, right_ref, out_hbm, block_ref, sems):
    copies = []
    for i, at in enumerate(tiles_of(out_hbm.shape[0], 256)):
        left = left_ref[:, at].T
        for part in tiles_of(out_hbm.shape[1], most):
            block_ref[at, part] = dot(left, right_ref[:, part], 1, 0).astype(bf16)
        copies.append(
            pltpu.make_async_copy(block_ref.at[at, :], out_hbm.at[at, :], sems.at[i])
        )
        copies[-1].start()
    for copy in copies:
        copy.wait()


def outer(left, right, name, most):
    count, high = left.shape
    wide = right.shape[1]
    return pl.pallas_call(
        functools.partial(outer_body, most),
        out_shape=like((high, wide), bf16),
        in_specs=[whole] * 2,
        out_specs=pl.BlockSpec(memory_space=pl.ANY),
        scratch_shapes=[
            pltpu.VMEM((high, wide), bf16),
            pltpu.SemaphoreType.DMA((len(tiles_of(high, 256)),)),
        ],
        cost_estimate=pl.CostEstimate(
            flops=2 * count * wide * high, bytes_accessed=2 * wide * high, transcendentals=0
        ),
        compiler_params=pltpu.CompilerParams(vmem_limit_bytes=16 * MIB),
        name=name,
    )(kept(left), kept(right))


def sum_body(rows, bias_ref, *refs):
    *term_refs, own_ref, sent_ref = refs
    wide = own_ref.shape[1]
    me = lax.axis_index("tok")
    summed = sum(ref[...].astype(f32) for ref in term_refs)
    bias = jnp.where(me == 0, bias_ref[:, :wide], bias_ref[:, wide:])
    is_fwd = lax.rem(lax.broadcasted_iota(jnp.int32, summed.shape, 0), 2 * rows) < rows
    summed = summed + jnp.where(is_fwd, bias, 0.0)
    low, high = summed[: 2 * rows], summed[2 * rows :]
    own_ref[...] = jnp.where(me == 0, low, high).astype(bf16)
    sent_ref[...] = jnp.where(me == 0, high, low).astype(bf16)


def final_body(
    rows, own_ref, got_ref, own_sums_ref, got_sums_ref, hidden_ref, rows_ref, grad_ref, sums_ref, bias_ref
):
    wide = own_ref.shape[1]
    me = lax.axis_index("tok")
    own, got = own_ref[...].astype(f32), got_ref[...].astype(f32)
    own_sums, got_sums = own_sums_ref[...], got_sums_ref[...]
    for i in range(2):
        at = pl.ds(i * wide, wide)
        part = jnp.where(me == i, own, got)
        rows_ref[:, at] = part[:rows].astype(bf16)
        grad_ref[:, at] = part[rows:].astype(bf16)
        sums_ref[:, at] = jnp.where(me == i, own_sums, got_sums)
    bias_ref[...] = jnp.sum(hidden_ref[...].astype(f32), axis=0, keepdims=True)


def make_small(nn):
    def across(array, shift):
        return lax.ppermute(array, "nout", [(i, i ^ shift) for i in range(nn)])

    def on_device(tokens, weight_in, bias_in, weight_out, bias_out, grad_out):
        rows, cols = tokens.shape
        wide, hid = weight_in.shape
        half = hid // 2
        pair = 2 * rows
        count = 2 * nn * rows
        piece = 2 * wide * half
        sem = pltpu.SemaphoreType.DMA

        mine = jnp.concatenate([tokens, grad_out], axis=0)
        me = lax.axis_index("tok")
        own = lax.dynamic_slice_in_dim(mine, me * wide, wide, 1)
        sent = lax.dynamic_slice_in_dim(mine, (1 - me) * wide, wide, 1)
        got = lax.ppermute(sent, "tok", swap)
        (out_far,) = call(
            load_far_body,
            "load_far",
            [like((half, wide), bf16)],
            grant=MIB,
            moved=piece,
            scratch=[sem((4,))],
            specs=[hbm, pl.BlockSpec(memory_space=pl.ANY)],
        )(in_hbm(weight_out), sent)
        (tiles,) = call(pair_body, "pair_tiles", [like((2 * pair, wide), bf16)])(
            kept(own), kept(got), kept(out_far)
        )
        pieces = [across(tiles, shift) for shift in reversed(range(1, nn))] + [tiles]
        in_far, in_own, out_own = call(
            load_body,
            "load_rest",
            [like((wide, half), bf16)] * 2 + [like((half, wide), bf16)],
            grant=MIB,
            moved=3 * piece,
            scratch=[sem((3, 4))],
            specs=[hbm] * 2 + [pl.BlockSpec(memory_space=pl.ANY)],
        )(in_hbm(weight_in), in_hbm(weight_out), tiles)

        def product(body, name, outs, *args):
            return call(body, name, outs, grant=8 * MIB)(*map(kept, args))

        side, ends = like((count, half), bf16), like((count, wide), f32)
        sent, x_cols, dy_cols, sums = product(
            functools.partial(far_pre_body, rows, nn),
            "far_pre",
            [side] + [like((count, wide), bf16)] * 2 + [like((1, wide), f32)],
            *pieces,
            in_far,
        )
        got_pre = lax.ppermute(sent, "kin", swap)
        (sent,) = product(far_grad_body, "far_grad", [side], dy_cols, out_far)
        got_grad = lax.ppermute(sent, "kin", swap)
        (own_pre,) = product(own_pre_body, "own_pre", [side], x_cols, in_own, got_pre, sent)
        other_pre = lax.ppermute(own_pre, "tok", swap)
        (own_grad,) = product(
            own_grad_body, "own_grad", [side], dy_cols, out_own, got_grad, own_pre
        )
        other_grad = lax.ppermute(own_grad, "tok", swap)
        got_sums = lax.ppermute(sums, "tok", swap)
        act_own, slopes = call(gelu_body, "gelu", [side, like((count, half), f32)])(
            bias_in.reshape(1, hid), kept(own_pre), kept(other_pre), kept(own_grad)
        )
        act_far = lax.ppermute(act_own, "kin", swap)
        (forward,) = product(own_forward_body, "own_forward", [ends], act_own, out_own)
        (grad_own,) = call(grad_pre_body, "grad_pre", [side])(
            kept(slopes), kept(own_grad), kept(other_grad), kept(forward), kept(got_sums)
        )
        act, forward = product(
            far_forward_body,
            "far_forward",
            [like((count, hid), bf16), ends],
            act_own,
            act_far,
            out_far,
            forward,
        )
        grad_far = lax.ppermute(grad_own, "kin", swap)
        (backward,) = product(own_backward_body, "own_backward", [ends], grad_own, in_own)
        grad, *blocks = product(
            functools.partial(blocks_body, rows),
            "output_blocks",
            [like((count, hid), bf16)] + [like((2 * pair, wide), bf16)] * nn,
            grad_own,
            grad_far,
            forward,
            backward,
            in_far,
        )

        weight_in_grad = outer(x_cols, grad, "weight_in_grad", 256)
        weight_out_grad = outer(act, dy_cols, "weight_out_grad", 1536)

        terms = [across(blocks[i], nn - 1 - i) for i in range(nn - 1)] + [blocks[-1]]
        own, sent = call(
            functools.partial(sum_body, rows), "sum_blocks", [like((pair, wide), bf16)] * 2
        )(bias_out.reshape(1, cols), *[kept(term) for term in terms])
        got = lax.ppermute(sent, "tok", swap)
        output_rows, grad_tokens, bias_out_grad, bias_in_grad = call(
            functools.partial(final_body, rows),
            "final_rows",
            [like((rows, cols), bf16)] * 2 + [like((1, cols), f32), like((1, hid), f32)],
            resident=False,
        )(kept(own), kept(got), kept(sums), kept(got_sums), kept(grad))
        return (
            output_rows,
            grad_tokens,
            weight_in_grad,
            weight_out_grad,
            bias_in_grad.reshape(hid),
            bias_out_grad.reshape(cols),
        )

    return on_device


def make_plain(nt, nk, nn):
    spread, square = nt * nn, nk * nt

    def on_device(tokens, weight_in, bias_in, weight_out, bias_out, grad_out):
        rows, cols = tokens.shape
        wide, hid = weight_in.shape
        part = hid // square
        pair = 2 * rows
        total = pair * spread

        mine = jnp.concatenate([tokens, grad_out], axis=0)
        by_owner = mine.reshape(pair, nt, wide).transpose(1, 0, 2)
        chunks = jnp.broadcast_to(by_owner[:, None], (nt, nn, pair, wide))
        mixed = exchange(chunks.reshape(spread, pair, wide), ("tok", "nout")).reshape(total, wide)
        is_fwd = (lax.broadcasted_iota(jnp.int32, (total, 1), 0) % pair) < rows

        col_sums = jnp.sum(jnp.where(is_fwd, 0.0, mixed.astype(jnp.float32)), axis=0)
        bias_out_grad = lax.all_gather(col_sums, "tok", axis=0, tiled=True)

        partial = jnp.where(is_fwd, dot(mixed, weight_in, 1, 0), dot(mixed, weight_out, 1, 1))
        partial = partial.astype(jnp.bfloat16).reshape(total, square, part).transpose(1, 0, 2)
        got = exchange(partial, ("kin", "tok"))
        summed = jnp.sum(got.astype(jnp.float32), axis=0).reshape(spread, 2, rows, part)
        at = lax.axis_index(("kin", "tok"))
        pre_act = summed[:, 0] + lax.dynamic_slice_in_dim(bias_in, at * part, part)
        activated, slopes = gelu_parts(pre_act)
        grad_pre = summed[:, 1] * slopes
        both = jnp.stack([activated, grad_pre], axis=1).astype(jnp.bfloat16).reshape(total, part)
        both = exchange(jnp.broadcast_to(both[None], (square, total, part)), ("kin", "tok"))
        both = both.transpose(1, 0, 2).reshape(total, hid)

        split = both.reshape(spread, 2, rows, hid)
        act = split[:, 0].reshape(spread * rows, hid)
        grad_half = split[:, 1].reshape(spread * rows, hid)
        split = mixed.reshape(spread, 2, rows, wide)
        x_cols = split[:, 0].reshape(spread * rows, wide)
        dy_cols = split[:, 1].reshape(spread * rows, wide)
        bias_in_grad = jnp.sum(grad_half.astype(jnp.float32), axis=0)

        block = jnp.stack(
            [
                dot(act, weight_out, 1, 0).reshape(spread, rows, wide),
                dot(grad_half, weight_in, 1, 1).reshape(spread, rows, wide),
            ],
            axis=1,
        )
        block = block.astype(jnp.bfloat16).reshape(spread, pair, wide)
        back = exchange(block, ("tok", "nout")).reshape(nt, nn, pair, wide)
        weight_in_grad = dot(x_cols, grad_half, 0, 0).astype(jnp.bfloat16)
        weight_out_grad = dot(act, dy_cols, 0, 0).astype(jnp.bfloat16)
        final = jnp.sum(back.astype(jnp.float32), axis=1).transpose(1, 0, 2).reshape(pair, cols)
        output_rows = (final[:rows] + bias_out).astype(jnp.bfloat16)
        grad_tokens = final[rows:].astype(jnp.bfloat16)
        return (output_rows, grad_tokens, weight_in_grad, weight_out_grad, bias_in_grad, bias_out_grad)

    return on_device


def solution(mesh):
    nt, nk, nn = mesh.shape["tok"], mesh.shape["kin"], mesh.shape["nout"]
    return jax.shard_map(
        make_small(nn) if (nt, nk) == (2, 2) and nn in (2, 4) else make_plain(nt, nk, nn),
        mesh=mesh,
        in_specs=(
            P(("groups", "tok", "nout"), "kin"),
            P(("kin", "tok"), "nout"),
            P("nout"),
            P("nout", ("kin", "tok")),
            P("kin"),
            P(("groups", "tok", "nout"), "kin"),
        ),
        out_specs=(
            P(("groups", "tok", "nout"), "kin"),
            P(("groups", "tok", "nout"), "kin"),
            P(("groups", "kin", "tok"), "nout"),
            P(("groups", "nout"), ("kin", "tok")),
            P(("groups", "nout")),
            P(("groups", "kin")),
        ),
        check_vma=False,
    )
```

```python
import functools

import jax
import jax.numpy as jnp
from jax import lax
from jax.experimental import pallas as pl
from jax.experimental.pallas import tpu as pltpu
from jax.sharding import PartitionSpec as P

inv_root_two = 0.7071067811865476
inv_root_two_pi = 0.3989422804014327

MIB = 1 << 20
bf16, f32 = jnp.bfloat16, jnp.float32
like = jax.ShapeDtypeStruct
whole = pl.BlockSpec(memory_space=pltpu.VMEM)
hbm = pl.BlockSpec(memory_space=pltpu.HBM)
swap = [(0, 1), (1, 0)]


def gelu_parts(hidden):
    normal_cdf = 0.5 * (1.0 + lax.erf(hidden * inv_root_two))
    density = jnp.exp(-0.5 * hidden * hidden) * inv_root_two_pi
    return (hidden * normal_cdf, normal_cdf + hidden * density)


def dot(left, right, left_dim, right_dim):
    return lax.dot_general(
        left, right, (((left_dim,), (right_dim,)), ((), ())), preferred_element_type=jnp.float32
    )


def exchange(chunks, axes):
    return lax.all_to_all(chunks, axes, split_axis=0, concat_axis=0, tiled=True)


def dot_turned(rows, weight):
    return dot(weight, rows, 1, 1).T


def tile_of(size, most):
    return max(t for t in range(128, most + 1, 128) if size % t == 0)


def tiles_of(size, most=512):
    tile = tile_of(size, most)
    return [pl.ds(i * tile, tile) for i in range(size // tile)]


def call(body, name, outs, grant=4 * MIB, flops=0, moved=0, scratch=(), resident=True, specs=None):
    shapes = [pltpu.VMEM(o.shape, o.dtype) if resident else o for o in outs]

    def run(*args):
        cost = pl.CostEstimate(flops=flops, bytes_accessed=moved, transcendentals=0)
        return pl.pallas_call(
            body,
            out_shape=shapes,
            in_specs=specs or [whole] * len(args),
            out_specs=[whole] * len(outs),
            scratch_shapes=list(scratch),
            cost_estimate=cost,
            compiler_params=pltpu.CompilerParams(vmem_limit_bytes=grant),
            name=name,
        )(*args)

    return run


def kept(array):
    return pltpu.with_memory_space_constraint(array, pltpu.VMEM)


def in_hbm(array):
    return pltpu.with_memory_space_constraint(array, pltpu.HBM)


def apart(mixed, rows):
    total, wide = mixed.shape
    tiles = mixed.reshape(total // (4 * rows), 2, 2 * rows, wide)
    even, odd = tiles[:, 0], tiles[:, 1]
    is_low = lax.broadcasted_iota(jnp.int32, even.shape, 1) < rows
    first = jnp.where(is_low, even, pltpu.roll(odd, rows, 1))
    second = jnp.where(is_low, pltpu.roll(even, rows, 1), odd)
    return first.reshape(total // 2, wide), second.reshape(total // 2, wide)


def together(first, second, rows):
    total, wide = first.shape
    first = first.reshape(total // (2 * rows), 2 * rows, wide)
    second = second.reshape(total // (2 * rows), 2 * rows, wide)
    is_low = lax.broadcasted_iota(jnp.int32, first.shape, 1) < rows
    even = jnp.where(is_low, first, pltpu.roll(second, rows, 1))
    odd = jnp.where(is_low, pltpu.roll(first, rows, 1), second)
    return jnp.stack([even, odd], axis=1).reshape(2 * total, wide)


def ordered(me, own, far, axis=0):
    low, high = jnp.where(me == 0, own, far), jnp.where(me == 0, far, own)
    return jnp.concatenate([low, high], axis=axis)


def half_of(size, mine):
    core = lax.axis_index("kin")
    at = core if mine else 1 - core
    return pl.ds(pl.multiple_of(at * size, size), size)


def quarters(source, target, sems):
    size = target.shape[0] // 4
    return [
        pltpu.make_async_copy(source.at[part, :], target.at[part, :], sems.at[i])
        for i, part in enumerate(pl.ds(j * size, size) for j in range(4))
    ]


def load_far_body(hbm_ref, after_ref, out_ref, sems):
    copies = quarters(hbm_ref.at[half_of(out_ref.shape[0], False), :], out_ref, sems)
    for copy in copies:
        copy.start()
    for copy in copies:
        copy.wait()


def load_body(in_hbm_ref, out_hbm_ref, after_ref, far_ref, own_ref, out_ref, sems):
    half = own_ref.shape[1]
    copies = quarters(in_hbm_ref.at[:, half_of(half, False)], far_ref, sems.at[0])
    copies += quarters(in_hbm_ref.at[:, half_of(half, True)], own_ref, sems.at[1])
    copies += quarters(out_hbm_ref.at[half_of(half, True), :], out_ref, sems.at[2])
    for copy in copies:
        copy.start()
    for copy in copies:
        copy.wait()


def pair_body(own_ref, got_ref, after_ref, out_ref):
    out_ref[...] = ordered(lax.axis_index("tok"), own_ref[...], got_ref[...])


def far_pre_body(rows, count, *refs):
    *piece_refs, w_in_ref = refs[: count + 1]
    sent_ref, x_ref, dy_ref, sums_ref = refs[count + 1 :]
    mixed = jnp.concatenate([ref[...] for ref in piece_refs], axis=0)
    x_cols, dy_cols = apart(mixed.astype(f32), rows)
    sums_ref[...] = jnp.sum(dy_cols, axis=0, keepdims=True)
    x_cols, dy_cols = x_cols.astype(bf16), dy_cols.astype(bf16)
    x_ref[...], dy_ref[...] = x_cols, dy_cols
    for at in tiles_of(sent_ref.shape[1]):
        sent_ref[:, at] = dot(x_cols, w_in_ref[:, at], 1, 0).astype(bf16)


def own_pre_body(x_ref, w_in_ref, after_ref, own_ref):
    x_cols = x_ref[...]
    for at in tiles_of(own_ref.shape[1]):
        own_ref[:, at] = dot(x_cols, w_in_ref[:, at], 1, 0)


def far_grad_body(dy_ref, w_out_ref, after_ref, *sent_refs):
    dy_cols = dy_ref[...]
    size = sent_refs[0].shape[0]
    for at in tiles_of(sent_refs[0].shape[1]):
        terms = dot_turned(dy_cols, w_out_ref[at, :]).astype(bf16)
        for i, sent_ref in enumerate(sent_refs):
            sent_ref[:, at] = terms[i * size : (i + 1) * size]


def own_grad_body(dy_ref, w_out_ref, own_ref):
    dy_cols = dy_ref[...]
    for at in tiles_of(own_ref.shape[1]):
        own_ref[:, at] = dot_turned(dy_cols, w_out_ref[at, :])


def add_body(own_ref, *refs):
    *got_refs, out_ref = refs
    got = jnp.concatenate([ref[...] for ref in got_refs], axis=0)
    out_ref[...] = (own_ref[...] + got.astype(f32)).astype(bf16)


def gelu_body(bias_ref, own_ref, other_ref, after_ref, slopes_ref, *act_refs):
    size, half = act_refs[0].shape
    bias = bias_ref[:, half_of(half, True)]
    tile = tile_of(half, 512)
    for i in range(half // tile):
        at = pl.ds(i * tile, tile)
        pre_act = own_ref[:, at].astype(f32) + other_ref[:, at].astype(f32)
        activated, slopes = gelu_parts(pre_act + bias[:, i * tile : (i + 1) * tile])
        slopes_ref[:, at] = slopes
        activated = activated.astype(bf16)
        for j, act_ref in enumerate(act_refs):
            act_ref[:, at] = activated[j * size : (j + 1) * size]


def grad_pre_body(slopes_ref, own_ref, other_ref, after_ref, grad_ref):
    grad_act = own_ref[...].astype(f32) + other_ref[...].astype(f32)
    grad_ref[...] = (grad_act * slopes_ref[...]).astype(bf16)


def own_forward_body(low_ref, high_ref, w_out_ref, out_ref):
    act = jnp.concatenate([low_ref[...], high_ref[...]], axis=0)
    for at in tiles_of(out_ref.shape[1]):
        out_ref[:, at] = dot(act, w_out_ref[:, at], 1, 0)


def far_forward_body(own_low, own_high, low_ref, high_ref, w_out_ref, terms_ref, act_ref, out_ref):
    own = jnp.concatenate([own_low[...], own_high[...]], axis=0)
    act = jnp.concatenate([low_ref[...], high_ref[...]], axis=0)
    act_ref[...] = ordered(lax.axis_index("kin"), own, act, 1)
    for at in tiles_of(out_ref.shape[1]):
        out_ref[:, at] = terms_ref[:, at] + dot(act, w_out_ref[:, at], 1, 0)


def own_backward_body(grad_ref, w_in_ref, out_ref):
    grad = grad_ref[...]
    for at in tiles_of(out_ref.shape[1]):
        out_ref[:, at] = dot_turned(grad, w_in_ref[at, :])


def blocks_body(rows, own_ref, far_ref, forward_ref, backward_ref, w_in_ref, grad_ref, *out_refs):
    grad = far_ref[...]
    grad_ref[...] = ordered(lax.axis_index("kin"), own_ref[...], grad, 1)
    size = out_refs[0].shape[0]
    for at in tiles_of(forward_ref.shape[1]):
        backward = backward_ref[:, at] + dot_turned(grad, w_in_ref[at, :])
        terms = together(forward_ref[:, at], backward, rows).astype(bf16)
        for i, out_ref in enumerate(out_refs):
            out_ref[:, at] = terms[i * size : (i + 1) * size]


def outer_body(most, left_ref, right_ref, out_hbm, block_ref, sems):
    copies = []
    for i, at in enumerate(tiles_of(out_hbm.shape[0], 256)):
        left = left_ref[:, at].T
        for part in tiles_of(out_hbm.shape[1], most):
            block_ref[at, part] = dot(left, right_ref[:, part], 1, 0).astype(bf16)
        copies.append(
            pltpu.make_async_copy(block_ref.at[at, :], out_hbm.at[at, :], sems.at[i])
        )
        copies[-1].start()
    for copy in copies:
        copy.wait()


def outer(left, right, name, most):
    count, high = left.shape
    wide = right.shape[1]
    return pl.pallas_call(
        functools.partial(outer_body, most),
        out_shape=like((high, wide), bf16),
        in_specs=[whole] * 2,
        out_specs=pl.BlockSpec(memory_space=pl.ANY),
        scratch_shapes=[
            pltpu.VMEM((high, wide), bf16),
            pltpu.SemaphoreType.DMA((len(tiles_of(high, 256)),)),
        ],
        cost_estimate=pl.CostEstimate(
            flops=2 * count * wide * high, bytes_accessed=2 * wide * high, transcendentals=0
        ),
        compiler_params=pltpu.CompilerParams(vmem_limit_bytes=16 * MIB),
        name=name,
    )(kept(left), kept(right))


def sum_body(rows, bias_ref, sums_ref, *refs):
    *term_refs, after_ref, own_ref, sent_ref = refs
    wide = own_ref.shape[1]
    me = lax.axis_index("tok")
    summed = sum(ref[...].astype(f32) for ref in term_refs)
    bias = jnp.where(me == 0, bias_ref[:, :wide], bias_ref[:, wide:])
    row = lax.broadcasted_iota(jnp.int32, summed.shape, 0)
    summed = summed + jnp.where(lax.rem(row, 2 * rows) < rows, bias, 0.0)
    low, high = summed[: 2 * rows], summed[2 * rows :]
    own_ref[...] = jnp.where(me == 0, low, high).astype(bf16)
    rest = sums_ref[...]
    row = lax.broadcasted_iota(jnp.int32, low.shape, 0)
    extra = jnp.zeros_like(low)
    for i in range(3):
        term = rest.astype(bf16).astype(f32)
        extra = jnp.where(row == i, term, extra)
        rest = rest - term
    sent = jnp.concatenate([jnp.where(me == 0, high, low), extra], axis=0)
    sent_ref[...] = sent.astype(bf16)


def final_body(rows, own_ref, got_ref, sums_ref, hidden_ref, rows_ref, grad_ref, out_sums_ref, bias_ref):
    wide = own_ref.shape[1]
    me = lax.axis_index("tok")
    own, got = own_ref[...].astype(f32), got_ref[...].astype(f32)
    own_sums, got_sums = sums_ref[...], jnp.sum(got[2 * rows :], axis=0, keepdims=True)
    for i in range(2):
        at = pl.ds(i * wide, wide)
        part = jnp.where(me == i, own, got[: 2 * rows])
        rows_ref[:, at] = part[:rows].astype(bf16)
        grad_ref[:, at] = part[rows:].astype(bf16)
        out_sums_ref[:, at] = jnp.where(me == i, own_sums, got_sums)
    bias_ref[...] = jnp.sum(hidden_ref[...].astype(f32), axis=0, keepdims=True)


def make_small(nn):
    def across(array, shift):
        return lax.ppermute(array, "nout", [(i, i ^ shift) for i in range(nn)])

    def on_device(tokens, weight_in, bias_in, weight_out, bias_out, grad_out):
        rows, cols = tokens.shape
        wide, hid = weight_in.shape
        half = hid // 2
        pair = 2 * rows
        count = 2 * nn * rows
        piece = 2 * wide * half
        sem = pltpu.SemaphoreType.DMA

        mine = jnp.concatenate([tokens, grad_out], axis=0)
        me = lax.axis_index("tok")
        own = lax.dynamic_slice_in_dim(mine, me * wide, wide, 1)
        sent = lax.dynamic_slice_in_dim(mine, (1 - me) * wide, wide, 1)
        got = lax.ppermute(sent, "tok", swap)
        (out_far,) = call(
            load_far_body,
            "load_far",
            [like((half, wide), bf16)],
            grant=MIB,
            moved=piece,
            scratch=[sem((4,))],
            specs=[hbm, pl.BlockSpec(memory_space=pl.ANY)],
        )(in_hbm(weight_out), sent)
        (tiles,) = call(pair_body, "pair_tiles", [like((2 * pair, wide), bf16)])(
            kept(own), kept(got), kept(out_far)
        )
        pieces = [across(tiles, shift) for shift in reversed(range(1, nn))] + [tiles]
        in_far, in_own, out_own = call(
            load_body,
            "load_rest",
            [like((wide, half), bf16)] * 2 + [like((half, wide), bf16)],
            grant=MIB,
            moved=3 * piece,
            scratch=[sem((3, 4))],
            specs=[hbm] * 2 + [pl.BlockSpec(memory_space=pl.ANY)],
        )(in_hbm(weight_in), in_hbm(weight_out), tiles)

        def product(body, name, outs, *args):
            return call(body, name, outs, grant=8 * MIB)(*map(kept, args))

        side, ends = like((count, half), bf16), like((count, wide), f32)
        sent, x_cols, dy_cols, sums = product(
            functools.partial(far_pre_body, rows, nn),
            "far_pre",
            [side] + [like((count, wide), bf16)] * 2 + [like((1, wide), f32)],
            *pieces,
            in_far,
        )
        got = lax.ppermute(sent, "kin", swap)
        (own,) = product(own_pre_body, "own_pre", [like((count, half), f32)], x_cols, in_own, sent)
        (own_pre,) = product(add_body, "add_pre", [side], own, got)
        other_pre = lax.ppermute(own_pre, "tok", swap)
        sides = [like((count // 2, half), bf16)] * 2
        sent = product(far_grad_body, "far_grad", sides, dy_cols, out_far, own_pre)
        got = [lax.ppermute(part, "kin", swap) for part in sent]
        (own,) = product(own_grad_body, "own_grad", [like((count, half), f32)], dy_cols, out_own)
        (own_grad,) = product(add_body, "add_grad", [side], own, *got)
        other_grad = lax.ppermute(own_grad, "tok", swap)
        slopes, *act_own = call(gelu_body, "gelu", [like((count, half), f32)] + sides)(
            bias_in.reshape(1, hid), kept(own_pre), kept(other_pre), kept(own_grad)
        )
        act_far = [lax.ppermute(part, "kin", swap) for part in act_own]
        (forward,) = product(own_forward_body, "own_forward", [ends], *act_own, out_own)
        act, forward = product(
            far_forward_body,
            "far_forward",
            [like((count, hid), bf16), ends],
            *act_own,
            *act_far,
            out_far,
            forward,
        )
        (grad_own,) = product(
            grad_pre_body, "grad_pre", [side], slopes, own_grad, other_grad, forward
        )
        grad_far = lax.ppermute(grad_own, "kin", swap)
        (backward,) = product(own_backward_body, "own_backward", [ends], grad_own, in_own)
        grad, *blocks = product(
            functools.partial(blocks_body, rows),
            "output_blocks",
            [like((count, hid), bf16)] + [like((2 * pair, wide), bf16)] * nn,
            grad_own,
            grad_far,
            forward,
            backward,
            in_far,
        )

        weight_in_grad = outer(x_cols, grad, "weight_in_grad", 256)
        weight_out_grad = outer(act, dy_cols, "weight_out_grad", 1536)

        terms = [across(blocks[i], nn - 1 - i) for i in range(nn - 1)] + [blocks[-1]]
        own, sent = call(
            functools.partial(sum_body, rows),
            "sum_blocks",
            [like((pair, wide), bf16), like((2 * pair, wide), bf16)],
            specs=[whole] * (nn + 2) + [hbm],
        )(
            bias_out.reshape(1, cols),
            kept(sums),
            *[kept(term) for term in terms],
            in_hbm(weight_in_grad),
        )
        got = lax.ppermute(sent, "tok", swap)
        output_rows, grad_tokens, bias_out_grad, bias_in_grad = call(
            functools.partial(final_body, rows),
            "final_rows",
            [like((rows, cols), bf16)] * 2 + [like((1, cols), f32), like((1, hid), f32)],
            resident=False,
        )(kept(own), kept(got), kept(sums), kept(grad))
        return (
            output_rows,
            grad_tokens,
            weight_in_grad,
            weight_out_grad,
            bias_in_grad.reshape(hid),
            bias_out_grad.reshape(cols),
        )

    return on_device


def make_plain(nt, nk, nn):
    spread, square = nt * nn, nk * nt

    def on_device(tokens, weight_in, bias_in, weight_out, bias_out, grad_out):
        rows, cols = tokens.shape
        wide, hid = weight_in.shape
        part = hid // square
        pair = 2 * rows
        total = pair * spread

        mine = jnp.concatenate([tokens, grad_out], axis=0)
        by_owner = mine.reshape(pair, nt, wide).transpose(1, 0, 2)
        chunks = jnp.broadcast_to(by_owner[:, None], (nt, nn, pair, wide))
        mixed = exchange(chunks.reshape(spread, pair, wide), ("tok", "nout")).reshape(total, wide)
        is_fwd = (lax.broadcasted_iota(jnp.int32, (total, 1), 0) % pair) < rows

        col_sums = jnp.sum(jnp.where(is_fwd, 0.0, mixed.astype(jnp.float32)), axis=0)
        bias_out_grad = lax.all_gather(col_sums, "tok", axis=0, tiled=True)

        partial = jnp.where(is_fwd, dot(mixed, weight_in, 1, 0), dot(mixed, weight_out, 1, 1))
        partial = partial.astype(jnp.bfloat16).reshape(total, square, part).transpose(1, 0, 2)
        got = exchange(partial, ("kin", "tok"))
        summed = jnp.sum(got.astype(jnp.float32), axis=0).reshape(spread, 2, rows, part)
        at = lax.axis_index(("kin", "tok"))
        pre_act = summed[:, 0] + lax.dynamic_slice_in_dim(bias_in, at * part, part)
        activated, slopes = gelu_parts(pre_act)
        grad_pre = summed[:, 1] * slopes
        both = jnp.stack([activated, grad_pre], axis=1).astype(jnp.bfloat16).reshape(total, part)
        both = exchange(jnp.broadcast_to(both[None], (square, total, part)), ("kin", "tok"))
        both = both.transpose(1, 0, 2).reshape(total, hid)

        split = both.reshape(spread, 2, rows, hid)
        act = split[:, 0].reshape(spread * rows, hid)
        grad_half = split[:, 1].reshape(spread * rows, hid)
        split = mixed.reshape(spread, 2, rows, wide)
        x_cols = split[:, 0].reshape(spread * rows, wide)
        dy_cols = split[:, 1].reshape(spread * rows, wide)
        bias_in_grad = jnp.sum(grad_half.astype(jnp.float32), axis=0)

        block = jnp.stack(
            [
                dot(act, weight_out, 1, 0).reshape(spread, rows, wide),
                dot(grad_half, weight_in, 1, 1).reshape(spread, rows, wide),
            ],
            axis=1,
        )
        block = block.astype(jnp.bfloat16).reshape(spread, pair, wide)
        back = exchange(block, ("tok", "nout")).reshape(nt, nn, pair, wide)
        weight_in_grad = dot(x_cols, grad_half, 0, 0).astype(jnp.bfloat16)
        weight_out_grad = dot(act, dy_cols, 0, 0).astype(jnp.bfloat16)
        final = jnp.sum(back.astype(jnp.float32), axis=1).transpose(1, 0, 2).reshape(pair, cols)
        output_rows = (final[:rows] + bias_out).astype(jnp.bfloat16)
        grad_tokens = final[rows:].astype(jnp.bfloat16)
        return (output_rows, grad_tokens, weight_in_grad, weight_out_grad, bias_in_grad, bias_out_grad)

    return on_device


def solution(mesh):
    nt, nk, nn = mesh.shape["tok"], mesh.shape["kin"], mesh.shape["nout"]
    return jax.shard_map(
        make_small(nn) if (nt, nk) == (2, 2) and nn in (2, 4) else make_plain(nt, nk, nn),
        mesh=mesh,
        in_specs=(
            P(("groups", "tok", "nout"), "kin"),
            P(("kin", "tok"), "nout"),
            P("nout"),
            P("nout", ("kin", "tok")),
            P("kin"),
            P(("groups", "tok", "nout"), "kin"),
        ),
        out_specs=(
            P(("groups", "tok", "nout"), "kin"),
            P(("groups", "tok", "nout"), "kin"),
            P(("groups", "kin", "tok"), "nout"),
            P(("groups", "nout"), ("kin", "tok")),
            P(("groups", "nout")),
            P(("groups", "kin")),
        ),
        check_vma=False,
    )
```

```python
import functools

import jax
import jax.numpy as jnp
from jax import lax
from jax.experimental import pallas as pl
from jax.experimental.pallas import tpu as pltpu
from jax.sharding import PartitionSpec as P

inv_root_two = 0.7071067811865476
inv_root_two_pi = 0.3989422804014327

MIB = 1 << 20
bf16, f32 = jnp.bfloat16, jnp.float32
like = jax.ShapeDtypeStruct
whole = pl.BlockSpec(memory_space=pltpu.VMEM)
hbm = pl.BlockSpec(memory_space=pltpu.HBM)
swap = [(0, 1), (1, 0)]


def gelu_parts(hidden):
    normal_cdf = 0.5 * (1.0 + lax.erf(hidden * inv_root_two))
    density = jnp.exp(-0.5 * hidden * hidden) * inv_root_two_pi
    return (hidden * normal_cdf, normal_cdf + hidden * density)


def dot(left, right, left_dim, right_dim):
    return lax.dot_general(
        left, right, (((left_dim,), (right_dim,)), ((), ())), preferred_element_type=jnp.float32
    )


def exchange(chunks, axes):
    return lax.all_to_all(chunks, axes, split_axis=0, concat_axis=0, tiled=True)


def dot_turned(rows, weight):
    return dot(weight, rows, 1, 1).T


def tile_of(size, most):
    return max(t for t in range(128, most + 1, 128) if size % t == 0)


def tiles_of(size, most=512):
    tile = tile_of(size, most)
    return [pl.ds(i * tile, tile) for i in range(size // tile)]


def call(body, name, outs, grant=4 * MIB, flops=0, moved=0, scratch=(), resident=True, specs=None):
    shapes = [pltpu.VMEM(o.shape, o.dtype) if resident else o for o in outs]

    def run(*args):
        cost = pl.CostEstimate(flops=flops, bytes_accessed=moved, transcendentals=0)
        return pl.pallas_call(
            body,
            out_shape=shapes,
            in_specs=specs or [whole] * len(args),
            out_specs=[whole] * len(outs),
            scratch_shapes=list(scratch),
            cost_estimate=cost,
            compiler_params=pltpu.CompilerParams(vmem_limit_bytes=grant),
            name=name,
        )(*args)

    return run


def kept(array):
    return pltpu.with_memory_space_constraint(array, pltpu.VMEM)


def in_hbm(array):
    return pltpu.with_memory_space_constraint(array, pltpu.HBM)


def apart(mixed, rows):
    total, wide = mixed.shape
    tiles = mixed.reshape(total // (4 * rows), 2, 2 * rows, wide)
    even, odd = tiles[:, 0], tiles[:, 1]
    is_low = lax.broadcasted_iota(jnp.int32, even.shape, 1) < rows
    first = jnp.where(is_low, even, pltpu.roll(odd, rows, 1))
    second = jnp.where(is_low, pltpu.roll(even, rows, 1), odd)
    return first.reshape(total // 2, wide), second.reshape(total // 2, wide)


def together(first, second, rows):
    total, wide = first.shape
    first = first.reshape(total // (2 * rows), 2 * rows, wide)
    second = second.reshape(total // (2 * rows), 2 * rows, wide)
    is_low = lax.broadcasted_iota(jnp.int32, first.shape, 1) < rows
    even = jnp.where(is_low, first, pltpu.roll(second, rows, 1))
    odd = jnp.where(is_low, pltpu.roll(first, rows, 1), second)
    return jnp.stack([even, odd], axis=1).reshape(2 * total, wide)


def ordered(me, own, far, axis=0):
    low, high = jnp.where(me == 0, own, far), jnp.where(me == 0, far, own)
    return jnp.concatenate([low, high], axis=axis)


def half_of(size, mine):
    core = lax.axis_index("kin")
    at = core if mine else 1 - core
    return pl.ds(pl.multiple_of(at * size, size), size)


def quarters(source, target, sems):
    size = target.shape[0] // 4
    return [
        pltpu.make_async_copy(source.at[part, :], target.at[part, :], sems.at[i])
        for i, part in enumerate(pl.ds(j * size, size) for j in range(4))
    ]


def load_far_body(hbm_ref, after_ref, out_ref, sems):
    copies = quarters(hbm_ref.at[half_of(out_ref.shape[0], False), :], out_ref, sems)
    for copy in copies:
        copy.start()
    for copy in copies:
        copy.wait()


def load_body(in_hbm_ref, out_hbm_ref, after_ref, far_ref, own_ref, out_ref, sems):
    half = own_ref.shape[1]
    copies = quarters(in_hbm_ref.at[:, half_of(half, False)], far_ref, sems.at[0])
    copies += quarters(in_hbm_ref.at[:, half_of(half, True)], own_ref, sems.at[1])
    copies += quarters(out_hbm_ref.at[half_of(half, True), :], out_ref, sems.at[2])
    for copy in copies:
        copy.start()
    for copy in copies:
        copy.wait()


def pair_body(own_ref, got_ref, after_ref, *out_refs):
    tiles = ordered(lax.axis_index("tok"), own_ref[...], got_ref[...])
    count, wide = tiles.shape
    for out_ref in out_refs:
        out_ref[:, :wide] = tiles
        if out_ref.shape[1] > wide:
            out_ref[:, wide:] = jnp.zeros((count, out_ref.shape[1] - wide), bf16)


def far_pre_body(rows, count, *refs):
    *piece_refs, w_in_ref = refs[: count + 1]
    sent_ref, x_ref, dy_ref, sums_ref = refs[count + 1 :]
    wide = x_ref.shape[1]
    mixed = jnp.concatenate([ref[:, :wide] for ref in piece_refs], axis=0)
    x_cols, dy_cols = apart(mixed.astype(f32), rows)
    sums_ref[...] = jnp.sum(dy_cols, axis=0, keepdims=True)
    x_cols, dy_cols = x_cols.astype(bf16), dy_cols.astype(bf16)
    x_ref[...], dy_ref[...] = x_cols, dy_cols
    for at in tiles_of(sent_ref.shape[1]):
        sent_ref[:, at] = dot(x_cols, w_in_ref[:, at], 1, 0).astype(bf16)


def own_pre_body(x_ref, w_in_ref, after_ref, own_ref):
    x_cols = x_ref[...]
    for at in tiles_of(own_ref.shape[1]):
        own_ref[:, at] = dot(x_cols, w_in_ref[:, at], 1, 0)


def far_grad_body(dy_ref, w_out_ref, after_ref, *sent_refs):
    dy_cols = dy_ref[...]
    size = sent_refs[0].shape[0]
    for at in tiles_of(sent_refs[0].shape[1]):
        terms = dot_turned(dy_cols, w_out_ref[at, :]).astype(bf16)
        for i, sent_ref in enumerate(sent_refs):
            sent_ref[:, at] = terms[i * size : (i + 1) * size]


def own_grad_body(dy_ref, w_out_ref, own_ref):
    dy_cols = dy_ref[...]
    for at in tiles_of(own_ref.shape[1]):
        own_ref[:, at] = dot_turned(dy_cols, w_out_ref[at, :])


def add_body(own_ref, got_ref, out_ref):
    half = own_ref.shape[1]
    out_ref[:, :half] = (own_ref[...] + got_ref[...].astype(f32)).astype(bf16)
    out_ref[:, half:] = jnp.zeros((own_ref.shape[0], out_ref.shape[1] - half), bf16)


def gelu_body(bias_ref, own_ref, other_ref, after_ref, slopes_ref, *act_refs):
    size, half = act_refs[0].shape
    bias = bias_ref[:, half_of(half, True)]
    tile = tile_of(half, 512)
    for i in range(half // tile):
        at = pl.ds(i * tile, tile)
        pre_act = own_ref[:, at].astype(f32) + other_ref[:, at].astype(f32)
        activated, slopes = gelu_parts(pre_act + bias[:, i * tile : (i + 1) * tile])
        slopes_ref[:, at] = slopes
        activated = activated.astype(bf16)
        for j, act_ref in enumerate(act_refs):
            act_ref[:, at] = activated[j * size : (j + 1) * size]


def grad_pre_body(slopes_ref, own_ref, other_ref, after_ref, grad_ref):
    half = pl.ds(0, grad_ref.shape[1])
    grad_act = own_ref[:, half].astype(f32) + other_ref[:, half].astype(f32)
    grad_ref[...] = (grad_act * slopes_ref[...]).astype(bf16)


def own_forward_body(act_ref, w_out_ref, out_ref):
    act = act_ref[...]
    for at in tiles_of(out_ref.shape[1]):
        out_ref[:, at] = dot(act, w_out_ref[:, at], 1, 0)


def far_forward_body(own_ref, far_ref, w_out_ref, terms_ref, act_ref, out_ref):
    act = far_ref[...]
    act_ref[...] = ordered(lax.axis_index("kin"), own_ref[...], act, 1)
    for at in tiles_of(out_ref.shape[1]):
        out_ref[:, at] = terms_ref[:, at] + dot(act, w_out_ref[:, at], 1, 0)


def own_backward_body(grad_ref, w_in_ref, out_ref):
    grad = grad_ref[...]
    for at in tiles_of(out_ref.shape[1]):
        out_ref[:, at] = dot_turned(grad, w_in_ref[at, :])


def blocks_body(rows, own_ref, far_ref, forward_ref, backward_ref, w_in_ref, grad_ref, *out_refs):
    grad = far_ref[...]
    grad_ref[...] = ordered(lax.axis_index("kin"), own_ref[...], grad, 1)
    size = out_refs[0].shape[0]
    for at in tiles_of(forward_ref.shape[1]):
        backward = backward_ref[:, at] + dot_turned(grad, w_in_ref[at, :])
        terms = together(forward_ref[:, at], backward, rows).astype(bf16)
        for i, out_ref in enumerate(out_refs):
            out_ref[:, at] = terms[i * size : (i + 1) * size]


def outer_body(most, left_ref, right_ref, out_hbm, block_ref, sems):
    copies = []
    for i, at in enumerate(tiles_of(out_hbm.shape[0], 256)):
        left = left_ref[:, at].T
        for part in tiles_of(out_hbm.shape[1], most):
            block_ref[at, part] = dot(left, right_ref[:, part], 1, 0).astype(bf16)
        copies.append(
            pltpu.make_async_copy(block_ref.at[at, :], out_hbm.at[at, :], sems.at[i])
        )
        copies[-1].start()
    for copy in copies:
        copy.wait()


def outer(left, right, name, most):
    count, high = left.shape
    wide = right.shape[1]
    return pl.pallas_call(
        functools.partial(outer_body, most),
        out_shape=like((high, wide), bf16),
        in_specs=[whole] * 2,
        out_specs=pl.BlockSpec(memory_space=pl.ANY),
        scratch_shapes=[
            pltpu.VMEM((high, wide), bf16),
            pltpu.SemaphoreType.DMA((len(tiles_of(high, 256)),)),
        ],
        cost_estimate=pl.CostEstimate(
            flops=2 * count * wide * high, bytes_accessed=2 * wide * high, transcendentals=0
        ),
        compiler_params=pltpu.CompilerParams(vmem_limit_bytes=16 * MIB),
        name=name,
    )(kept(left), kept(right))


def sum_body(rows, bias_ref, sums_ref, *refs):
    *term_refs, after_ref, own_ref, sent_ref = refs
    wide = own_ref.shape[1]
    me = lax.axis_index("tok")
    summed = sum(ref[...].astype(f32) for ref in term_refs)
    bias = jnp.where(me == 0, bias_ref[:, :wide], bias_ref[:, wide:])
    row = lax.broadcasted_iota(jnp.int32, summed.shape, 0)
    summed = summed + jnp.where(lax.rem(row, 2 * rows) < rows, bias, 0.0)
    low, high = summed[: 2 * rows], summed[2 * rows :]
    own_ref[...] = jnp.where(me == 0, low, high).astype(bf16)
    rest = sums_ref[...]
    row = lax.broadcasted_iota(jnp.int32, low.shape, 0)
    extra = jnp.zeros_like(low)
    for i in range(3):
        term = rest.astype(bf16).astype(f32)
        extra = jnp.where(row == i, term, extra)
        rest = rest - term
    sent = jnp.concatenate([jnp.where(me == 0, high, low), extra], axis=0)
    sent_ref[...] = sent.astype(bf16)


def final_body(rows, own_ref, got_ref, sums_ref, hidden_ref, rows_ref, grad_ref, out_sums_ref, bias_ref):
    wide = own_ref.shape[1]
    me = lax.axis_index("tok")
    own, got = own_ref[...].astype(f32), got_ref[...].astype(f32)
    own_sums, got_sums = sums_ref[...], jnp.sum(got[2 * rows :], axis=0, keepdims=True)
    for i in range(2):
        at = pl.ds(i * wide, wide)
        part = jnp.where(me == i, own, got[: 2 * rows])
        rows_ref[:, at] = part[:rows].astype(bf16)
        grad_ref[:, at] = part[rows:].astype(bf16)
        out_sums_ref[:, at] = jnp.where(me == i, own_sums, got_sums)
    bias_ref[...] = jnp.sum(hidden_ref[...].astype(f32), axis=0, keepdims=True)


def make_small(nn):
    def across(array, shift):
        return lax.ppermute(array, "nout", [(i, i ^ shift) for i in range(nn)])

    def on_device(tokens, weight_in, bias_in, weight_out, bias_out, grad_out):
        rows, cols = tokens.shape
        wide, hid = weight_in.shape
        half = hid // 2
        pair = 2 * rows
        count = 2 * nn * rows
        piece = 2 * wide * half
        sem = pltpu.SemaphoreType.DMA

        mine = jnp.concatenate([tokens, grad_out], axis=0)
        me = lax.axis_index("tok")
        own = lax.dynamic_slice_in_dim(mine, me * wide, wide, 1)
        sent = lax.dynamic_slice_in_dim(mine, (1 - me) * wide, wide, 1)
        got = lax.ppermute(sent, "tok", swap)
        (out_far,) = call(
            load_far_body,
            "load_far",
            [like((half, wide), bf16)],
            grant=MIB,
            moved=piece,
            scratch=[sem((4,))],
            specs=[hbm, pl.BlockSpec(memory_space=pl.ANY)],
        )(in_hbm(weight_out), sent)
        tiles, farthest = call(
            pair_body, "pair_tiles", [like((2 * pair, wide + more), bf16) for more in (0, 128)]
        )(
            kept(own), kept(got), kept(out_far)
        )
        pieces = [across(tiles, shift) for shift in range(1, nn - 1)]
        pieces = [across(farthest, nn - 1)] + pieces[::-1] + [tiles]
        in_far, in_own, out_own = call(
            load_body,
            "load_rest",
            [like((wide, half), bf16)] * 2 + [like((half, wide), bf16)],
            grant=MIB,
            moved=3 * piece,
            scratch=[sem((3, 4))],
            specs=[hbm] * 2 + [pl.BlockSpec(memory_space=pl.ANY)],
        )(in_hbm(weight_in), in_hbm(weight_out), tiles)

        def product(body, name, outs, *args):
            return call(body, name, outs, grant=8 * MIB)(*map(kept, args))

        crossing = like((count, half + 128), bf16)
        side, ends = like((count, half), bf16), like((count, wide), f32)
        sent, x_cols, dy_cols, sums = product(
            functools.partial(far_pre_body, rows, nn),
            "far_pre",
            [side] + [like((count, wide), bf16)] * 2 + [like((1, wide), f32)],
            *pieces,
            in_far,
        )
        got = lax.ppermute(sent, "kin", swap)
        (own,) = product(own_pre_body, "own_pre", [like((count, half), f32)], x_cols, in_own, sent)
        (own_pre,) = product(add_body, "add_pre", [crossing], own, got)
        other_pre = lax.ppermute(own_pre, "tok", swap)
        sides = [side]
        sent = product(far_grad_body, "far_grad", sides, dy_cols, out_far, own_pre)
        got = [lax.ppermute(part, "kin", swap) for part in sent]
        (own,) = product(own_grad_body, "own_grad", [like((count, half), f32)], dy_cols, out_own)
        (own_grad,) = product(add_body, "add_grad", [crossing], own, *got)
        other_grad = lax.ppermute(own_grad, "tok", swap)
        slopes, *act_own = call(gelu_body, "gelu", [like((count, half), f32)] + sides)(
            bias_in.reshape(1, hid), kept(own_pre), kept(other_pre), kept(own_grad)
        )
        act_far = [lax.ppermute(part, "kin", swap) for part in act_own]
        (forward,) = product(own_forward_body, "own_forward", [ends], *act_own, out_own)
        act, forward = product(
            far_forward_body,
            "far_forward",
            [like((count, hid), bf16), ends],
            *act_own,
            *act_far,
            out_far,
            forward,
        )
        (grad_own,) = product(
            grad_pre_body, "grad_pre", [side], slopes, own_grad, other_grad, forward
        )
        grad_far = lax.ppermute(grad_own, "kin", swap)
        (backward,) = product(own_backward_body, "own_backward", [ends], grad_own, in_own)
        grad, *blocks = product(
            functools.partial(blocks_body, rows),
            "output_blocks",
            [like((count, hid), bf16)] + [like((2 * pair, wide), bf16)] * nn,
            grad_own,
            grad_far,
            forward,
            backward,
            in_far,
        )

        weight_in_grad = outer(x_cols, grad, "weight_in_grad", 256)
        weight_out_grad = outer(act, dy_cols, "weight_out_grad", 1536)

        terms = [across(blocks[i], nn - 1 - i) for i in range(nn - 1)] + [blocks[-1]]
        own, sent = call(
            functools.partial(sum_body, rows),
            "sum_blocks",
            [like((pair, wide), bf16), like((2 * pair, wide), bf16)],
            specs=[whole] * (nn + 2) + [hbm],
        )(
            bias_out.reshape(1, cols),
            kept(sums),
            *[kept(term) for term in terms],
            in_hbm(weight_in_grad),
        )
        got = lax.ppermute(sent, "tok", swap)
        output_rows, grad_tokens, bias_out_grad, bias_in_grad = call(
            functools.partial(final_body, rows),
            "final_rows",
            [like((rows, cols), bf16)] * 2 + [like((1, cols), f32), like((1, hid), f32)],
            resident=False,
        )(kept(own), kept(got), kept(sums), kept(grad))
        return (
            output_rows,
            grad_tokens,
            weight_in_grad,
            weight_out_grad,
            bias_in_grad.reshape(hid),
            bias_out_grad.reshape(cols),
        )

    return on_device


def make_plain(nt, nk, nn):
    spread, square = nt * nn, nk * nt

    def on_device(tokens, weight_in, bias_in, weight_out, bias_out, grad_out):
        rows, cols = tokens.shape
        wide, hid = weight_in.shape
        part = hid // square
        pair = 2 * rows
        total = pair * spread

        mine = jnp.concatenate([tokens, grad_out], axis=0)
        by_owner = mine.reshape(pair, nt, wide).transpose(1, 0, 2)
        chunks = jnp.broadcast_to(by_owner[:, None], (nt, nn, pair, wide))
        mixed = exchange(chunks.reshape(spread, pair, wide), ("tok", "nout")).reshape(total, wide)
        is_fwd = (lax.broadcasted_iota(jnp.int32, (total, 1), 0) % pair) < rows

        col_sums = jnp.sum(jnp.where(is_fwd, 0.0, mixed.astype(jnp.float32)), axis=0)
        bias_out_grad = lax.all_gather(col_sums, "tok", axis=0, tiled=True)

        partial = jnp.where(is_fwd, dot(mixed, weight_in, 1, 0), dot(mixed, weight_out, 1, 1))
        partial = partial.astype(jnp.bfloat16).reshape(total, square, part).transpose(1, 0, 2)
        got = exchange(partial, ("kin", "tok"))
        summed = jnp.sum(got.astype(jnp.float32), axis=0).reshape(spread, 2, rows, part)
        at = lax.axis_index(("kin", "tok"))
        pre_act = summed[:, 0] + lax.dynamic_slice_in_dim(bias_in, at * part, part)
        activated, slopes = gelu_parts(pre_act)
        grad_pre = summed[:, 1] * slopes
        both = jnp.stack([activated, grad_pre], axis=1).astype(jnp.bfloat16).reshape(total, part)
        both = exchange(jnp.broadcast_to(both[None], (square, total, part)), ("kin", "tok"))
        both = both.transpose(1, 0, 2).reshape(total, hid)

        split = both.reshape(spread, 2, rows, hid)
        act = split[:, 0].reshape(spread * rows, hid)
        grad_half = split[:, 1].reshape(spread * rows, hid)
        split = mixed.reshape(spread, 2, rows, wide)
        x_cols = split[:, 0].reshape(spread * rows, wide)
        dy_cols = split[:, 1].reshape(spread * rows, wide)
        bias_in_grad = jnp.sum(grad_half.astype(jnp.float32), axis=0)

        block = jnp.stack(
            [
                dot(act, weight_out, 1, 0).reshape(spread, rows, wide),
                dot(grad_half, weight_in, 1, 1).reshape(spread, rows, wide),
            ],
            axis=1,
        )
        block = block.astype(jnp.bfloat16).reshape(spread, pair, wide)
        back = exchange(block, ("tok", "nout")).reshape(nt, nn, pair, wide)
        weight_in_grad = dot(x_cols, grad_half, 0, 0).astype(jnp.bfloat16)
        weight_out_grad = dot(act, dy_cols, 0, 0).astype(jnp.bfloat16)
        final = jnp.sum(back.astype(jnp.float32), axis=1).transpose(1, 0, 2).reshape(pair, cols)
        output_rows = (final[:rows] + bias_out).astype(jnp.bfloat16)
        grad_tokens = final[rows:].astype(jnp.bfloat16)
        return (output_rows, grad_tokens, weight_in_grad, weight_out_grad, bias_in_grad, bias_out_grad)

    return on_device


def solution(mesh):
    nt, nk, nn = mesh.shape["tok"], mesh.shape["kin"], mesh.shape["nout"]
    return jax.shard_map(
        make_small(nn) if (nt, nk) == (2, 2) and nn in (2, 4) else make_plain(nt, nk, nn),
        mesh=mesh,
        in_specs=(
            P(("groups", "tok", "nout"), "kin"),
            P(("kin", "tok"), "nout"),
            P("nout"),
            P("nout", ("kin", "tok")),
            P("kin"),
            P(("groups", "tok", "nout"), "kin"),
        ),
        out_specs=(
            P(("groups", "tok", "nout"), "kin"),
            P(("groups", "tok", "nout"), "kin"),
            P(("groups", "kin", "tok"), "nout"),
            P(("groups", "nout"), ("kin", "tok")),
            P(("groups", "nout")),
            P(("groups", "kin")),
        ),
        check_vma=False,
    )
```

```python
import functools

import jax
import jax.numpy as jnp
from jax import lax
from jax.experimental import pallas as pl
from jax.experimental.pallas import tpu as pltpu
from jax.sharding import PartitionSpec as P

inv_root_two = 0.7071067811865476
inv_root_two_pi = 0.3989422804014327

MIB = 1 << 20
bf16, f32 = jnp.bfloat16, jnp.float32
like = jax.ShapeDtypeStruct
whole = pl.BlockSpec(memory_space=pltpu.VMEM)
hbm = pl.BlockSpec(memory_space=pltpu.HBM)
swap = [(0, 1), (1, 0)]


def gelu_parts(hidden):
    normal_cdf = 0.5 * (1.0 + lax.erf(hidden * inv_root_two))
    density = jnp.exp(-0.5 * hidden * hidden) * inv_root_two_pi
    return (hidden * normal_cdf, normal_cdf + hidden * density)


def dot(left, right, left_dim, right_dim):
    return lax.dot_general(
        left, right, (((left_dim,), (right_dim,)), ((), ())), preferred_element_type=jnp.float32
    )


def exchange(chunks, axes):
    return lax.all_to_all(chunks, axes, split_axis=0, concat_axis=0, tiled=True)


def dot_turned(rows, weight):
    return dot(weight, rows, 1, 1).T


def tile_of(size, most):
    return max(t for t in range(128, most + 1, 128) if size % t == 0)


def tiles_of(size, most=512):
    tile = tile_of(size, most)
    return [pl.ds(i * tile, tile) for i in range(size // tile)]


def call(body, name, outs, grant=4 * MIB, flops=0, moved=0, scratch=(), resident=True, specs=None):
    shapes = [pltpu.VMEM(o.shape, o.dtype) if resident else o for o in outs]

    def run(*args):
        cost = pl.CostEstimate(flops=flops, bytes_accessed=moved, transcendentals=0)
        return pl.pallas_call(
            body,
            out_shape=shapes,
            in_specs=specs or [whole] * len(args),
            out_specs=[whole] * len(outs),
            scratch_shapes=list(scratch),
            cost_estimate=cost,
            compiler_params=pltpu.CompilerParams(vmem_limit_bytes=grant),
            name=name,
        )(*args)

    return run


def kept(array):
    return pltpu.with_memory_space_constraint(array, pltpu.VMEM)


def in_hbm(array):
    return pltpu.with_memory_space_constraint(array, pltpu.HBM)


def apart(mixed, rows):
    total, wide = mixed.shape
    tiles = mixed.reshape(total // (4 * rows), 2, 2 * rows, wide)
    even, odd = tiles[:, 0], tiles[:, 1]
    is_low = lax.broadcasted_iota(jnp.int32, even.shape, 1) < rows
    first = jnp.where(is_low, even, pltpu.roll(odd, rows, 1))
    second = jnp.where(is_low, pltpu.roll(even, rows, 1), odd)
    return first.reshape(total // 2, wide), second.reshape(total // 2, wide)


def together(first, second, rows):
    total, wide = first.shape
    first = first.reshape(total // (2 * rows), 2 * rows, wide)
    second = second.reshape(total // (2 * rows), 2 * rows, wide)
    is_low = lax.broadcasted_iota(jnp.int32, first.shape, 1) < rows
    even = jnp.where(is_low, first, pltpu.roll(second, rows, 1))
    odd = jnp.where(is_low, pltpu.roll(first, rows, 1), second)
    return jnp.stack([even, odd], axis=1).reshape(2 * total, wide)


def ordered(me, own, far, axis=0):
    low, high = jnp.where(me == 0, own, far), jnp.where(me == 0, far, own)
    return jnp.concatenate([low, high], axis=axis)


def half_of(size, mine):
    core = lax.axis_index("kin")
    at = core if mine else 1 - core
    return pl.ds(pl.multiple_of(at * size, size), size)


def half_tiles(half, mine):
    core = lax.axis_index("kin")
    first = (core if mine else 1 - core) * half
    tile = tile_of(half, 512)
    return [
        (pl.ds(i * tile, tile), pl.ds(pl.multiple_of(first + i * tile, tile), tile))
        for i in range(half // tile)
    ]


def load_body(mine, hbm_ref, after_ref, out_ref, sems):
    size = out_ref.shape[0] // 4
    source = hbm_ref.at[:, half_of(out_ref.shape[1], mine)]
    copies = [
        pltpu.make_async_copy(source.at[part, :], out_ref.at[part, :], sems.at[i])
        for i, part in enumerate(pl.ds(j * size, size) for j in range(4))
    ]
    for copy in copies:
        copy.start()
    for copy in copies:
        copy.wait()


def pair_body(own_ref, got_ref, after_ref, *out_refs):
    tiles = ordered(lax.axis_index("tok"), own_ref[...], got_ref[...])
    count, wide = tiles.shape
    for out_ref in out_refs:
        out_ref[:, :wide] = tiles
        if out_ref.shape[1] > wide:
            out_ref[:, wide:] = jnp.zeros((count, out_ref.shape[1] - wide), bf16)


def far_pre_body(rows, count, *refs):
    *piece_refs, w_in_ref, after_ref = refs[: count + 2]
    sent_ref, x_ref, dy_ref, sums_ref = refs[count + 2 :]
    wide = x_ref.shape[1]
    mixed = jnp.concatenate([ref[:, :wide] for ref in piece_refs], axis=0)
    x_cols, dy_cols = apart(mixed.astype(f32), rows)
    sums_ref[...] = jnp.sum(dy_cols, axis=0, keepdims=True)
    x_cols, dy_cols = x_cols.astype(bf16), dy_cols.astype(bf16)
    x_ref[...], dy_ref[...] = x_cols, dy_cols
    for at in tiles_of(sent_ref.shape[1]):
        sent_ref[:, at] = dot(x_cols, w_in_ref[:, at], 1, 0).astype(bf16)


def own_pre_body(x_ref, w_in_ref, after_ref, own_ref):
    x_cols = x_ref[...]
    for at in tiles_of(own_ref.shape[1]):
        own_ref[:, at] = dot(x_cols, w_in_ref[:, at], 1, 0)


def far_grad_body(dy_ref, w_out_ref, after_ref, *sent_refs):
    dy_cols = dy_ref[...]
    size = sent_refs[0].shape[0]
    for at, there in half_tiles(sent_refs[0].shape[1], False):
        terms = dot_turned(dy_cols, w_out_ref[there, :]).astype(bf16)
        for i, sent_ref in enumerate(sent_refs):
            sent_ref[:, at] = terms[i * size : (i + 1) * size]


def own_grad_body(dy_ref, w_out_ref, own_ref):
    dy_cols = dy_ref[...]
    for at, there in half_tiles(own_ref.shape[1], True):
        own_ref[:, at] = dot_turned(dy_cols, w_out_ref[there, :])


def add_body(own_ref, got_ref, out_ref):
    half = own_ref.shape[1]
    out_ref[:, :half] = (own_ref[...] + got_ref[...].astype(f32)).astype(bf16)
    out_ref[:, half:] = jnp.zeros((own_ref.shape[0], out_ref.shape[1] - half), bf16)


def gelu_body(bias_ref, own_ref, other_ref, after_ref, slopes_ref, *act_refs):
    size, half = act_refs[0].shape
    bias = bias_ref[:, half_of(half, True)]
    tile = tile_of(half, 512)
    for i in range(half // tile):
        at = pl.ds(i * tile, tile)
        pre_act = own_ref[:, at].astype(f32) + other_ref[:, at].astype(f32)
        activated, slopes = gelu_parts(pre_act + bias[:, i * tile : (i + 1) * tile])
        slopes_ref[:, at] = slopes
        activated = activated.astype(bf16)
        for j, act_ref in enumerate(act_refs):
            act_ref[:, at] = activated[j * size : (j + 1) * size]


def grad_pre_body(slopes_ref, own_ref, other_ref, after_ref, grad_ref):
    half = pl.ds(0, grad_ref.shape[1])
    grad_act = own_ref[:, half].astype(f32) + other_ref[:, half].astype(f32)
    grad_ref[...] = (grad_act * slopes_ref[...]).astype(bf16)


def own_forward_body(act_ref, w_out_ref, out_ref):
    act = act_ref[...]
    part = half_of(act.shape[1], True)
    for at in tiles_of(out_ref.shape[1]):
        out_ref[:, at] = dot(act, w_out_ref[part, at], 1, 0)


def far_forward_body(own_ref, far_ref, w_out_ref, terms_ref, act_ref, out_ref):
    act = far_ref[...]
    act_ref[...] = ordered(lax.axis_index("kin"), own_ref[...], act, 1)
    part = half_of(act.shape[1], False)
    for at in tiles_of(out_ref.shape[1]):
        out_ref[:, at] = terms_ref[:, at] + dot(act, w_out_ref[part, at], 1, 0)


def own_backward_body(grad_ref, w_in_ref, out_ref):
    grad = grad_ref[...]
    for at in tiles_of(out_ref.shape[1]):
        out_ref[:, at] = dot_turned(grad, w_in_ref[at, :])


def blocks_body(rows, own_ref, far_ref, forward_ref, backward_ref, w_in_ref, grad_ref, *out_refs):
    grad = far_ref[...]
    grad_ref[...] = ordered(lax.axis_index("kin"), own_ref[...], grad, 1)
    size = out_refs[0].shape[0]
    for at in tiles_of(forward_ref.shape[1]):
        backward = backward_ref[:, at] + dot_turned(grad, w_in_ref[at, :])
        terms = together(forward_ref[:, at], backward, rows).astype(bf16)
        for i, out_ref in enumerate(out_refs):
            out_ref[:, at] = terms[i * size : (i + 1) * size]


def outer_body(most, left_ref, right_ref, out_hbm, block_ref, sems):
    copies = []
    for i, at in enumerate(tiles_of(out_hbm.shape[0], 256)):
        left = left_ref[:, at].T
        for part in tiles_of(out_hbm.shape[1], most):
            block_ref[at, part] = dot(left, right_ref[:, part], 1, 0).astype(bf16)
        copies.append(
            pltpu.make_async_copy(block_ref.at[at, :], out_hbm.at[at, :], sems.at[i])
        )
        copies[-1].start()
    for copy in copies:
        copy.wait()


def outer(left, right, name, most):
    count, high = left.shape
    wide = right.shape[1]
    return pl.pallas_call(
        functools.partial(outer_body, most),
        out_shape=like((high, wide), bf16),
        in_specs=[whole] * 2,
        out_specs=pl.BlockSpec(memory_space=pl.ANY),
        scratch_shapes=[
            pltpu.VMEM((high, wide), bf16),
            pltpu.SemaphoreType.DMA((len(tiles_of(high, 256)),)),
        ],
        cost_estimate=pl.CostEstimate(
            flops=2 * count * wide * high, bytes_accessed=2 * wide * high, transcendentals=0
        ),
        compiler_params=pltpu.CompilerParams(vmem_limit_bytes=16 * MIB),
        name=name,
    )(kept(left), kept(right))


def sum_body(rows, bias_ref, sums_ref, *refs):
    *term_refs, after_ref, own_ref, sent_ref = refs
    wide = own_ref.shape[1]
    me = lax.axis_index("tok")
    summed = sum(ref[...].astype(f32) for ref in term_refs)
    bias = jnp.where(me == 0, bias_ref[:, :wide], bias_ref[:, wide:])
    row = lax.broadcasted_iota(jnp.int32, summed.shape, 0)
    summed = summed + jnp.where(lax.rem(row, 2 * rows) < rows, bias, 0.0)
    low, high = summed[: 2 * rows], summed[2 * rows :]
    own_ref[...] = jnp.where(me == 0, low, high).astype(bf16)
    rest = sums_ref[...]
    row = lax.broadcasted_iota(jnp.int32, low.shape, 0)
    extra = jnp.zeros_like(low)
    for i in range(3):
        term = rest.astype(bf16).astype(f32)
        extra = jnp.where(row == i, term, extra)
        rest = rest - term
    sent = jnp.concatenate([jnp.where(me == 0, high, low), extra], axis=0)
    sent_ref[...] = sent.astype(bf16)


def final_body(rows, own_ref, got_ref, sums_ref, hidden_ref, rows_ref, grad_ref, out_sums_ref, bias_ref):
    wide = own_ref.shape[1]
    me = lax.axis_index("tok")
    own, got = own_ref[...].astype(f32), got_ref[...].astype(f32)
    own_sums, got_sums = sums_ref[...], jnp.sum(got[2 * rows :], axis=0, keepdims=True)
    for i in range(2):
        at = pl.ds(i * wide, wide)
        part = jnp.where(me == i, own, got[: 2 * rows])
        rows_ref[:, at] = part[:rows].astype(bf16)
        grad_ref[:, at] = part[rows:].astype(bf16)
        out_sums_ref[:, at] = jnp.where(me == i, own_sums, got_sums)
    bias_ref[...] = jnp.sum(hidden_ref[...].astype(f32), axis=0, keepdims=True)


def make_small(nn):
    def across(array, shift):
        return lax.ppermute(array, "nout", [(i, i ^ shift) for i in range(nn)])

    def on_device(tokens, weight_in, bias_in, weight_out, bias_out, grad_out):
        rows, cols = tokens.shape
        wide, hid = weight_in.shape
        half = hid // 2
        pair = 2 * rows
        count = 2 * nn * rows
        sem = pltpu.SemaphoreType.DMA

        mine = jnp.concatenate([tokens, grad_out], axis=0)
        me = lax.axis_index("tok")
        own = lax.dynamic_slice_in_dim(mine, me * wide, wide, 1)
        sent = lax.dynamic_slice_in_dim(mine, (1 - me) * wide, wide, 1)
        got = lax.ppermute(sent, "tok", swap)

        def load_in(mine, name, after):
            return call(
                functools.partial(load_body, mine),
                name,
                [like((wide, half), bf16)],
                grant=MIB,
                scratch=[sem((4,))],
                specs=[hbm, pl.BlockSpec(memory_space=pl.ANY)],
            )(in_hbm(weight_in), after)

        (in_far,) = load_in(False, "load_far", sent)
        tiles, farthest = call(
            pair_body, "pair_tiles", [like((2 * pair, wide + more), bf16) for more in (0, 128)]
        )(
            kept(own), kept(got), kept(in_far)
        )
        pieces = [across(tiles, shift) for shift in range(1, nn - 1)]
        pieces = [across(farthest, nn - 1)] + pieces[::-1] + [tiles]
        (in_own,) = load_in(True, "load_own", tiles)

        def product(body, name, outs, *args):
            return call(body, name, outs, grant=8 * MIB)(*map(kept, args))

        crossing = like((count, half + 128), bf16)
        side, ends = like((count, half), bf16), like((count, wide), f32)
        sent, x_cols, dy_cols, sums = product(
            functools.partial(far_pre_body, rows, nn),
            "far_pre",
            [side] + [like((count, wide), bf16)] * 2 + [like((1, wide), f32)],
            *pieces,
            in_far,
            in_own,
        )
        got = lax.ppermute(sent, "kin", swap)
        (own,) = product(own_pre_body, "own_pre", [like((count, half), f32)], x_cols, in_own, sent)
        (own_pre,) = product(add_body, "add_pre", [crossing], own, got)
        other_pre = lax.ppermute(own_pre, "tok", swap)
        sides = [side]
        sent = product(far_grad_body, "far_grad", sides, dy_cols, weight_out, own_pre)
        got = [lax.ppermute(part, "kin", swap) for part in sent]
        (own,) = product(own_grad_body, "own_grad", [like((count, half), f32)], dy_cols, weight_out)
        (own_grad,) = product(add_body, "add_grad", [crossing], own, *got)
        other_grad = lax.ppermute(own_grad, "tok", swap)
        slopes, *act_own = call(gelu_body, "gelu", [like((count, half), f32)] + sides)(
            bias_in.reshape(1, hid), kept(own_pre), kept(other_pre), kept(own_grad)
        )
        act_far = [lax.ppermute(part, "kin", swap) for part in act_own]
        (forward,) = product(own_forward_body, "own_forward", [ends], *act_own, weight_out)
        act, forward = product(
            far_forward_body,
            "far_forward",
            [like((count, hid), bf16), ends],
            *act_own,
            *act_far,
            weight_out,
            forward,
        )
        (grad_own,) = product(
            grad_pre_body, "grad_pre", [side], slopes, own_grad, other_grad, forward
        )
        grad_far = lax.ppermute(grad_own, "kin", swap)
        (backward,) = product(own_backward_body, "own_backward", [ends], grad_own, in_own)
        grad, *blocks = product(
            functools.partial(blocks_body, rows),
            "output_blocks",
            [like((count, hid), bf16)] + [like((2 * pair, wide), bf16)] * nn,
            grad_own,
            grad_far,
            forward,
            backward,
            in_far,
        )

        weight_in_grad = outer(x_cols, grad, "weight_in_grad", 256)
        weight_out_grad = outer(act, dy_cols, "weight_out_grad", 1536)

        terms = [across(blocks[i], nn - 1 - i) for i in range(nn - 1)] + [blocks[-1]]
        own, sent = call(
            functools.partial(sum_body, rows),
            "sum_blocks",
            [like((pair, wide), bf16), like((2 * pair, wide), bf16)],
            specs=[whole] * (nn + 2) + [hbm],
        )(
            bias_out.reshape(1, cols),
            kept(sums),
            *[kept(term) for term in terms],
            in_hbm(weight_in_grad),
        )
        got = lax.ppermute(sent, "tok", swap)
        output_rows, grad_tokens, bias_out_grad, bias_in_grad = call(
            functools.partial(final_body, rows),
            "final_rows",
            [like((rows, cols), bf16)] * 2 + [like((1, cols), f32), like((1, hid), f32)],
            resident=False,
        )(kept(own), kept(got), kept(sums), kept(grad))
        return (
            output_rows,
            grad_tokens,
            weight_in_grad,
            weight_out_grad,
            bias_in_grad.reshape(hid),
            bias_out_grad.reshape(cols),
        )

    return on_device


def make_plain(nt, nk, nn):
    spread, square = nt * nn, nk * nt

    def on_device(tokens, weight_in, bias_in, weight_out, bias_out, grad_out):
        rows, cols = tokens.shape
        wide, hid = weight_in.shape
        part = hid // square
        pair = 2 * rows
        total = pair * spread

        mine = jnp.concatenate([tokens, grad_out], axis=0)
        by_owner = mine.reshape(pair, nt, wide).transpose(1, 0, 2)
        chunks = jnp.broadcast_to(by_owner[:, None], (nt, nn, pair, wide))
        mixed = exchange(chunks.reshape(spread, pair, wide), ("tok", "nout")).reshape(total, wide)
        is_fwd = (lax.broadcasted_iota(jnp.int32, (total, 1), 0) % pair) < rows

        col_sums = jnp.sum(jnp.where(is_fwd, 0.0, mixed.astype(jnp.float32)), axis=0)
        bias_out_grad = lax.all_gather(col_sums, "tok", axis=0, tiled=True)

        partial = jnp.where(is_fwd, dot(mixed, weight_in, 1, 0), dot(mixed, weight_out, 1, 1))
        partial = partial.astype(jnp.bfloat16).reshape(total, square, part).transpose(1, 0, 2)
        got = exchange(partial, ("kin", "tok"))
        summed = jnp.sum(got.astype(jnp.float32), axis=0).reshape(spread, 2, rows, part)
        at = lax.axis_index(("kin", "tok"))
        pre_act = summed[:, 0] + lax.dynamic_slice_in_dim(bias_in, at * part, part)
        activated, slopes = gelu_parts(pre_act)
        grad_pre = summed[:, 1] * slopes
        both = jnp.stack([activated, grad_pre], axis=1).astype(jnp.bfloat16).reshape(total, part)
        both = exchange(jnp.broadcast_to(both[None], (square, total, part)), ("kin", "tok"))
        both = both.transpose(1, 0, 2).reshape(total, hid)

        split = both.reshape(spread, 2, rows, hid)
        act = split[:, 0].reshape(spread * rows, hid)
        grad_half = split[:, 1].reshape(spread * rows, hid)
        split = mixed.reshape(spread, 2, rows, wide)
        x_cols = split[:, 0].reshape(spread * rows, wide)
        dy_cols = split[:, 1].reshape(spread * rows, wide)
        bias_in_grad = jnp.sum(grad_half.astype(jnp.float32), axis=0)

        block = jnp.stack(
            [
                dot(act, weight_out, 1, 0).reshape(spread, rows, wide),
                dot(grad_half, weight_in, 1, 1).reshape(spread, rows, wide),
            ],
            axis=1,
        )
        block = block.astype(jnp.bfloat16).reshape(spread, pair, wide)
        back = exchange(block, ("tok", "nout")).reshape(nt, nn, pair, wide)
        weight_in_grad = dot(x_cols, grad_half, 0, 0).astype(jnp.bfloat16)
        weight_out_grad = dot(act, dy_cols, 0, 0).astype(jnp.bfloat16)
        final = jnp.sum(back.astype(jnp.float32), axis=1).transpose(1, 0, 2).reshape(pair, cols)
        output_rows = (final[:rows] + bias_out).astype(jnp.bfloat16)
        grad_tokens = final[rows:].astype(jnp.bfloat16)
        return (output_rows, grad_tokens, weight_in_grad, weight_out_grad, bias_in_grad, bias_out_grad)

    return on_device


def solution(mesh):
    nt, nk, nn = mesh.shape["tok"], mesh.shape["kin"], mesh.shape["nout"]
    return jax.shard_map(
        make_small(nn) if (nt, nk) == (2, 2) and nn in (2, 4) else make_plain(nt, nk, nn),
        mesh=mesh,
        in_specs=(
            P(("groups", "tok", "nout"), "kin"),
            P(("kin", "tok"), "nout"),
            P("nout"),
            P("nout", ("kin", "tok")),
            P("kin"),
            P(("groups", "tok", "nout"), "kin"),
        ),
        out_specs=(
            P(("groups", "tok", "nout"), "kin"),
            P(("groups", "tok", "nout"), "kin"),
            P(("groups", "kin", "tok"), "nout"),
            P(("groups", "nout"), ("kin", "tok")),
            P(("groups", "nout")),
            P(("groups", "kin")),
        ),
        check_vma=False,
    )
```

```python
import functools

import jax
import jax.numpy as jnp
from jax import lax
from jax.experimental import pallas as pl
from jax.experimental.pallas import tpu as pltpu
from jax.sharding import PartitionSpec as P

inv_root_two = 0.7071067811865476
inv_root_two_pi = 0.3989422804014327

MIB = 1 << 20
bf16, f32 = jnp.bfloat16, jnp.float32
like = jax.ShapeDtypeStruct
whole = pl.BlockSpec(memory_space=pltpu.VMEM)
hbm = pl.BlockSpec(memory_space=pltpu.HBM)
swap = [(0, 1), (1, 0)]


def gelu_parts(hidden):
    normal_cdf = 0.5 * (1.0 + lax.erf(hidden * inv_root_two))
    density = jnp.exp(-0.5 * hidden * hidden) * inv_root_two_pi
    return (hidden * normal_cdf, normal_cdf + hidden * density)


def dot(left, right, left_dim, right_dim):
    return lax.dot_general(
        left, right, (((left_dim,), (right_dim,)), ((), ())), preferred_element_type=jnp.float32
    )


def exchange(chunks, axes):
    return lax.all_to_all(chunks, axes, split_axis=0, concat_axis=0, tiled=True)


def dot_turned(rows, weight):
    return dot(weight, rows, 1, 1).T


def tile_of(size, most):
    return max(t for t in range(128, most + 1, 128) if size % t == 0)


def tiles_of(size, most=512):
    tile = tile_of(size, most)
    return [pl.ds(i * tile, tile) for i in range(size // tile)]


def call(body, name, outs, grant=4 * MIB, flops=0, moved=0, scratch=(), resident=True, specs=None):
    shapes = [pltpu.VMEM(o.shape, o.dtype) if resident else o for o in outs]

    def run(*args):
        cost = pl.CostEstimate(flops=flops, bytes_accessed=moved, transcendentals=0)
        return pl.pallas_call(
            body,
            out_shape=shapes,
            in_specs=specs or [whole] * len(args),
            out_specs=[whole] * len(outs),
            scratch_shapes=list(scratch),
            cost_estimate=cost,
            compiler_params=pltpu.CompilerParams(vmem_limit_bytes=grant),
            name=name,
        )(*args)

    return run


def kept(array):
    return pltpu.with_memory_space_constraint(array, pltpu.VMEM)


def in_hbm(array):
    return pltpu.with_memory_space_constraint(array, pltpu.HBM)


def apart(mixed, rows):
    total, wide = mixed.shape
    tiles = mixed.reshape(total // (4 * rows), 2, 2 * rows, wide)
    even, odd = tiles[:, 0], tiles[:, 1]
    is_low = lax.broadcasted_iota(jnp.int32, even.shape, 1) < rows
    first = jnp.where(is_low, even, pltpu.roll(odd, rows, 1))
    second = jnp.where(is_low, pltpu.roll(even, rows, 1), odd)
    return first.reshape(total // 2, wide), second.reshape(total // 2, wide)


def together(first, second, rows):
    total, wide = first.shape
    first = first.reshape(total // (2 * rows), 2 * rows, wide)
    second = second.reshape(total // (2 * rows), 2 * rows, wide)
    is_low = lax.broadcasted_iota(jnp.int32, first.shape, 1) < rows
    even = jnp.where(is_low, first, pltpu.roll(second, rows, 1))
    odd = jnp.where(is_low, pltpu.roll(first, rows, 1), second)
    return jnp.stack([even, odd], axis=1).reshape(2 * total, wide)


def ordered(me, own, far, axis=0):
    low, high = jnp.where(me == 0, own, far), jnp.where(me == 0, far, own)
    return jnp.concatenate([low, high], axis=axis)


def half_of(size, mine):
    core = lax.axis_index("kin")
    at = core if mine else 1 - core
    return pl.ds(pl.multiple_of(at * size, size), size)


def own_rows(half):
    return lax.axis_index("kin") * half


def far_rows(half):
    return (1 - lax.axis_index("kin")) * half


def half_tiles(half, mine):
    first = own_rows(half) if mine else far_rows(half)
    tile = tile_of(half, 512)
    return [
        (pl.ds(i * tile, tile), pl.ds(pl.multiple_of(first + i * tile, tile), tile))
        for i in range(half // tile)
    ]


def load_body(firsts_of, hbm_ref, after_ref, *refs):
    *out_refs, sems = refs
    copies = []
    for i, (first_of, out_ref) in enumerate(zip(firsts_of, out_refs)):
        size, wide = out_ref.shape
        source = hbm_ref.at[:, pl.ds(pl.multiple_of(first_of(), 128), wide)]
        for j in range(4):
            part = pl.ds(j * (size // 4), size // 4)
            copies.append(
                pltpu.make_async_copy(source.at[part, :], out_ref.at[part, :], sems.at[i, j])
            )
    for copy in copies:
        copy.start()
    for copy in copies:
        copy.wait()


def pair_body(own_ref, got_ref, after_ref, *out_refs):
    tiles = ordered(lax.axis_index("tok"), own_ref[...], got_ref[...])
    count, wide = tiles.shape
    for out_ref in out_refs:
        out_ref[:, :wide] = tiles
        if out_ref.shape[1] > wide:
            out_ref[:, wide:] = jnp.zeros((count, out_ref.shape[1] - wide), bf16)


def far_pre_body(rows, count, *refs):
    *piece_refs, w_in_ref, w_last_ref, after_ref = refs[: count + 3]
    sent_ref, x_ref, dy_ref, sums_ref = refs[count + 3 :]
    wide = x_ref.shape[1]
    mixed = jnp.concatenate([ref[:, :wide] for ref in piece_refs], axis=0)
    x_cols, dy_cols = apart(mixed.astype(f32), rows)
    sums_ref[...] = jnp.sum(dy_cols, axis=0, keepdims=True)
    x_cols, dy_cols = x_cols.astype(bf16), dy_cols.astype(bf16)
    x_ref[...], dy_ref[...] = x_cols, dy_cols
    first = w_in_ref.shape[1]
    for at in tiles_of(first):
        sent_ref[:, at] = dot(x_cols, w_in_ref[:, at], 1, 0).astype(bf16)
    sent_ref[:, first:] = dot(x_cols, w_last_ref[...], 1, 0).astype(bf16)


def own_pre_body(x_ref, w_in_ref, after_ref, own_ref):
    x_cols = x_ref[...]
    for at in tiles_of(own_ref.shape[1]):
        own_ref[:, at] = dot(x_cols, w_in_ref[:, at], 1, 0)


def far_grad_body(dy_ref, w_out_ref, after_ref, sent_ref):
    dy_cols = dy_ref[...]
    for at, there in half_tiles(sent_ref.shape[1], False):
        sent_ref[:, at] = dot_turned(dy_cols, w_out_ref[there, :]).astype(bf16)


def own_grad_body(dy_ref, w_out_ref, own_ref):
    dy_cols = dy_ref[...]
    for at, there in half_tiles(own_ref.shape[1], True):
        own_ref[:, at] = dot_turned(dy_cols, w_out_ref[there, :])


def add_body(own_ref, got_ref, out_ref):
    half = own_ref.shape[1]
    out_ref[:, :half] = (own_ref[...] + got_ref[...].astype(f32)).astype(bf16)
    out_ref[:, half:] = jnp.zeros((own_ref.shape[0], out_ref.shape[1] - half), bf16)


def gelu_body(bias_ref, own_ref, other_ref, after_ref, slopes_ref, act_ref):
    half = act_ref.shape[1]
    bias = bias_ref[:, half_of(half, True)]
    tile = tile_of(half, 512)
    for i in range(half // tile):
        at = pl.ds(i * tile, tile)
        pre_act = own_ref[:, at].astype(f32) + other_ref[:, at].astype(f32)
        activated, slopes = gelu_parts(pre_act + bias[:, i * tile : (i + 1) * tile])
        slopes_ref[:, at] = slopes
        act_ref[:, at] = activated.astype(bf16)


def grad_pre_body(slopes_ref, own_ref, other_ref, after_ref, later_ref, grad_ref):
    half = pl.ds(0, grad_ref.shape[1])
    grad_act = own_ref[:, half].astype(f32) + other_ref[:, half].astype(f32)
    grad_ref[...] = (grad_act * slopes_ref[...]).astype(bf16)


def own_forward_body(act_ref, w_out_ref, out_ref):
    act = act_ref[...]
    part = half_of(act.shape[1], True)
    for at in tiles_of(out_ref.shape[1]):
        out_ref[:, at] = dot(act, w_out_ref[part, at], 1, 0)


def far_forward_body(far_ref, w_out_ref, terms_ref, out_ref):
    act = far_ref[...]
    part = half_of(act.shape[1], False)
    for at in tiles_of(out_ref.shape[1]):
        out_ref[:, at] = terms_ref[:, at] + dot(act, w_out_ref[part, at], 1, 0)


def own_backward_body(grad_ref, w_in_ref, out_ref):
    grad = grad_ref[...]
    for at in tiles_of(out_ref.shape[1]):
        out_ref[:, at] = dot_turned(grad, w_in_ref[at, :])


def blocks_body(
    rows, own_ref, far_ref, forward_ref, backward_ref, w_in_ref, w_last_ref, grad_ref, *out_refs
):
    grad = far_ref[...]
    grad_ref[...] = ordered(lax.axis_index("kin"), own_ref[...], grad, 1)
    size = out_refs[0].shape[0]
    first = w_in_ref.shape[1]
    for at in tiles_of(forward_ref.shape[1]):
        backward = backward_ref[:, at] + dot_turned(grad[:, :first], w_in_ref[at, :])
        backward = backward + dot_turned(grad[:, first:], w_last_ref[at, :])
        terms = together(forward_ref[:, at], backward, rows).astype(bf16)
        for i, out_ref in enumerate(out_refs):
            out_ref[:, at] = terms[i * size : (i + 1) * size]


def outer_body(most, first_of, left_ref, right_ref, *refs):
    out_hbm, block_ref, sems = refs[-3:]
    first = first_of(left_ref.shape[1])
    copies = []
    for i, at in enumerate(tiles_of(left_ref.shape[1], most)):
        left = left_ref[:, at].T
        for part in tiles_of(out_hbm.shape[1], 512):
            block_ref[at, part] = dot(left, right_ref[:, part], 1, 0).astype(bf16)
        there = pl.ds(pl.multiple_of(first + at.start, at.size), at.size)
        copies.append(
            pltpu.make_async_copy(block_ref.at[at, :], out_hbm.at[there, :], sems.at[i])
        )
        copies[-1].start()
    for copy in copies:
        copy.wait()


def outer(left, right, high, name, first_of, into=None, most=128):
    count, size = left.shape
    wide = right.shape[1]
    anywhere = pl.BlockSpec(memory_space=pl.ANY)
    return pl.pallas_call(
        functools.partial(outer_body, most, first_of),
        out_shape=like((high, wide), bf16),
        in_specs=[whole] * 2 + ([] if into is None else [anywhere]),
        out_specs=anywhere,
        scratch_shapes=[
            pltpu.VMEM((size, wide), bf16),
            pltpu.SemaphoreType.DMA((len(tiles_of(size, most)),)),
        ],
        input_output_aliases={} if into is None else {2: 0},
        compiler_params=pltpu.CompilerParams(vmem_limit_bytes=16 * MIB),
        name=name,
    )(kept(left), kept(right), *([] if into is None else [into]))


def sum_body(rows, bias_ref, sums_ref, *refs):
    *term_refs, after_ref, own_ref, sent_ref = refs
    wide = own_ref.shape[1]
    me = lax.axis_index("tok")
    summed = sum(ref[...].astype(f32) for ref in term_refs)
    bias = jnp.where(me == 0, bias_ref[:, :wide], bias_ref[:, wide:])
    row = lax.broadcasted_iota(jnp.int32, summed.shape, 0)
    summed = summed + jnp.where(lax.rem(row, 2 * rows) < rows, bias, 0.0)
    low, high = summed[: 2 * rows], summed[2 * rows :]
    own_ref[...] = jnp.where(me == 0, low, high).astype(bf16)
    rest = sums_ref[...]
    row = lax.broadcasted_iota(jnp.int32, low.shape, 0)
    extra = jnp.zeros_like(low)
    for i in range(3):
        term = rest.astype(bf16).astype(f32)
        extra = jnp.where(row == i, term, extra)
        rest = rest - term
    sent = jnp.concatenate([jnp.where(me == 0, high, low), extra], axis=0)
    sent_ref[...] = sent.astype(bf16)


def final_body(rows, own_ref, got_ref, sums_ref, hidden_ref, rows_ref, grad_ref, out_sums_ref, bias_ref):
    wide = own_ref.shape[1]
    me = lax.axis_index("tok")
    own, got = own_ref[...].astype(f32), got_ref[...].astype(f32)
    own_sums, got_sums = sums_ref[...], jnp.sum(got[2 * rows :], axis=0, keepdims=True)
    for i in range(2):
        at = pl.ds(i * wide, wide)
        part = jnp.where(me == i, own, got[: 2 * rows])
        rows_ref[:, at] = part[:rows].astype(bf16)
        grad_ref[:, at] = part[rows:].astype(bf16)
        out_sums_ref[:, at] = jnp.where(me == i, own_sums, got_sums)
    bias_ref[...] = jnp.sum(hidden_ref[...].astype(f32), axis=0, keepdims=True)


def make_small(nn):
    def across(array, shift):
        return lax.ppermute(array, "nout", [(i, i ^ shift) for i in range(nn)])

    def on_device(tokens, weight_in, bias_in, weight_out, bias_out, grad_out):
        rows, cols = tokens.shape
        wide, hid = weight_in.shape
        half = hid // 2
        pair = 2 * rows
        count = 2 * nn * rows
        sem = pltpu.SemaphoreType.DMA

        mine = jnp.concatenate([tokens, grad_out], axis=0)
        me = lax.axis_index("tok")
        own = lax.dynamic_slice_in_dim(mine, me * wide, wide, 1)
        sent = lax.dynamic_slice_in_dim(mine, (1 - me) * wide, wide, 1)
        got = lax.ppermute(sent, "tok", swap)

        last = tile_of(half, 512)

        def load_in(name, after, *parts):
            return call(
                functools.partial(load_body, [first_of for first_of, _ in parts]),
                name,
                [like((wide, width), bf16) for _, width in parts],
                grant=MIB,
                scratch=[sem((len(parts), 4))],
                specs=[hbm, pl.BlockSpec(memory_space=pl.ANY)],
            )(in_hbm(weight_in), after)

        (in_far,) = load_in("load_far", sent, (lambda: far_rows(half), half - last))
        tiles, farthest = call(
            pair_body, "pair_tiles", [like((2 * pair, wide + more), bf16) for more in (0, 128)]
        )(
            kept(own), kept(got), kept(in_far)
        )
        pieces = [across(tiles, shift) for shift in range(1, nn - 1)]
        pieces = [across(farthest, nn - 1)] + pieces[::-1] + [tiles]
        in_own, in_last = load_in(
            "load_own",
            tiles,
            (lambda: own_rows(half), half),
            (lambda: far_rows(half) + half - last, last),
        )

        def product(body, name, outs, *args):
            return call(body, name, outs, grant=8 * MIB)(*map(kept, args))

        crossing = like((count, half + 128), bf16)
        side, ends = like((count, half), bf16), like((count, wide), f32)
        sent, x_cols, dy_cols, sums = product(
            functools.partial(far_pre_body, rows, nn),
            "far_pre",
            [side] + [like((count, wide), bf16)] * 2 + [like((1, wide), f32)],
            *pieces,
            in_far,
            in_last,
            in_own,
        )
        got = lax.ppermute(sent, "kin", swap)
        (own,) = product(own_pre_body, "own_pre", [like((count, half), f32)], x_cols, in_own, sent)
        (own_pre,) = product(add_body, "add_pre", [crossing], own, got)
        other_pre = lax.ppermute(own_pre, "tok", swap)
        (sent,) = product(far_grad_body, "far_grad", [side], dy_cols, weight_out, own_pre)
        got = lax.ppermute(sent, "kin", swap)
        (own,) = product(own_grad_body, "own_grad", [like((count, half), f32)], dy_cols, weight_out)
        (own_grad,) = product(add_body, "add_grad", [crossing], own, got)
        other_grad = lax.ppermute(own_grad, "tok", swap)
        slopes, act_own = call(gelu_body, "gelu", [like((count, half), f32), side])(
            bias_in.reshape(1, hid), kept(own_pre), kept(other_pre), kept(own_grad)
        )
        act_far = lax.ppermute(act_own, "kin", swap)
        (forward,) = product(own_forward_body, "own_forward", [ends], act_own, weight_out)
        (forward,) = product(
            far_forward_body, "far_forward", [ends], act_far, weight_out, forward
        )
        weight_out_grad = outer(act_own, dy_cols, hid, "weight_out_grad_own", own_rows)
        (grad_own,) = call(
            grad_pre_body, "grad_pre", [side], specs=[whole] * 4 + [hbm]
        )(
            kept(slopes),
            kept(own_grad),
            kept(other_grad),
            kept(forward),
            in_hbm(weight_out_grad),
        )
        grad_far = lax.ppermute(grad_own, "kin", swap)
        (backward,) = product(own_backward_body, "own_backward", [ends], grad_own, in_own)
        grad, *blocks = product(
            functools.partial(blocks_body, rows),
            "output_blocks",
            [like((count, hid), bf16)] + [like((2 * pair, wide), bf16)] * nn,
            grad_own,
            grad_far,
            forward,
            backward,
            in_far,
            in_last,
        )

        weight_in_grad = outer(x_cols, grad, wide, "weight_in_grad", lambda size: 0)
        weight_out_grad = outer(
            act_far, dy_cols, hid, "weight_out_grad_far", far_rows, into=weight_out_grad
        )

        terms = [across(blocks[i], nn - 1 - i) for i in range(nn - 1)] + [blocks[-1]]
        own, sent = call(
            functools.partial(sum_body, rows),
            "sum_blocks",
            [like((pair, wide), bf16), like((2 * pair, wide), bf16)],
            specs=[whole] * (nn + 2) + [hbm],
        )(
            bias_out.reshape(1, cols),
            kept(sums),
            *[kept(term) for term in terms],
            in_hbm(weight_in_grad),
        )
        got = lax.ppermute(sent, "tok", swap)
        output_rows, grad_tokens, bias_out_grad, bias_in_grad = call(
            functools.partial(final_body, rows),
            "final_rows",
            [like((rows, cols), bf16)] * 2 + [like((1, cols), f32), like((1, hid), f32)],
            resident=False,
        )(kept(own), kept(got), kept(sums), kept(grad))
        return (
            output_rows,
            grad_tokens,
            weight_in_grad,
            weight_out_grad,
            bias_in_grad.reshape(hid),
            bias_out_grad.reshape(cols),
        )

    return on_device


def make_plain(nt, nk, nn):
    spread, square = nt * nn, nk * nt

    def on_device(tokens, weight_in, bias_in, weight_out, bias_out, grad_out):
        rows, cols = tokens.shape
        wide, hid = weight_in.shape
        part = hid // square
        pair = 2 * rows
        total = pair * spread

        mine = jnp.concatenate([tokens, grad_out], axis=0)
        by_owner = mine.reshape(pair, nt, wide).transpose(1, 0, 2)
        chunks = jnp.broadcast_to(by_owner[:, None], (nt, nn, pair, wide))
        mixed = exchange(chunks.reshape(spread, pair, wide), ("tok", "nout")).reshape(total, wide)
        is_fwd = (lax.broadcasted_iota(jnp.int32, (total, 1), 0) % pair) < rows

        col_sums = jnp.sum(jnp.where(is_fwd, 0.0, mixed.astype(jnp.float32)), axis=0)
        bias_out_grad = lax.all_gather(col_sums, "tok", axis=0, tiled=True)

        partial = jnp.where(is_fwd, dot(mixed, weight_in, 1, 0), dot(mixed, weight_out, 1, 1))
        partial = partial.astype(jnp.bfloat16).reshape(total, square, part).transpose(1, 0, 2)
        got = exchange(partial, ("kin", "tok"))
        summed = jnp.sum(got.astype(jnp.float32), axis=0).reshape(spread, 2, rows, part)
        at = lax.axis_index(("kin", "tok"))
        pre_act = summed[:, 0] + lax.dynamic_slice_in_dim(bias_in, at * part, part)
        activated, slopes = gelu_parts(pre_act)
        grad_pre = summed[:, 1] * slopes
        both = jnp.stack([activated, grad_pre], axis=1).astype(jnp.bfloat16).reshape(total, part)
        both = exchange(jnp.broadcast_to(both[None], (square, total, part)), ("kin", "tok"))
        both = both.transpose(1, 0, 2).reshape(total, hid)

        split = both.reshape(spread, 2, rows, hid)
        act = split[:, 0].reshape(spread * rows, hid)
        grad_half = split[:, 1].reshape(spread * rows, hid)
        split = mixed.reshape(spread, 2, rows, wide)
        x_cols = split[:, 0].reshape(spread * rows, wide)
        dy_cols = split[:, 1].reshape(spread * rows, wide)
        bias_in_grad = jnp.sum(grad_half.astype(jnp.float32), axis=0)

        block = jnp.stack(
            [
                dot(act, weight_out, 1, 0).reshape(spread, rows, wide),
                dot(grad_half, weight_in, 1, 1).reshape(spread, rows, wide),
            ],
            axis=1,
        )
        block = block.astype(jnp.bfloat16).reshape(spread, pair, wide)
        back = exchange(block, ("tok", "nout")).reshape(nt, nn, pair, wide)
        weight_in_grad = dot(x_cols, grad_half, 0, 0).astype(jnp.bfloat16)
        weight_out_grad = dot(act, dy_cols, 0, 0).astype(jnp.bfloat16)
        final = jnp.sum(back.astype(jnp.float32), axis=1).transpose(1, 0, 2).reshape(pair, cols)
        output_rows = (final[:rows] + bias_out).astype(jnp.bfloat16)
        grad_tokens = final[rows:].astype(jnp.bfloat16)
        return (output_rows, grad_tokens, weight_in_grad, weight_out_grad, bias_in_grad, bias_out_grad)

    return on_device


def solution(mesh):
    nt, nk, nn = mesh.shape["tok"], mesh.shape["kin"], mesh.shape["nout"]
    return jax.shard_map(
        make_small(nn) if (nt, nk) == (2, 2) and nn in (2, 4) else make_plain(nt, nk, nn),
        mesh=mesh,
        in_specs=(
            P(("groups", "tok", "nout"), "kin"),
            P(("kin", "tok"), "nout"),
            P("nout"),
            P("nout", ("kin", "tok")),
            P("kin"),
            P(("groups", "tok", "nout"), "kin"),
        ),
        out_specs=(
            P(("groups", "tok", "nout"), "kin"),
            P(("groups", "tok", "nout"), "kin"),
            P(("groups", "kin", "tok"), "nout"),
            P(("groups", "nout"), ("kin", "tok")),
            P(("groups", "nout")),
            P(("groups", "kin")),
        ),
        check_vma=False,
    )
```

```python
import functools

import jax
import jax.numpy as jnp
from jax import lax
from jax.experimental import pallas as pl
from jax.experimental.pallas import tpu as pltpu
from jax.sharding import PartitionSpec as P

inv_root_two = 0.7071067811865476
inv_root_two_pi = 0.3989422804014327

MIB = 1 << 20
bf16, f32 = jnp.bfloat16, jnp.float32
like = jax.ShapeDtypeStruct
whole = pl.BlockSpec(memory_space=pltpu.VMEM)
hbm = pl.BlockSpec(memory_space=pltpu.HBM)
swap = [(0, 1), (1, 0)]


def gelu_parts(hidden):
    normal_cdf = 0.5 * (1.0 + lax.erf(hidden * inv_root_two))
    density = jnp.exp(-0.5 * hidden * hidden) * inv_root_two_pi
    return (hidden * normal_cdf, normal_cdf + hidden * density)


def dot(left, right, left_dim, right_dim):
    return lax.dot_general(
        left, right, (((left_dim,), (right_dim,)), ((), ())), preferred_element_type=jnp.float32
    )


def exchange(chunks, axes):
    return lax.all_to_all(chunks, axes, split_axis=0, concat_axis=0, tiled=True)


def dot_turned(rows, weight):
    return dot(weight, rows, 1, 1).T


def tile_of(size, most):
    return max(t for t in range(128, most + 1, 128) if size % t == 0)


def tiles_of(size, most=512):
    tile = tile_of(size, most)
    return [pl.ds(i * tile, tile) for i in range(size // tile)]


def call(body, name, outs, grant=4 * MIB, flops=0, moved=0, scratch=(), resident=True, specs=None):
    shapes = [pltpu.VMEM(o.shape, o.dtype) if resident else o for o in outs]

    def run(*args):
        cost = pl.CostEstimate(flops=flops, bytes_accessed=moved, transcendentals=0)
        return pl.pallas_call(
            body,
            out_shape=shapes,
            in_specs=specs or [whole] * len(args),
            out_specs=[whole] * len(outs),
            scratch_shapes=list(scratch),
            cost_estimate=cost,
            compiler_params=pltpu.CompilerParams(vmem_limit_bytes=grant),
            name=name,
        )(*args)

    return run


def kept(array):
    return pltpu.with_memory_space_constraint(array, pltpu.VMEM)


def in_hbm(array):
    return pltpu.with_memory_space_constraint(array, pltpu.HBM)


def apart(mixed, rows):
    total, wide = mixed.shape
    tiles = mixed.reshape(total // (4 * rows), 2, 2 * rows, wide)
    even, odd = tiles[:, 0], tiles[:, 1]
    is_low = lax.broadcasted_iota(jnp.int32, even.shape, 1) < rows
    first = jnp.where(is_low, even, pltpu.roll(odd, rows, 1))
    second = jnp.where(is_low, pltpu.roll(even, rows, 1), odd)
    return first.reshape(total // 2, wide), second.reshape(total // 2, wide)


def together(first, second, rows):
    total, wide = first.shape
    first = first.reshape(total // (2 * rows), 2 * rows, wide)
    second = second.reshape(total // (2 * rows), 2 * rows, wide)
    is_low = lax.broadcasted_iota(jnp.int32, first.shape, 1) < rows
    even = jnp.where(is_low, first, pltpu.roll(second, rows, 1))
    odd = jnp.where(is_low, pltpu.roll(first, rows, 1), second)
    return jnp.stack([even, odd], axis=1).reshape(2 * total, wide)


def ordered(me, own, far, axis=0):
    low, high = jnp.where(me == 0, own, far), jnp.where(me == 0, far, own)
    return jnp.concatenate([low, high], axis=axis)


def half_of(size, mine):
    core = lax.axis_index("kin")
    at = core if mine else 1 - core
    return pl.ds(pl.multiple_of(at * size, size), size)


def own_rows(half):
    return lax.axis_index("kin") * half


def far_rows(half):
    return (1 - lax.axis_index("kin")) * half


def half_tiles(half, mine, most):
    first = own_rows(half) if mine else far_rows(half)
    tile = tile_of(half, most)
    return [
        (pl.ds(i * tile, tile), pl.ds(pl.multiple_of(first + i * tile, tile), tile))
        for i in range(half // tile)
    ]


def load_body(hbm_ref, after_ref, out_ref, sems):
    size, wide = out_ref.shape
    half = hbm_ref.shape[1] // 2
    source = pl.ds(pl.multiple_of(far_rows(half), 128), wide)
    copies = []
    for j in range(4):
        part = pl.ds(j * (size // 4), size // 4)
        copies.append(
            pltpu.make_async_copy(hbm_ref.at[part, source], out_ref.at[part, :], sems.at[j])
        )
    for copy in copies:
        copy.start()
    for copy in copies:
        copy.wait()


def load_and_turn_body(hbm_ref, after_ref, far_ref, own_ref, last_ref, own_turned, far_turned, sems):
    wide, half = own_ref.shape
    first, last = far_ref.shape[1], last_ref.shape[1]
    size = wide // 4
    parts = [pl.ds(j * size, size) for j in range(4)]
    from_own = pl.ds(pl.multiple_of(own_rows(half), 128), half)
    from_last = pl.ds(pl.multiple_of(far_rows(half) + first, 128), last)
    copies = [
        [
            pltpu.make_async_copy(hbm_ref.at[part, source], ref.at[part, :], sems.at[i, j])
            for j, part in enumerate(parts)
        ]
        for i, (source, ref) in enumerate(((from_own, own_ref), (from_last, last_ref)))
    ]
    for copy in copies[0] + copies[1]:
        copy.start()
    for part in parts:
        far_turned[:first, part] = far_ref[part, :].T
    for part, copy in zip(parts, copies[0]):
        copy.wait()
        own_turned[:, part] = own_ref[part, :].T
    for part, copy in zip(parts, copies[1]):
        copy.wait()
        far_turned[first:, part] = last_ref[part, :].T


def pair_body(own_ref, got_ref, after_ref, *out_refs):
    tiles = ordered(lax.axis_index("tok"), own_ref[...], got_ref[...])
    count, wide = tiles.shape
    for out_ref in out_refs:
        out_ref[:, :wide] = tiles
        if out_ref.shape[1] > wide:
            out_ref[:, wide:] = jnp.zeros((count, out_ref.shape[1] - wide), bf16)


def far_pre_body(rows, count, *refs):
    *piece_refs, w_in_ref, w_last_ref, after_ref = refs[: count + 3]
    sent_ref, x_ref, dy_ref, sums_ref = refs[count + 3 :]
    wide = x_ref.shape[1]
    mixed = jnp.concatenate([ref[:, :wide] for ref in piece_refs], axis=0)
    x_cols, dy_cols = apart(mixed.astype(f32), rows)
    sums_ref[...] = jnp.sum(dy_cols, axis=0, keepdims=True)
    x_cols, dy_cols = x_cols.astype(bf16), dy_cols.astype(bf16)
    x_ref[...], dy_ref[...] = x_cols, dy_cols
    first = w_in_ref.shape[1]
    for at in tiles_of(first):
        sent_ref[:, at] = dot(x_cols, w_in_ref[:, at], 1, 0).astype(bf16)
    sent_ref[:, first:] = dot(x_cols, w_last_ref[...], 1, 0).astype(bf16)


def own_pre_body(x_ref, w_in_ref, after_ref, own_ref):
    x_cols = x_ref[...]
    for at in tiles_of(own_ref.shape[1]):
        own_ref[:, at] = dot(x_cols, w_in_ref[:, at], 1, 0)


def far_grad_body(dy_ref, w_out_ref, after_ref, sent_ref):
    dy_cols = dy_ref[...]
    for at, there in half_tiles(sent_ref.shape[1], False, 1536):
        sent_ref[:, at] = dot_turned(dy_cols, w_out_ref[there, :]).astype(bf16)


def own_grad_body(dy_ref, w_out_ref, own_ref):
    dy_cols = dy_ref[...]
    for at, there in half_tiles(own_ref.shape[1], True, 1536):
        own_ref[:, at] = dot(dy_cols, w_out_ref[there, :], 1, 1)


def add_body(own_ref, got_ref, out_ref):
    count, half = own_ref.shape
    out_ref[:, :half] = (own_ref[...] + got_ref[...].astype(f32)).astype(bf16)
    out_ref[:, half:] = jnp.zeros((count, out_ref.shape[1] - half), bf16)


def add_pre_body(own_ref, got_ref, sums_ref, out_ref):
    count, half = own_ref.shape
    out_ref[:, :half] = (own_ref[...] + got_ref[...].astype(f32)).astype(bf16)
    sums = [sums_ref[:, at] for at in tiles_of(sums_ref.shape[1], 128)]
    sums = jnp.concatenate(sums, axis=0)
    high = sums.astype(bf16).astype(f32)
    rest = jnp.zeros((count - 2 * sums.shape[0], 128), f32)
    out_ref[:, half:] = jnp.concatenate([high, sums - high, rest], axis=0).astype(bf16)


def gelu_body(bias_ref, own_ref, other_ref, after_ref, slopes_ref, act_ref):
    half = act_ref.shape[1]
    bias = bias_ref[:, half_of(half, True)]
    tile = tile_of(half, 512)
    for i in range(half // tile):
        at = pl.ds(i * tile, tile)
        pre_act = own_ref[:, at].astype(f32) + other_ref[:, at].astype(f32)
        activated, slopes = gelu_parts(pre_act + bias[:, i * tile : (i + 1) * tile])
        slopes_ref[:, at] = slopes
        act_ref[:, at] = activated.astype(bf16)


def grad_pre_body(slopes_ref, own_ref, other_ref, after_ref, later_ref, grad_ref):
    half = pl.ds(0, grad_ref.shape[1])
    grad_act = own_ref[:, half].astype(f32) + other_ref[:, half].astype(f32)
    grad_ref[...] = (grad_act * slopes_ref[...]).astype(bf16)


def own_forward_body(act_ref, w_out_ref, out_ref):
    act = act_ref[...]
    part = half_of(act.shape[1], True)
    for at in tiles_of(out_ref.shape[1]):
        out_ref[:, at] = dot(act, w_out_ref[part, at], 1, 0)


def far_forward_body(far_ref, w_out_ref, terms_ref, out_ref):
    act = far_ref[...]
    part = half_of(act.shape[1], False)
    for at in tiles_of(out_ref.shape[1], 1536):
        out_ref[:, at] = terms_ref[:, at] + dot(act, w_out_ref[part, at], 1, 0)


def own_backward_body(grad_ref, turned_ref, out_ref):
    grad = grad_ref[...]
    for at in tiles_of(out_ref.shape[1]):
        out_ref[:, at] = dot(grad, turned_ref[:, at], 1, 0)


def blocks_body(rows, own_ref, far_ref, forward_ref, backward_ref, turned_ref, grad_ref, *out_refs):
    grad = far_ref[...]
    grad_ref[...] = ordered(lax.axis_index("kin"), own_ref[...], grad, 1)
    size = out_refs[0].shape[0]
    for at in tiles_of(forward_ref.shape[1]):
        backward = backward_ref[:, at] + dot(grad, turned_ref[:, at], 1, 0)
        terms = together(forward_ref[:, at], backward, rows).astype(bf16)
        for i, out_ref in enumerate(out_refs):
            out_ref[:, at] = terms[i * size : (i + 1) * size]


def outer_body(most, first_of, left_ref, right_ref, *refs):
    out_hbm, block_ref, sems = refs[-3:]
    first = first_of(left_ref.shape[1])
    copies = []
    for i, at in enumerate(tiles_of(left_ref.shape[1], most)):
        left = left_ref[:, at].T
        for part in tiles_of(out_hbm.shape[1], 512):
            block_ref[at, part] = dot(left, right_ref[:, part], 1, 0).astype(bf16)
        there = pl.ds(pl.multiple_of(first + at.start, at.size), at.size)
        copies.append(
            pltpu.make_async_copy(block_ref.at[at, :], out_hbm.at[there, :], sems.at[i])
        )
        copies[-1].start()
    for copy in copies:
        copy.wait()


def outer(left, right, high, name, first_of, into=None, most=128):
    count, size = left.shape
    wide = right.shape[1]
    anywhere = pl.BlockSpec(memory_space=pl.ANY)
    return pl.pallas_call(
        functools.partial(outer_body, most, first_of),
        out_shape=like((high, wide), bf16),
        in_specs=[whole] * 2 + ([] if into is None else [anywhere]),
        out_specs=anywhere,
        scratch_shapes=[
            pltpu.VMEM((size, wide), bf16),
            pltpu.SemaphoreType.DMA((len(tiles_of(size, most)),)),
        ],
        input_output_aliases={} if into is None else {2: 0},
        compiler_params=pltpu.CompilerParams(vmem_limit_bytes=16 * MIB),
        name=name,
    )(kept(left), kept(right), *([] if into is None else [into]))


def sum_body(rows, bias_ref, *refs):
    *term_refs, after_ref, own_ref, sent_ref = refs
    wide = own_ref.shape[1]
    me = lax.axis_index("tok")
    summed = sum(ref[...].astype(f32) for ref in term_refs)
    bias = jnp.where(me == 0, bias_ref[:, :wide], bias_ref[:, wide:])
    row = lax.broadcasted_iota(jnp.int32, summed.shape, 0)
    summed = summed + jnp.where(lax.rem(row, 2 * rows) < rows, bias, 0.0)
    low, high = summed[: 2 * rows], summed[2 * rows :]
    own_ref[...] = jnp.where(me == 0, low, high).astype(bf16)
    sent_ref[...] = jnp.where(me == 0, high, low).astype(bf16)


def final_body(
    rows, own_ref, got_ref, sums_ref, other_ref, hidden_ref, rows_ref, grad_ref, out_sums_ref, bias_ref
):
    wide = own_ref.shape[1]
    me = lax.axis_index("tok")
    own, got = own_ref[...].astype(f32), got_ref[...].astype(f32)
    extra = other_ref[:, other_ref.shape[1] - 128 :].astype(f32)
    steps = wide // 128
    got_sums = extra[:steps] + extra[steps : 2 * steps]
    got_sums = jnp.concatenate([got_sums[i : i + 1] for i in range(steps)], axis=1)
    for i in range(2):
        at = pl.ds(i * wide, wide)
        part = jnp.where(me == i, own, got)
        rows_ref[:, at] = part[:rows].astype(bf16)
        grad_ref[:, at] = part[rows:].astype(bf16)
        out_sums_ref[:, at] = jnp.where(me == i, sums_ref[...], got_sums)
    bias_ref[...] = jnp.sum(hidden_ref[...].astype(f32), axis=0, keepdims=True)


def make_small(nn):
    def across(array, shift):
        return lax.ppermute(array, "nout", [(i, i ^ shift) for i in range(nn)])

    def on_device(tokens, weight_in, bias_in, weight_out, bias_out, grad_out):
        rows, cols = tokens.shape
        wide, hid = weight_in.shape
        half = hid // 2
        pair = 2 * rows
        count = 2 * nn * rows
        sem = pltpu.SemaphoreType.DMA

        mine = jnp.concatenate([tokens, grad_out], axis=0)
        me = lax.axis_index("tok")
        own = lax.dynamic_slice_in_dim(mine, me * wide, wide, 1)
        sent = lax.dynamic_slice_in_dim(mine, (1 - me) * wide, wide, 1)
        got = lax.ppermute(sent, "tok", swap)

        last = tile_of(half, 512)
        (in_far,) = call(
            load_body,
            "load_far",
            [like((wide, half - last), bf16)],
            grant=MIB,
            scratch=[sem((4,))],
            specs=[hbm, pl.BlockSpec(memory_space=pl.ANY)],
        )(in_hbm(weight_in), sent)
        tiles, farthest = call(
            pair_body, "pair_tiles", [like((2 * pair, wide + more), bf16) for more in (0, 128)]
        )(
            kept(own), kept(got), kept(in_far)
        )
        pieces = [across(tiles, shift) for shift in range(1, nn - 1)]
        pieces = [across(farthest, nn - 1)] + pieces[::-1] + [tiles]
        in_own, in_last, own_turned, far_turned = call(
            load_and_turn_body,
            "load_own",
            [like((wide, half), bf16), like((wide, last), bf16)] + [like((half, wide), bf16)] * 2,
            grant=8 * MIB,
            scratch=[sem((2, 4))],
            specs=[hbm, pl.BlockSpec(memory_space=pl.ANY), whole],
        )(in_hbm(weight_in), tiles, kept(in_far))

        def product(body, name, outs, *args):
            return call(body, name, outs, grant=8 * MIB)(*map(kept, args))

        crossing = like((count, half + 128), bf16)
        side, ends = like((count, half), bf16), like((count, wide), f32)
        sent, x_cols, dy_cols, sums = product(
            functools.partial(far_pre_body, rows, nn),
            "far_pre",
            [side] + [like((count, wide), bf16)] * 2 + [like((1, wide), f32)],
            *pieces,
            in_far,
            in_last,
            in_own,
        )
        got = lax.ppermute(sent, "kin", swap)
        (own,) = product(own_pre_body, "own_pre", [like((count, half), f32)], x_cols, in_own, sent)
        (own_pre,) = product(add_pre_body, "add_pre", [crossing], own, got, sums)
        other_pre = lax.ppermute(own_pre, "tok", swap)
        (sent,) = product(far_grad_body, "far_grad", [side], dy_cols, weight_out, own_pre)
        got = lax.ppermute(sent, "kin", swap)
        (own,) = product(own_grad_body, "own_grad", [like((count, half), f32)], dy_cols, weight_out)
        (own_grad,) = product(add_body, "add_grad", [crossing], own, got)
        other_grad = lax.ppermute(own_grad, "tok", swap)
        slopes, act_own = call(gelu_body, "gelu", [like((count, half), f32), side])(
            bias_in.reshape(1, hid), kept(own_pre), kept(other_pre), kept(own_grad)
        )
        act_far = lax.ppermute(act_own, "kin", swap)
        (forward,) = product(own_forward_body, "own_forward", [ends], act_own, weight_out)
        (forward,) = product(
            far_forward_body, "far_forward", [ends], act_far, weight_out, forward
        )
        weight_out_grad = outer(act_own, dy_cols, hid, "weight_out_grad_own", own_rows)
        (grad_own,) = call(
            grad_pre_body, "grad_pre", [side], specs=[whole] * 4 + [hbm]
        )(
            kept(slopes),
            kept(own_grad),
            kept(other_grad),
            kept(forward),
            in_hbm(weight_out_grad),
        )
        grad_far = lax.ppermute(grad_own, "kin", swap)
        (backward,) = product(own_backward_body, "own_backward", [ends], grad_own, own_turned)
        grad, *blocks = product(
            functools.partial(blocks_body, rows),
            "output_blocks",
            [like((count, hid), bf16)] + [like((2 * pair, wide), bf16)] * nn,
            grad_own,
            grad_far,
            forward,
            backward,
            far_turned,
        )

        weight_in_grad = outer(x_cols, grad, wide, "weight_in_grad", lambda size: 0)
        weight_out_grad = outer(
            act_far, dy_cols, hid, "weight_out_grad_far", far_rows, into=weight_out_grad
        )

        terms = [across(blocks[i], nn - 1 - i) for i in range(nn - 1)] + [blocks[-1]]
        own, sent = call(
            functools.partial(sum_body, rows),
            "sum_blocks",
            [like((pair, wide), bf16)] * 2,
            specs=[whole] * (nn + 1) + [hbm],
        )(
            bias_out.reshape(1, cols),
            *[kept(term) for term in terms],
            in_hbm(weight_in_grad),
        )
        got = lax.ppermute(sent, "tok", swap)
        output_rows, grad_tokens, bias_out_grad, bias_in_grad = call(
            functools.partial(final_body, rows),
            "final_rows",
            [like((rows, cols), bf16)] * 2 + [like((1, cols), f32), like((1, hid), f32)],
            resident=False,
        )(kept(own), kept(got), kept(sums), kept(other_pre), kept(grad))
        return (
            output_rows,
            grad_tokens,
            weight_in_grad,
            weight_out_grad,
            bias_in_grad.reshape(hid),
            bias_out_grad.reshape(cols),
        )

    return on_device


def make_plain(nt, nk, nn):
    spread, square = nt * nn, nk * nt

    def on_device(tokens, weight_in, bias_in, weight_out, bias_out, grad_out):
        rows, cols = tokens.shape
        wide, hid = weight_in.shape
        part = hid // square
        pair = 2 * rows
        total = pair * spread

        mine = jnp.concatenate([tokens, grad_out], axis=0)
        by_owner = mine.reshape(pair, nt, wide).transpose(1, 0, 2)
        chunks = jnp.broadcast_to(by_owner[:, None], (nt, nn, pair, wide))
        mixed = exchange(chunks.reshape(spread, pair, wide), ("tok", "nout")).reshape(total, wide)
        is_fwd = (lax.broadcasted_iota(jnp.int32, (total, 1), 0) % pair) < rows

        col_sums = jnp.sum(jnp.where(is_fwd, 0.0, mixed.astype(jnp.float32)), axis=0)
        bias_out_grad = lax.all_gather(col_sums, "tok", axis=0, tiled=True)

        partial = jnp.where(is_fwd, dot(mixed, weight_in, 1, 0), dot(mixed, weight_out, 1, 1))
        partial = partial.astype(jnp.bfloat16).reshape(total, square, part).transpose(1, 0, 2)
        got = exchange(partial, ("kin", "tok"))
        summed = jnp.sum(got.astype(jnp.float32), axis=0).reshape(spread, 2, rows, part)
        at = lax.axis_index(("kin", "tok"))
        pre_act = summed[:, 0] + lax.dynamic_slice_in_dim(bias_in, at * part, part)
        activated, slopes = gelu_parts(pre_act)
        grad_pre = summed[:, 1] * slopes
        both = jnp.stack([activated, grad_pre], axis=1).astype(jnp.bfloat16).reshape(total, part)
        both = exchange(jnp.broadcast_to(both[None], (square, total, part)), ("kin", "tok"))
        both = both.transpose(1, 0, 2).reshape(total, hid)

        split = both.reshape(spread, 2, rows, hid)
        act = split[:, 0].reshape(spread * rows, hid)
        grad_half = split[:, 1].reshape(spread * rows, hid)
        split = mixed.reshape(spread, 2, rows, wide)
        x_cols = split[:, 0].reshape(spread * rows, wide)
        dy_cols = split[:, 1].reshape(spread * rows, wide)
        bias_in_grad = jnp.sum(grad_half.astype(jnp.float32), axis=0)

        block = jnp.stack(
            [
                dot(act, weight_out, 1, 0).reshape(spread, rows, wide),
                dot(grad_half, weight_in, 1, 1).reshape(spread, rows, wide),
            ],
            axis=1,
        )
        block = block.astype(jnp.bfloat16).reshape(spread, pair, wide)
        back = exchange(block, ("tok", "nout")).reshape(nt, nn, pair, wide)
        weight_in_grad = dot(x_cols, grad_half, 0, 0).astype(jnp.bfloat16)
        weight_out_grad = dot(act, dy_cols, 0, 0).astype(jnp.bfloat16)
        final = jnp.sum(back.astype(jnp.float32), axis=1).transpose(1, 0, 2).reshape(pair, cols)
        output_rows = (final[:rows] + bias_out).astype(jnp.bfloat16)
        grad_tokens = final[rows:].astype(jnp.bfloat16)
        return (output_rows, grad_tokens, weight_in_grad, weight_out_grad, bias_in_grad, bias_out_grad)

    return on_device


def solution(mesh):
    nt, nk, nn = mesh.shape["tok"], mesh.shape["kin"], mesh.shape["nout"]
    return jax.shard_map(
        make_small(nn) if (nt, nk) == (2, 2) and nn in (2, 4) else make_plain(nt, nk, nn),
        mesh=mesh,
        in_specs=(
            P(("groups", "tok", "nout"), "kin"),
            P(("kin", "tok"), "nout"),
            P("nout"),
            P("nout", ("kin", "tok")),
            P("kin"),
            P(("groups", "tok", "nout"), "kin"),
        ),
        out_specs=(
            P(("groups", "tok", "nout"), "kin"),
            P(("groups", "tok", "nout"), "kin"),
            P(("groups", "kin", "tok"), "nout"),
            P(("groups", "nout"), ("kin", "tok")),
            P(("groups", "nout")),
            P(("groups", "kin")),
        ),
        check_vma=False,
    )
```

```python
import functools

import jax
import jax.numpy as jnp
from jax import lax
from jax.experimental import pallas as pl
from jax.experimental.pallas import tpu as pltpu
from jax.sharding import PartitionSpec as P

inv_root_two = 0.7071067811865476
inv_root_two_pi = 0.3989422804014327

MIB = 1 << 20
bf16, f32 = jnp.bfloat16, jnp.float32
like = jax.ShapeDtypeStruct
whole = pl.BlockSpec(memory_space=pltpu.VMEM)
hbm = pl.BlockSpec(memory_space=pltpu.HBM)
swap = [(0, 1), (1, 0)]


def gelu_parts(hidden):
    normal_cdf = 0.5 * (1.0 + lax.erf(hidden * inv_root_two))
    density = jnp.exp(-0.5 * hidden * hidden) * inv_root_two_pi
    return (hidden * normal_cdf, normal_cdf + hidden * density)


def dot(left, right, left_dim, right_dim):
    return lax.dot_general(
        left, right, (((left_dim,), (right_dim,)), ((), ())), preferred_element_type=jnp.float32
    )


def exchange(chunks, axes):
    return lax.all_to_all(chunks, axes, split_axis=0, concat_axis=0, tiled=True)


def tile_of(size, most):
    return max(t for t in range(128, most + 1, 128) if size % t == 0)


def tiles_of(size, most=512):
    tile = tile_of(size, most)
    return [pl.ds(i * tile, tile) for i in range(size // tile)]


def call(body, name, outs, grant=4 * MIB, flops=0, moved=0, scratch=(), resident=True, specs=None):
    shapes = [pltpu.VMEM(o.shape, o.dtype) if resident else o for o in outs]

    def run(*args):
        cost = pl.CostEstimate(flops=flops, bytes_accessed=moved, transcendentals=0)
        return pl.pallas_call(
            body,
            out_shape=shapes,
            in_specs=specs or [whole] * len(args),
            out_specs=[whole] * len(outs),
            scratch_shapes=list(scratch),
            cost_estimate=cost,
            compiler_params=pltpu.CompilerParams(vmem_limit_bytes=grant),
            name=name,
        )(*args)

    return run


def kept(array):
    return pltpu.with_memory_space_constraint(array, pltpu.VMEM)


def in_hbm(array):
    return pltpu.with_memory_space_constraint(array, pltpu.HBM)


def apart(mixed, rows):
    total, wide = mixed.shape
    tiles = mixed.reshape(total // (4 * rows), 2, 2 * rows, wide)
    even, odd = tiles[:, 0], tiles[:, 1]
    is_low = lax.broadcasted_iota(jnp.int32, even.shape, 1) < rows
    first = jnp.where(is_low, even, pltpu.roll(odd, rows, 1))
    second = jnp.where(is_low, pltpu.roll(even, rows, 1), odd)
    return first.reshape(total // 2, wide), second.reshape(total // 2, wide)


def together(first, second, rows):
    total, wide = first.shape
    first = first.reshape(total // (2 * rows), 2 * rows, wide)
    second = second.reshape(total // (2 * rows), 2 * rows, wide)
    is_low = lax.broadcasted_iota(jnp.int32, first.shape, 1) < rows
    even = jnp.where(is_low, first, pltpu.roll(second, rows, 1))
    odd = jnp.where(is_low, pltpu.roll(first, rows, 1), second)
    return jnp.stack([even, odd], axis=1).reshape(2 * total, wide)


def ordered(me, own, far, axis=0):
    low, high = jnp.where(me == 0, own, far), jnp.where(me == 0, far, own)
    return jnp.concatenate([low, high], axis=axis)


def half_of(size, mine):
    core = lax.axis_index("kin")
    at = core if mine else 1 - core
    return pl.ds(pl.multiple_of(at * size, size), size)


def own_rows(half):
    return lax.axis_index("kin") * half


def far_rows(half):
    return (1 - lax.axis_index("kin")) * half


def half_tiles(half, mine):
    first = own_rows(half) if mine else far_rows(half)
    tile = tile_of(half, 512)
    return [
        (pl.ds(i * tile, tile), pl.ds(pl.multiple_of(first + i * tile, tile), tile))
        for i in range(half // tile)
    ]


def load_body(hbm_ref, after_ref, out_ref, sems):
    size, wide = out_ref.shape
    half = hbm_ref.shape[1] // 2
    source = pl.ds(pl.multiple_of(far_rows(half), 128), wide)
    copies = []
    for j in range(4):
        part = pl.ds(j * (size // 4), size // 4)
        copies.append(
            pltpu.make_async_copy(hbm_ref.at[part, source], out_ref.at[part, :], sems.at[j])
        )
    for copy in copies:
        copy.start()
    for copy in copies:
        copy.wait()


def load_and_turn_body(hbm_ref, after_ref, far_ref, w_out_ref, *refs):
    own_ref, last_ref, own_turned, far_turned, out_turned, sems = refs
    wide, half = own_ref.shape
    first, last = far_ref.shape[1], last_ref.shape[1]
    size = wide // 4
    parts = [pl.ds(j * size, size) for j in range(4)]
    from_own = pl.ds(pl.multiple_of(own_rows(half), 128), half)
    from_last = pl.ds(pl.multiple_of(far_rows(half) + first, 128), last)
    copies = [
        [
            pltpu.make_async_copy(hbm_ref.at[part, source], ref.at[part, :], sems.at[i, j])
            for j, part in enumerate(parts)
        ]
        for i, (source, ref) in enumerate(((from_own, own_ref), (from_last, last_ref)))
    ]
    for copy in copies[0] + copies[1]:
        copy.start()
    for part in tiles_of(w_out_ref.shape[0]):
        out_turned[:, part] = w_out_ref[part, :].T
    for part in parts:
        far_turned[:first, part] = far_ref[part, :].T
    for part, copy in zip(parts, copies[0]):
        copy.wait()
        own_turned[:, part] = own_ref[part, :].T
    for part, copy in zip(parts, copies[1]):
        copy.wait()
        far_turned[first:, part] = last_ref[part, :].T


def pair_body(own_ref, got_ref, after_ref, *out_refs):
    tiles = ordered(lax.axis_index("tok"), own_ref[...], got_ref[...])
    count, wide = tiles.shape
    for out_ref in out_refs:
        out_ref[:, :wide] = tiles
        if out_ref.shape[1] > wide:
            out_ref[:, wide:] = jnp.zeros((count, out_ref.shape[1] - wide), bf16)


def far_pre_body(rows, count, *refs):
    *piece_refs, w_in_ref, w_last_ref, after_ref = refs[: count + 3]
    sent_ref, x_ref, dy_ref, sums_ref = refs[count + 3 :]
    wide = x_ref.shape[1]
    mixed = jnp.concatenate([ref[:, :wide] for ref in piece_refs], axis=0)
    x_cols, dy_cols = apart(mixed.astype(f32), rows)
    sums_ref[...] = jnp.sum(dy_cols, axis=0, keepdims=True)
    x_cols, dy_cols = x_cols.astype(bf16), dy_cols.astype(bf16)
    x_ref[...], dy_ref[...] = x_cols, dy_cols
    first = w_in_ref.shape[1]
    for at in tiles_of(first):
        sent_ref[:, at] = dot(x_cols, w_in_ref[:, at], 1, 0).astype(bf16)
    sent_ref[:, first:] = dot(x_cols, w_last_ref[...], 1, 0).astype(bf16)


def own_pre_body(x_ref, w_in_ref, after_ref, own_ref):
    x_cols = x_ref[...]
    for at in tiles_of(own_ref.shape[1]):
        own_ref[:, at] = dot(x_cols, w_in_ref[:, at], 1, 0)


def far_grad_body(dy_ref, turned_ref, after_ref, sent_ref):
    dy_cols = dy_ref[...]
    for at, there in half_tiles(sent_ref.shape[1], False):
        sent_ref[:, at] = dot(dy_cols, turned_ref[:, there], 1, 0).astype(bf16)


def own_grad_body(dy_ref, turned_ref, own_ref):
    dy_cols = dy_ref[...]
    for at, there in half_tiles(own_ref.shape[1], True):
        own_ref[:, at] = dot(dy_cols, turned_ref[:, there], 1, 0)


def add_body(own_ref, got_ref, out_ref):
    count, half = own_ref.shape
    out_ref[:, :half] = (own_ref[...] + got_ref[...].astype(f32)).astype(bf16)
    out_ref[:, half:] = jnp.zeros((count, out_ref.shape[1] - half), bf16)


def add_pre_body(own_ref, got_ref, sums_ref, out_ref):
    count, half = own_ref.shape
    out_ref[:, :half] = (own_ref[...] + got_ref[...].astype(f32)).astype(bf16)
    sums = [sums_ref[:, at] for at in tiles_of(sums_ref.shape[1], 128)]
    sums = jnp.concatenate(sums, axis=0)
    high = sums.astype(bf16).astype(f32)
    rest = jnp.zeros((count - 2 * sums.shape[0], 128), f32)
    out_ref[:, half:] = jnp.concatenate([high, sums - high, rest], axis=0).astype(bf16)


def gelu_body(bias_ref, own_ref, other_ref, after_ref, slopes_ref, act_ref):
    half = act_ref.shape[1]
    bias = bias_ref[:, half_of(half, True)]
    tile = tile_of(half, 512)
    for i in range(half // tile):
        at = pl.ds(i * tile, tile)
        pre_act = own_ref[:, at].astype(f32) + other_ref[:, at].astype(f32)
        activated, slopes = gelu_parts(pre_act + bias[:, i * tile : (i + 1) * tile])
        slopes_ref[:, at] = slopes
        act_ref[:, at] = activated.astype(bf16)


def grad_pre_body(slopes_ref, own_ref, other_ref, after_ref, later_ref, grad_ref):
    half = pl.ds(0, grad_ref.shape[1])
    grad_act = own_ref[:, half].astype(f32) + other_ref[:, half].astype(f32)
    grad_ref[...] = (grad_act * slopes_ref[...]).astype(bf16)


def own_forward_body(act_ref, w_out_ref, out_ref):
    act = act_ref[...]
    part = half_of(act.shape[1], True)
    for at in tiles_of(out_ref.shape[1]):
        out_ref[:, at] = dot(act, w_out_ref[part, at], 1, 0)


def far_forward_body(far_ref, w_out_ref, terms_ref, out_ref):
    act = far_ref[...]
    part = half_of(act.shape[1], False)
    for at in tiles_of(out_ref.shape[1]):
        out_ref[:, at] = terms_ref[:, at] + dot(act, w_out_ref[part, at], 1, 0)


def own_backward_body(grad_ref, turned_ref, out_ref):
    grad = grad_ref[...]
    for at in tiles_of(out_ref.shape[1]):
        out_ref[:, at] = dot(grad, turned_ref[:, at], 1, 0)


def blocks_body(rows, own_ref, far_ref, forward_ref, backward_ref, turned_ref, grad_ref, *out_refs):
    grad = far_ref[...]
    grad_ref[...] = ordered(lax.axis_index("kin"), own_ref[...], grad, 1)
    size = out_refs[0].shape[0]
    for at in tiles_of(forward_ref.shape[1]):
        backward = backward_ref[:, at] + dot(grad, turned_ref[:, at], 1, 0)
        terms = together(forward_ref[:, at], backward, rows).astype(bf16)
        for i, out_ref in enumerate(out_refs):
            out_ref[:, at] = terms[i * size : (i + 1) * size]


def outer_body(most, first_of, left_ref, right_ref, *refs):
    out_hbm, block_ref, sems = refs[-3:]
    first = first_of(left_ref.shape[1])
    copies = []
    for i, at in enumerate(tiles_of(left_ref.shape[1], most)):
        left = left_ref[:, at].T
        for part in tiles_of(out_hbm.shape[1], 512):
            block_ref[at, part] = dot(left, right_ref[:, part], 1, 0).astype(bf16)
        there = pl.ds(pl.multiple_of(first + at.start, at.size), at.size)
        copies.append(
            pltpu.make_async_copy(block_ref.at[at, :], out_hbm.at[there, :], sems.at[i])
        )
        copies[-1].start()
    for copy in copies:
        copy.wait()


def outer(left, right, high, name, first_of, into=None, most=128):
    count, size = left.shape
    wide = right.shape[1]
    anywhere = pl.BlockSpec(memory_space=pl.ANY)
    return pl.pallas_call(
        functools.partial(outer_body, most, first_of),
        out_shape=like((high, wide), bf16),
        in_specs=[whole] * 2 + ([] if into is None else [anywhere]),
        out_specs=anywhere,
        scratch_shapes=[
            pltpu.VMEM((size, wide), bf16),
            pltpu.SemaphoreType.DMA((len(tiles_of(size, most)),)),
        ],
        input_output_aliases={} if into is None else {2: 0},
        compiler_params=pltpu.CompilerParams(vmem_limit_bytes=16 * MIB),
        name=name,
    )(kept(left), kept(right), *([] if into is None else [into]))


def sum_body(rows, bias_ref, *refs):
    *term_refs, after_ref, own_ref, sent_ref = refs
    wide = own_ref.shape[1]
    me = lax.axis_index("tok")
    summed = sum(ref[...].astype(f32) for ref in term_refs)
    bias = jnp.where(me == 0, bias_ref[:, :wide], bias_ref[:, wide:])
    row = lax.broadcasted_iota(jnp.int32, summed.shape, 0)
    summed = summed + jnp.where(lax.rem(row, 2 * rows) < rows, bias, 0.0)
    low, high = summed[: 2 * rows], summed[2 * rows :]
    own_ref[...] = jnp.where(me == 0, low, high).astype(bf16)
    sent_ref[...] = jnp.where(me == 0, high, low).astype(bf16)


def final_body(
    rows, own_ref, got_ref, sums_ref, other_ref, hidden_ref, rows_ref, grad_ref, out_sums_ref, bias_ref
):
    wide = own_ref.shape[1]
    me = lax.axis_index("tok")
    own, got = own_ref[...].astype(f32), got_ref[...].astype(f32)
    extra = other_ref[:, other_ref.shape[1] - 128 :].astype(f32)
    steps = wide // 128
    got_sums = extra[:steps] + extra[steps : 2 * steps]
    got_sums = jnp.concatenate([got_sums[i : i + 1] for i in range(steps)], axis=1)
    for i in range(2):
        at = pl.ds(i * wide, wide)
        part = jnp.where(me == i, own, got)
        rows_ref[:, at] = part[:rows].astype(bf16)
        grad_ref[:, at] = part[rows:].astype(bf16)
        out_sums_ref[:, at] = jnp.where(me == i, sums_ref[...], got_sums)
    bias_ref[...] = jnp.sum(hidden_ref[...].astype(f32), axis=0, keepdims=True)


def make_small(nn):
    def across(array, shift):
        return lax.ppermute(array, "nout", [(i, i ^ shift) for i in range(nn)])

    def on_device(tokens, weight_in, bias_in, weight_out, bias_out, grad_out):
        rows, cols = tokens.shape
        wide, hid = weight_in.shape
        half = hid // 2
        pair = 2 * rows
        count = 2 * nn * rows
        sem = pltpu.SemaphoreType.DMA

        mine = jnp.concatenate([tokens, grad_out], axis=0)
        me = lax.axis_index("tok")
        own = lax.dynamic_slice_in_dim(mine, me * wide, wide, 1)
        sent = lax.dynamic_slice_in_dim(mine, (1 - me) * wide, wide, 1)
        got = lax.ppermute(sent, "tok", swap)

        last = tile_of(half, 512)
        (in_far,) = call(
            load_body,
            "load_far",
            [like((wide, half - last), bf16)],
            grant=MIB,
            scratch=[sem((4,))],
            specs=[hbm, pl.BlockSpec(memory_space=pl.ANY)],
        )(in_hbm(weight_in), sent)
        tiles, farthest = call(
            pair_body, "pair_tiles", [like((2 * pair, wide + more), bf16) for more in (0, 128)]
        )(
            kept(own), kept(got), kept(in_far)
        )
        pieces = [across(tiles, shift) for shift in range(1, nn - 1)]
        pieces = [across(farthest, nn - 1)] + pieces[::-1] + [tiles]
        in_own, in_last, own_turned, far_turned, out_turned = call(
            load_and_turn_body,
            "load_own",
            [like((wide, half), bf16), like((wide, last), bf16)]
            + [like((half, wide), bf16)] * 2
            + [like((wide, hid), bf16)],
            grant=8 * MIB,
            scratch=[sem((2, 4))],
            specs=[hbm, pl.BlockSpec(memory_space=pl.ANY), whole, whole],
        )(in_hbm(weight_in), tiles, kept(in_far), kept(weight_out))

        def product(body, name, outs, *args):
            return call(body, name, outs, grant=8 * MIB)(*map(kept, args))

        crossing = like((count, half + 128), bf16)
        side, ends = like((count, half), bf16), like((count, wide), f32)
        sent, x_cols, dy_cols, sums = product(
            functools.partial(far_pre_body, rows, nn),
            "far_pre",
            [side] + [like((count, wide), bf16)] * 2 + [like((1, wide), f32)],
            *pieces,
            in_far,
            in_last,
            in_own,
        )
        got = lax.ppermute(sent, "kin", swap)
        (own,) = product(own_pre_body, "own_pre", [like((count, half), f32)], x_cols, in_own, sent)
        (own_pre,) = product(add_pre_body, "add_pre", [crossing], own, got, sums)
        other_pre = lax.ppermute(own_pre, "tok", swap)
        (sent,) = product(far_grad_body, "far_grad", [side], dy_cols, out_turned, own_pre)
        got = lax.ppermute(sent, "kin", swap)
        (own,) = product(own_grad_body, "own_grad", [like((count, half), f32)], dy_cols, out_turned)
        (own_grad,) = product(add_body, "add_grad", [crossing], own, got)
        other_grad = lax.ppermute(own_grad, "tok", swap)
        slopes, act_own = call(gelu_body, "gelu", [like((count, half), f32), side])(
            bias_in.reshape(1, hid), kept(own_pre), kept(other_pre), kept(own_grad)
        )
        act_far = lax.ppermute(act_own, "kin", swap)
        (forward,) = product(own_forward_body, "own_forward", [ends], act_own, weight_out)
        (forward,) = product(
            far_forward_body, "far_forward", [ends], act_far, weight_out, forward
        )
        weight_out_grad = outer(act_own, dy_cols, hid, "weight_out_grad_own", own_rows)
        (grad_own,) = call(
            grad_pre_body, "grad_pre", [side], specs=[whole] * 4 + [hbm]
        )(
            kept(slopes),
            kept(own_grad),
            kept(other_grad),
            kept(forward),
            in_hbm(weight_out_grad),
        )
        grad_far = lax.ppermute(grad_own, "kin", swap)
        (backward,) = product(own_backward_body, "own_backward", [ends], grad_own, own_turned)
        grad, *blocks = product(
            functools.partial(blocks_body, rows),
            "output_blocks",
            [like((count, hid), bf16)] + [like((2 * pair, wide), bf16)] * nn,
            grad_own,
            grad_far,
            forward,
            backward,
            far_turned,
        )

        weight_in_grad = outer(x_cols, grad, wide, "weight_in_grad", lambda size: 0)
        weight_out_grad = outer(
            act_far, dy_cols, hid, "weight_out_grad_far", far_rows, into=weight_out_grad
        )

        terms = [across(blocks[i], nn - 1 - i) for i in range(nn - 1)] + [blocks[-1]]
        own, sent = call(
            functools.partial(sum_body, rows),
            "sum_blocks",
            [like((pair, wide), bf16)] * 2,
            specs=[whole] * (nn + 1) + [hbm],
        )(
            bias_out.reshape(1, cols),
            *[kept(term) for term in terms],
            in_hbm(weight_in_grad),
        )
        got = lax.ppermute(sent, "tok", swap)
        output_rows, grad_tokens, bias_out_grad, bias_in_grad = call(
            functools.partial(final_body, rows),
            "final_rows",
            [like((rows, cols), bf16)] * 2 + [like((1, cols), f32), like((1, hid), f32)],
            resident=False,
        )(kept(own), kept(got), kept(sums), kept(other_pre), kept(grad))
        return (
            output_rows,
            grad_tokens,
            weight_in_grad,
            weight_out_grad,
            bias_in_grad.reshape(hid),
            bias_out_grad.reshape(cols),
        )

    return on_device


def make_plain(nt, nk, nn):
    spread, square = nt * nn, nk * nt

    def on_device(tokens, weight_in, bias_in, weight_out, bias_out, grad_out):
        rows, cols = tokens.shape
        wide, hid = weight_in.shape
        part = hid // square
        pair = 2 * rows
        total = pair * spread

        mine = jnp.concatenate([tokens, grad_out], axis=0)
        by_owner = mine.reshape(pair, nt, wide).transpose(1, 0, 2)
        chunks = jnp.broadcast_to(by_owner[:, None], (nt, nn, pair, wide))
        mixed = exchange(chunks.reshape(spread, pair, wide), ("tok", "nout")).reshape(total, wide)
        is_fwd = (lax.broadcasted_iota(jnp.int32, (total, 1), 0) % pair) < rows

        col_sums = jnp.sum(jnp.where(is_fwd, 0.0, mixed.astype(jnp.float32)), axis=0)
        bias_out_grad = lax.all_gather(col_sums, "tok", axis=0, tiled=True)

        partial = jnp.where(is_fwd, dot(mixed, weight_in, 1, 0), dot(mixed, weight_out, 1, 1))
        partial = partial.astype(jnp.bfloat16).reshape(total, square, part).transpose(1, 0, 2)
        got = exchange(partial, ("kin", "tok"))
        summed = jnp.sum(got.astype(jnp.float32), axis=0).reshape(spread, 2, rows, part)
        at = lax.axis_index(("kin", "tok"))
        pre_act = summed[:, 0] + lax.dynamic_slice_in_dim(bias_in, at * part, part)
        activated, slopes = gelu_parts(pre_act)
        grad_pre = summed[:, 1] * slopes
        both = jnp.stack([activated, grad_pre], axis=1).astype(jnp.bfloat16).reshape(total, part)
        both = exchange(jnp.broadcast_to(both[None], (square, total, part)), ("kin", "tok"))
        both = both.transpose(1, 0, 2).reshape(total, hid)

        split = both.reshape(spread, 2, rows, hid)
        act = split[:, 0].reshape(spread * rows, hid)
        grad_half = split[:, 1].reshape(spread * rows, hid)
        split = mixed.reshape(spread, 2, rows, wide)
        x_cols = split[:, 0].reshape(spread * rows, wide)
        dy_cols = split[:, 1].reshape(spread * rows, wide)
        bias_in_grad = jnp.sum(grad_half.astype(jnp.float32), axis=0)

        block = jnp.stack(
            [
                dot(act, weight_out, 1, 0).reshape(spread, rows, wide),
                dot(grad_half, weight_in, 1, 1).reshape(spread, rows, wide),
            ],
            axis=1,
        )
        block = block.astype(jnp.bfloat16).reshape(spread, pair, wide)
        back = exchange(block, ("tok", "nout")).reshape(nt, nn, pair, wide)
        weight_in_grad = dot(x_cols, grad_half, 0, 0).astype(jnp.bfloat16)
        weight_out_grad = dot(act, dy_cols, 0, 0).astype(jnp.bfloat16)
        final = jnp.sum(back.astype(jnp.float32), axis=1).transpose(1, 0, 2).reshape(pair, cols)
        output_rows = (final[:rows] + bias_out).astype(jnp.bfloat16)
        grad_tokens = final[rows:].astype(jnp.bfloat16)
        return (output_rows, grad_tokens, weight_in_grad, weight_out_grad, bias_in_grad, bias_out_grad)

    return on_device


def solution(mesh):
    nt, nk, nn = mesh.shape["tok"], mesh.shape["kin"], mesh.shape["nout"]
    return jax.shard_map(
        make_small(nn) if (nt, nk) == (2, 2) and nn in (2, 4) else make_plain(nt, nk, nn),
        mesh=mesh,
        in_specs=(
            P(("groups", "tok", "nout"), "kin"),
            P(("kin", "tok"), "nout"),
            P("nout"),
            P("nout", ("kin", "tok")),
            P("kin"),
            P(("groups", "tok", "nout"), "kin"),
        ),
        out_specs=(
            P(("groups", "tok", "nout"), "kin"),
            P(("groups", "tok", "nout"), "kin"),
            P(("groups", "kin", "tok"), "nout"),
            P(("groups", "nout"), ("kin", "tok")),
            P(("groups", "nout")),
            P(("groups", "kin")),
        ),
        check_vma=False,
    )
```

```python
import functools

import jax
import jax.numpy as jnp
from jax import lax
from jax.experimental import pallas as pl
from jax.experimental.pallas import tpu as pltpu
from jax.sharding import PartitionSpec as P

inv_root_two = 0.7071067811865476
inv_root_two_pi = 0.3989422804014327

MIB = 1 << 20
bf16, f32 = jnp.bfloat16, jnp.float32
like = jax.ShapeDtypeStruct
whole = pl.BlockSpec(memory_space=pltpu.VMEM)
hbm = pl.BlockSpec(memory_space=pltpu.HBM)
swap = [(0, 1), (1, 0)]


def gelu_parts(hidden):
    normal_cdf = 0.5 * (1.0 + lax.erf(hidden * inv_root_two))
    density = jnp.exp(-0.5 * hidden * hidden) * inv_root_two_pi
    return (hidden * normal_cdf, normal_cdf + hidden * density)


def dot(left, right, left_dim, right_dim):
    return lax.dot_general(
        left, right, (((left_dim,), (right_dim,)), ((), ())), preferred_element_type=jnp.float32
    )


def exchange(chunks, axes):
    return lax.all_to_all(chunks, axes, split_axis=0, concat_axis=0, tiled=True)


def dot_turned(rows, weight):
    return dot(weight, rows, 1, 1).T


def tile_of(size, most):
    return max(t for t in range(128, most + 1, 128) if size % t == 0)


def tiles_of(size, most=512):
    tile = tile_of(size, most)
    return [pl.ds(i * tile, tile) for i in range(size // tile)]


def call(body, name, outs, grant=4 * MIB, flops=0, moved=0, scratch=(), resident=True, specs=None):
    shapes = [pltpu.VMEM(o.shape, o.dtype) if resident else o for o in outs]

    def run(*args):
        cost = pl.CostEstimate(flops=flops, bytes_accessed=moved, transcendentals=0)
        return pl.pallas_call(
            body,
            out_shape=shapes,
            in_specs=specs or [whole] * len(args),
            out_specs=[whole] * len(outs),
            scratch_shapes=list(scratch),
            cost_estimate=cost,
            compiler_params=pltpu.CompilerParams(vmem_limit_bytes=grant),
            name=name,
        )(*args)

    return run


def kept(array):
    return pltpu.with_memory_space_constraint(array, pltpu.VMEM)


def in_hbm(array):
    return pltpu.with_memory_space_constraint(array, pltpu.HBM)


def apart(mixed, rows):
    total, wide = mixed.shape
    tiles = mixed.reshape(total // (4 * rows), 2, 2 * rows, wide)
    even, odd = tiles[:, 0], tiles[:, 1]
    is_low = lax.broadcasted_iota(jnp.int32, even.shape, 1) < rows
    first = jnp.where(is_low, even, pltpu.roll(odd, rows, 1))
    second = jnp.where(is_low, pltpu.roll(even, rows, 1), odd)
    return first.reshape(total // 2, wide), second.reshape(total // 2, wide)


def together(first, second, rows):
    total, wide = first.shape
    first = first.reshape(total // (2 * rows), 2 * rows, wide)
    second = second.reshape(total // (2 * rows), 2 * rows, wide)
    is_low = lax.broadcasted_iota(jnp.int32, first.shape, 1) < rows
    even = jnp.where(is_low, first, pltpu.roll(second, rows, 1))
    odd = jnp.where(is_low, pltpu.roll(first, rows, 1), second)
    return jnp.stack([even, odd], axis=1).reshape(2 * total, wide)


def ordered(me, own, far, axis=0):
    low, high = jnp.where(me == 0, own, far), jnp.where(me == 0, far, own)
    return jnp.concatenate([low, high], axis=axis)


def half_of(size, mine):
    core = lax.axis_index("kin")
    at = core if mine else 1 - core
    return pl.ds(pl.multiple_of(at * size, size), size)


def own_rows(half):
    return lax.axis_index("kin") * half


def far_rows(half):
    return (1 - lax.axis_index("kin")) * half


def half_tiles(half, mine, most):
    first = own_rows(half) if mine else far_rows(half)
    tile = tile_of(half, most)
    return [
        (pl.ds(i * tile, tile), pl.ds(pl.multiple_of(first + i * tile, tile), tile))
        for i in range(half // tile)
    ]


def load_body(hbm_ref, after_ref, out_ref, sems):
    size, wide = out_ref.shape
    half = hbm_ref.shape[1] // 2
    source = pl.ds(pl.multiple_of(far_rows(half), 128), wide)
    copies = []
    for j in range(4):
        part = pl.ds(j * (size // 4), size // 4)
        copies.append(
            pltpu.make_async_copy(hbm_ref.at[part, source], out_ref.at[part, :], sems.at[j])
        )
    for copy in copies:
        copy.start()
    for copy in copies:
        copy.wait()


def load_and_turn_body(hbm_ref, after_ref, far_ref, own_ref, last_ref, own_turned, far_turned, sems):
    wide, half = own_ref.shape
    first, last = far_ref.shape[1], last_ref.shape[1]
    size = wide // 4
    parts = [pl.ds(j * size, size) for j in range(4)]
    from_own = pl.ds(pl.multiple_of(own_rows(half), 128), half)
    from_last = pl.ds(pl.multiple_of(far_rows(half) + first, 128), last)
    copies = [
        [
            pltpu.make_async_copy(hbm_ref.at[part, source], ref.at[part, :], sems.at[i, j])
            for j, part in enumerate(parts)
        ]
        for i, (source, ref) in enumerate(((from_own, own_ref), (from_last, last_ref)))
    ]
    for copy in copies[0] + copies[1]:
        copy.start()
    for part in parts:
        far_turned[:first, part] = far_ref[part, :].T
    for part, copy in zip(parts, copies[0]):
        copy.wait()
        own_turned[:, part] = own_ref[part, :].T
    for part, copy in zip(parts, copies[1]):
        copy.wait()
        far_turned[first:, part] = last_ref[part, :].T


def pair_body(own_ref, got_ref, after_ref, *out_refs):
    tiles = ordered(lax.axis_index("tok"), own_ref[...], got_ref[...])
    count, wide = tiles.shape
    for out_ref in out_refs:
        out_ref[:, :wide] = tiles
        if out_ref.shape[1] > wide:
            out_ref[:, wide:] = jnp.zeros((count, out_ref.shape[1] - wide), bf16)


def far_pre_body(rows, count, *refs):
    *piece_refs, w_in_ref, w_last_ref, after_ref = refs[: count + 3]
    sent_ref, x_ref, dy_ref, sums_ref = refs[count + 3 :]
    wide = x_ref.shape[1]
    mixed = jnp.concatenate([ref[:, :wide] for ref in piece_refs], axis=0)
    x_cols, dy_cols = apart(mixed.astype(f32), rows)
    sums_ref[...] = jnp.sum(dy_cols, axis=0, keepdims=True)
    x_cols, dy_cols = x_cols.astype(bf16), dy_cols.astype(bf16)
    x_ref[...], dy_ref[...] = x_cols, dy_cols
    first = w_in_ref.shape[1]
    for at in tiles_of(first):
        sent_ref[:, at] = dot(x_cols, w_in_ref[:, at], 1, 0).astype(bf16)
    sent_ref[:, first:] = dot(x_cols, w_last_ref[...], 1, 0).astype(bf16)


def own_pre_body(x_ref, w_in_ref, after_ref, own_ref):
    x_cols = x_ref[...]
    for at in tiles_of(own_ref.shape[1]):
        own_ref[:, at] = dot(x_cols, w_in_ref[:, at], 1, 0)


def far_grad_body(dy_ref, w_out_ref, after_ref, sent_ref):
    dy_cols = dy_ref[...]
    for at, there in half_tiles(sent_ref.shape[1], False, 1536):
        sent_ref[:, at] = dot_turned(dy_cols, w_out_ref[there, :]).astype(bf16)


def own_grad_body(dy_ref, w_out_ref, own_ref):
    dy_cols = dy_ref[...]
    for at, there in half_tiles(own_ref.shape[1], True, 1536):
        own_ref[:, at] = dot(dy_cols, w_out_ref[there, :], 1, 1)


def add_body(own_ref, got_ref, out_ref):
    count, half = own_ref.shape
    out_ref[:, :half] = (own_ref[...] + got_ref[...].astype(f32)).astype(bf16)
    out_ref[:, half:] = jnp.zeros((count, out_ref.shape[1] - half), bf16)


def add_pre_body(own_ref, got_ref, sums_ref, out_ref):
    count, half = own_ref.shape
    out_ref[:, :half] = (own_ref[...] + got_ref[...].astype(f32)).astype(bf16)
    sums = [sums_ref[:, at] for at in tiles_of(sums_ref.shape[1], 128)]
    sums = jnp.concatenate(sums, axis=0)
    high = sums.astype(bf16).astype(f32)
    rest = jnp.zeros((count - 2 * sums.shape[0], 128), f32)
    out_ref[:, half:] = jnp.concatenate([high, sums - high, rest], axis=0).astype(bf16)


def gelu_body(bias_ref, own_ref, other_ref, after_ref, slopes_ref, act_ref):
    half = act_ref.shape[1]
    bias = bias_ref[:, half_of(half, True)]
    tile = tile_of(half, 512)
    for i in range(half // tile):
        at = pl.ds(i * tile, tile)
        pre_act = own_ref[:, at].astype(f32) + other_ref[:, at].astype(f32)
        activated, slopes = gelu_parts(pre_act + bias[:, i * tile : (i + 1) * tile])
        slopes_ref[:, at] = slopes
        act_ref[:, at] = activated.astype(bf16)


def grad_pre_body(slopes_ref, own_ref, other_ref, after_ref, later_ref, grad_ref):
    half = pl.ds(0, grad_ref.shape[1])
    grad_act = own_ref[:, half].astype(f32) + other_ref[:, half].astype(f32)
    grad_ref[...] = (grad_act * slopes_ref[...]).astype(bf16)


def far_forward_body(far_ref, w_out_ref, terms_ref, out_ref):
    act = far_ref[...]
    part = half_of(act.shape[1], False)
    for at in tiles_of(out_ref.shape[1], 1536):
        out_ref[:, at] = terms_ref[:, at] + dot(act, w_out_ref[part, at], 1, 0)


def own_backward_body(grad_ref, turned_ref, out_ref):
    grad = grad_ref[...]
    for at in tiles_of(out_ref.shape[1]):
        out_ref[:, at] = dot(grad, turned_ref[:, at], 1, 0)


def blocks_body(rows, own_ref, far_ref, forward_ref, backward_ref, turned_ref, grad_ref, *out_refs):
    grad = far_ref[...]
    grad_ref[...] = ordered(lax.axis_index("kin"), own_ref[...], grad, 1)
    size = out_refs[0].shape[0]
    for at in tiles_of(forward_ref.shape[1]):
        backward = backward_ref[:, at] + dot(grad, turned_ref[:, at], 1, 0)
        terms = together(forward_ref[:, at], backward, rows).astype(bf16)
        for i, out_ref in enumerate(out_refs):
            out_ref[:, at] = terms[i * size : (i + 1) * size]


def outer_body(most, first_of, left_ref, right_ref, *refs):
    copies = start_outer(most, first_of, left_ref, right_ref, *refs[-3:])
    for copy in copies:
        copy.wait()


def start_outer(most, first_of, left_ref, right_ref, out_hbm, block_ref, sems):
    first = first_of(left_ref.shape[1])
    copies = []
    for i, at in enumerate(tiles_of(left_ref.shape[1], most)):
        left = left_ref[:, at].T
        for part in tiles_of(out_hbm.shape[1], 512):
            block_ref[at, part] = dot(left, right_ref[:, part], 1, 0).astype(bf16)
        there = pl.ds(pl.multiple_of(first + at.start, at.size), at.size)
        copies.append(
            pltpu.make_async_copy(block_ref.at[at, :], out_hbm.at[there, :], sems.at[i])
        )
        copies[-1].start()
    return copies


def own_forward_body(act_ref, dy_ref, w_out_ref, terms_ref, out_hbm, block_ref, sems):
    copies = start_outer(128, own_rows, act_ref, dy_ref, out_hbm, block_ref, sems)
    act = act_ref[...]
    part = half_of(act.shape[1], True)
    for at in tiles_of(terms_ref.shape[1]):
        terms_ref[:, at] = dot(act, w_out_ref[part, at], 1, 0)
    for copy in copies:
        copy.wait()


def own_forward(act, dy_cols, weight_out):
    count, half = act.shape
    hid, wide = weight_out.shape
    return pl.pallas_call(
        own_forward_body,
        out_shape=[pltpu.VMEM((count, wide), f32), like((hid, wide), bf16)],
        in_specs=[whole] * 3,
        out_specs=[whole, pl.BlockSpec(memory_space=pl.ANY)],
        scratch_shapes=[
            pltpu.VMEM((half, wide), bf16),
            pltpu.SemaphoreType.DMA((len(tiles_of(half, 128)),)),
        ],
        compiler_params=pltpu.CompilerParams(vmem_limit_bytes=16 * MIB),
        name="own_forward",
    )(kept(act), kept(dy_cols), kept(weight_out))


def outer(left, right, high, name, first_of, into=None, most=128):
    count, size = left.shape
    wide = right.shape[1]
    anywhere = pl.BlockSpec(memory_space=pl.ANY)
    return pl.pallas_call(
        functools.partial(outer_body, most, first_of),
        out_shape=like((high, wide), bf16),
        in_specs=[whole] * 2 + ([] if into is None else [anywhere]),
        out_specs=anywhere,
        scratch_shapes=[
            pltpu.VMEM((size, wide), bf16),
            pltpu.SemaphoreType.DMA((len(tiles_of(size, most)),)),
        ],
        input_output_aliases={} if into is None else {2: 0},
        compiler_params=pltpu.CompilerParams(vmem_limit_bytes=16 * MIB),
        name=name,
    )(kept(left), kept(right), *([] if into is None else [into]))


def sum_body(rows, bias_ref, *refs):
    *term_refs, after_ref, own_ref, sent_ref = refs
    wide = own_ref.shape[1]
    me = lax.axis_index("tok")
    summed = sum(ref[...].astype(f32) for ref in term_refs)
    bias = jnp.where(me == 0, bias_ref[:, :wide], bias_ref[:, wide:])
    row = lax.broadcasted_iota(jnp.int32, summed.shape, 0)
    summed = summed + jnp.where(lax.rem(row, 2 * rows) < rows, bias, 0.0)
    low, high = summed[: 2 * rows], summed[2 * rows :]
    own_ref[...] = jnp.where(me == 0, low, high).astype(bf16)
    sent_ref[...] = jnp.where(me == 0, high, low).astype(bf16)


def final_body(
    rows, own_ref, got_ref, sums_ref, other_ref, hidden_ref, rows_ref, grad_ref, out_sums_ref, bias_ref
):
    wide = own_ref.shape[1]
    me = lax.axis_index("tok")
    own, got = own_ref[...].astype(f32), got_ref[...].astype(f32)
    extra = other_ref[:, other_ref.shape[1] - 128 :].astype(f32)
    steps = wide // 128
    got_sums = extra[:steps] + extra[steps : 2 * steps]
    got_sums = jnp.concatenate([got_sums[i : i + 1] for i in range(steps)], axis=1)
    for i in range(2):
        at = pl.ds(i * wide, wide)
        part = jnp.where(me == i, own, got)
        rows_ref[:, at] = part[:rows].astype(bf16)
        grad_ref[:, at] = part[rows:].astype(bf16)
        out_sums_ref[:, at] = jnp.where(me == i, sums_ref[...], got_sums)
    bias_ref[...] = jnp.sum(hidden_ref[...].astype(f32), axis=0, keepdims=True)


def make_small(nn):
    def across(array, shift):
        return lax.ppermute(array, "nout", [(i, i ^ shift) for i in range(nn)])

    def on_device(tokens, weight_in, bias_in, weight_out, bias_out, grad_out):
        rows, cols = tokens.shape
        wide, hid = weight_in.shape
        half = hid // 2
        pair = 2 * rows
        count = 2 * nn * rows
        sem = pltpu.SemaphoreType.DMA

        mine = jnp.concatenate([tokens, grad_out], axis=0)
        me = lax.axis_index("tok")
        own = lax.dynamic_slice_in_dim(mine, me * wide, wide, 1)
        sent = lax.dynamic_slice_in_dim(mine, (1 - me) * wide, wide, 1)
        got = lax.ppermute(sent, "tok", swap)

        last = tile_of(half, 512)
        (in_far,) = call(
            load_body,
            "load_far",
            [like((wide, half - last), bf16)],
            grant=MIB,
            scratch=[sem((4,))],
            specs=[hbm, pl.BlockSpec(memory_space=pl.ANY)],
        )(in_hbm(weight_in), sent)
        tiles, farthest = call(
            pair_body, "pair_tiles", [like((2 * pair, wide + more), bf16) for more in (0, 128)]
        )(
            kept(own), kept(got), kept(in_far)
        )
        pieces = [across(tiles, shift) for shift in range(1, nn - 1)]
        pieces = [across(farthest, nn - 1)] + pieces[::-1] + [tiles]
        in_own, in_last, own_turned, far_turned = call(
            load_and_turn_body,
            "load_own",
            [like((wide, half), bf16), like((wide, last), bf16)] + [like((half, wide), bf16)] * 2,
            grant=8 * MIB,
            scratch=[sem((2, 4))],
            specs=[hbm, pl.BlockSpec(memory_space=pl.ANY), whole],
        )(in_hbm(weight_in), tiles, kept(in_far))

        def product(body, name, outs, *args):
            return call(body, name, outs, grant=8 * MIB)(*map(kept, args))

        crossing = like((count, half + 128), bf16)
        side, ends = like((count, half), bf16), like((count, wide), f32)
        sent, x_cols, dy_cols, sums = product(
            functools.partial(far_pre_body, rows, nn),
            "far_pre",
            [side] + [like((count, wide), bf16)] * 2 + [like((1, wide), f32)],
            *pieces,
            in_far,
            in_last,
            in_own,
        )
        got = lax.ppermute(sent, "kin", swap)
        (own,) = product(own_pre_body, "own_pre", [like((count, half), f32)], x_cols, in_own, sent)
        (own_pre,) = product(add_pre_body, "add_pre", [crossing], own, got, sums)
        other_pre = lax.ppermute(own_pre, "tok", swap)
        (sent,) = product(far_grad_body, "far_grad", [side], dy_cols, weight_out, own_pre)
        got = lax.ppermute(sent, "kin", swap)
        (own,) = product(own_grad_body, "own_grad", [like((count, half), f32)], dy_cols, weight_out)
        (own_grad,) = product(add_body, "add_grad", [crossing], own, got)
        other_grad = lax.ppermute(own_grad, "tok", swap)
        slopes, act_own = call(gelu_body, "gelu", [like((count, half), f32), side])(
            bias_in.reshape(1, hid), kept(own_pre), kept(other_pre), kept(own_grad)
        )
        act_far = lax.ppermute(act_own, "kin", swap)
        forward, weight_out_grad = own_forward(act_own, dy_cols, weight_out)
        (forward,) = product(
            far_forward_body, "far_forward", [ends], act_far, weight_out, forward
        )
        (grad_own,) = call(
            grad_pre_body, "grad_pre", [side], specs=[whole] * 4 + [hbm]
        )(
            kept(slopes),
            kept(own_grad),
            kept(other_grad),
            kept(forward),
            in_hbm(weight_out_grad),
        )
        grad_far = lax.ppermute(grad_own, "kin", swap)
        (backward,) = product(own_backward_body, "own_backward", [ends], grad_own, own_turned)
        grad, *blocks = product(
            functools.partial(blocks_body, rows),
            "output_blocks",
            [like((count, hid), bf16)] + [like((2 * pair, wide), bf16)] * nn,
            grad_own,
            grad_far,
            forward,
            backward,
            far_turned,
        )

        weight_in_grad = outer(x_cols, grad, wide, "weight_in_grad", lambda size: 0)
        weight_out_grad = outer(
            act_far, dy_cols, hid, "weight_out_grad_far", far_rows, into=weight_out_grad
        )

        terms = [across(blocks[i], nn - 1 - i) for i in range(nn - 1)] + [blocks[-1]]
        own, sent = call(
            functools.partial(sum_body, rows),
            "sum_blocks",
            [like((pair, wide), bf16)] * 2,
            specs=[whole] * (nn + 1) + [hbm],
        )(
            bias_out.reshape(1, cols),
            *[kept(term) for term in terms],
            in_hbm(weight_in_grad),
        )
        got = lax.ppermute(sent, "tok", swap)
        output_rows, grad_tokens, bias_out_grad, bias_in_grad = call(
            functools.partial(final_body, rows),
            "final_rows",
            [like((rows, cols), bf16)] * 2 + [like((1, cols), f32), like((1, hid), f32)],
            resident=False,
        )(kept(own), kept(got), kept(sums), kept(other_pre), kept(grad))
        return (
            output_rows,
            grad_tokens,
            weight_in_grad,
            weight_out_grad,
            bias_in_grad.reshape(hid),
            bias_out_grad.reshape(cols),
        )

    return on_device


def make_plain(nt, nk, nn):
    spread, square = nt * nn, nk * nt

    def on_device(tokens, weight_in, bias_in, weight_out, bias_out, grad_out):
        rows, cols = tokens.shape
        wide, hid = weight_in.shape
        part = hid // square
        pair = 2 * rows
        total = pair * spread

        mine = jnp.concatenate([tokens, grad_out], axis=0)
        by_owner = mine.reshape(pair, nt, wide).transpose(1, 0, 2)
        chunks = jnp.broadcast_to(by_owner[:, None], (nt, nn, pair, wide))
        mixed = exchange(chunks.reshape(spread, pair, wide), ("tok", "nout")).reshape(total, wide)
        is_fwd = (lax.broadcasted_iota(jnp.int32, (total, 1), 0) % pair) < rows

        col_sums = jnp.sum(jnp.where(is_fwd, 0.0, mixed.astype(jnp.float32)), axis=0)
        bias_out_grad = lax.all_gather(col_sums, "tok", axis=0, tiled=True)

        partial = jnp.where(is_fwd, dot(mixed, weight_in, 1, 0), dot(mixed, weight_out, 1, 1))
        partial = partial.astype(jnp.bfloat16).reshape(total, square, part).transpose(1, 0, 2)
        got = exchange(partial, ("kin", "tok"))
        summed = jnp.sum(got.astype(jnp.float32), axis=0).reshape(spread, 2, rows, part)
        at = lax.axis_index(("kin", "tok"))
        pre_act = summed[:, 0] + lax.dynamic_slice_in_dim(bias_in, at * part, part)
        activated, slopes = gelu_parts(pre_act)
        grad_pre = summed[:, 1] * slopes
        both = jnp.stack([activated, grad_pre], axis=1).astype(jnp.bfloat16).reshape(total, part)
        both = exchange(jnp.broadcast_to(both[None], (square, total, part)), ("kin", "tok"))
        both = both.transpose(1, 0, 2).reshape(total, hid)

        split = both.reshape(spread, 2, rows, hid)
        act = split[:, 0].reshape(spread * rows, hid)
        grad_half = split[:, 1].reshape(spread * rows, hid)
        split = mixed.reshape(spread, 2, rows, wide)
        x_cols = split[:, 0].reshape(spread * rows, wide)
        dy_cols = split[:, 1].reshape(spread * rows, wide)
        bias_in_grad = jnp.sum(grad_half.astype(jnp.float32), axis=0)

        block = jnp.stack(
            [
                dot(act, weight_out, 1, 0).reshape(spread, rows, wide),
                dot(grad_half, weight_in, 1, 1).reshape(spread, rows, wide),
            ],
            axis=1,
        )
        block = block.astype(jnp.bfloat16).reshape(spread, pair, wide)
        back = exchange(block, ("tok", "nout")).reshape(nt, nn, pair, wide)
        weight_in_grad = dot(x_cols, grad_half, 0, 0).astype(jnp.bfloat16)
        weight_out_grad = dot(act, dy_cols, 0, 0).astype(jnp.bfloat16)
        final = jnp.sum(back.astype(jnp.float32), axis=1).transpose(1, 0, 2).reshape(pair, cols)
        output_rows = (final[:rows] + bias_out).astype(jnp.bfloat16)
        grad_tokens = final[rows:].astype(jnp.bfloat16)
        return (output_rows, grad_tokens, weight_in_grad, weight_out_grad, bias_in_grad, bias_out_grad)

    return on_device


def solution(mesh):
    nt, nk, nn = mesh.shape["tok"], mesh.shape["kin"], mesh.shape["nout"]
    return jax.shard_map(
        make_small(nn) if (nt, nk) == (2, 2) and nn in (2, 4) else make_plain(nt, nk, nn),
        mesh=mesh,
        in_specs=(
            P(("groups", "tok", "nout"), "kin"),
            P(("kin", "tok"), "nout"),
            P("nout"),
            P("nout", ("kin", "tok")),
            P("kin"),
            P(("groups", "tok", "nout"), "kin"),
        ),
        out_specs=(
            P(("groups", "tok", "nout"), "kin"),
            P(("groups", "tok", "nout"), "kin"),
            P(("groups", "kin", "tok"), "nout"),
            P(("groups", "nout"), ("kin", "tok")),
            P(("groups", "nout")),
            P(("groups", "kin")),
        ),
        check_vma=False,
    )
```

```python
import functools

import jax
import jax.numpy as jnp
from jax import lax
from jax.experimental import pallas as pl
from jax.experimental.pallas import tpu as pltpu
from jax.sharding import PartitionSpec as P

inv_root_two = 0.7071067811865476
inv_root_two_pi = 0.3989422804014327

MIB = 1 << 20
bf16, f32 = jnp.bfloat16, jnp.float32
like = jax.ShapeDtypeStruct
whole = pl.BlockSpec(memory_space=pltpu.VMEM)
hbm = pl.BlockSpec(memory_space=pltpu.HBM)
swap = [(0, 1), (1, 0)]


def gelu_parts(hidden):
    normal_cdf = 0.5 * (1.0 + lax.erf(hidden * inv_root_two))
    density = jnp.exp(-0.5 * hidden * hidden) * inv_root_two_pi
    return (hidden * normal_cdf, normal_cdf + hidden * density)


def dot(left, right, left_dim, right_dim):
    return lax.dot_general(
        left, right, (((left_dim,), (right_dim,)), ((), ())), preferred_element_type=jnp.float32
    )


def exchange(chunks, axes):
    return lax.all_to_all(chunks, axes, split_axis=0, concat_axis=0, tiled=True)


def tile_of(size, most):
    return max(t for t in range(128, most + 1, 128) if size % t == 0)


def tiles_of(size, most=512):
    tile = tile_of(size, most)
    return [pl.ds(i * tile, tile) for i in range(size // tile)]


def call(body, name, outs, grant=4 * MIB, flops=0, moved=0, scratch=(), resident=True, specs=None):
    shapes = [pltpu.VMEM(o.shape, o.dtype) if resident else o for o in outs]

    def run(*args):
        cost = pl.CostEstimate(flops=flops, bytes_accessed=moved, transcendentals=0)
        return pl.pallas_call(
            body,
            out_shape=shapes,
            in_specs=specs or [whole] * len(args),
            out_specs=[whole] * len(outs),
            scratch_shapes=list(scratch),
            cost_estimate=cost,
            compiler_params=pltpu.CompilerParams(vmem_limit_bytes=grant),
            name=name,
        )(*args)

    return run


def kept(array):
    return pltpu.with_memory_space_constraint(array, pltpu.VMEM)


def in_hbm(array):
    return pltpu.with_memory_space_constraint(array, pltpu.HBM)


def apart(mixed, rows):
    total, wide = mixed.shape
    tiles = mixed.reshape(total // (4 * rows), 2, 2 * rows, wide)
    even, odd = tiles[:, 0], tiles[:, 1]
    is_low = lax.broadcasted_iota(jnp.int32, even.shape, 1) < rows
    first = jnp.where(is_low, even, pltpu.roll(odd, rows, 1))
    second = jnp.where(is_low, pltpu.roll(even, rows, 1), odd)
    return first.reshape(total // 2, wide), second.reshape(total // 2, wide)


def together(first, second, rows):
    total, wide = first.shape
    first = first.reshape(total // (2 * rows), 2 * rows, wide)
    second = second.reshape(total // (2 * rows), 2 * rows, wide)
    is_low = lax.broadcasted_iota(jnp.int32, first.shape, 1) < rows
    even = jnp.where(is_low, first, pltpu.roll(second, rows, 1))
    odd = jnp.where(is_low, pltpu.roll(first, rows, 1), second)
    return jnp.stack([even, odd], axis=1).reshape(2 * total, wide)


def ordered(me, own, far, axis=0):
    low, high = jnp.where(me == 0, own, far), jnp.where(me == 0, far, own)
    return jnp.concatenate([low, high], axis=axis)


def half_of(size, mine):
    core = lax.axis_index("kin")
    at = core if mine else 1 - core
    return pl.ds(pl.multiple_of(at * size, size), size)


def own_rows(half):
    return lax.axis_index("kin") * half


def far_rows(half):
    return (1 - lax.axis_index("kin")) * half


def half_tiles(half, mine):
    first = own_rows(half) if mine else far_rows(half)
    tile = tile_of(half, 512)
    return [
        (pl.ds(i * tile, tile), pl.ds(pl.multiple_of(first + i * tile, tile), tile))
        for i in range(half // tile)
    ]


def load_body(hbm_ref, after_ref, out_ref, sems):
    size, wide = out_ref.shape
    half = hbm_ref.shape[1] // 2
    source = pl.ds(pl.multiple_of(far_rows(half), 128), wide)
    copies = []
    for j in range(4):
        part = pl.ds(j * (size // 4), size // 4)
        copies.append(
            pltpu.make_async_copy(hbm_ref.at[part, source], out_ref.at[part, :], sems.at[j])
        )
    for copy in copies:
        copy.start()
    for copy in copies:
        copy.wait()


def load_and_turn_body(hbm_ref, after_ref, far_ref, w_out_ref, *refs):
    own_ref, last_ref, own_turned, far_turned, sems = refs
    wide, half = own_ref.shape
    first, last = far_ref.shape[1], last_ref.shape[1]
    size = wide // 4
    parts = [pl.ds(j * size, size) for j in range(4)]
    from_own = pl.ds(pl.multiple_of(own_rows(half), 128), half)
    from_last = pl.ds(pl.multiple_of(far_rows(half) + first, 128), last)
    copies = [
        [
            pltpu.make_async_copy(hbm_ref.at[part, source], ref.at[part, :], sems.at[i, j])
            for j, part in enumerate(parts)
        ]
        for i, (source, ref) in enumerate(((from_own, own_ref), (from_last, last_ref)))
    ]
    for copy in copies[0] + copies[1]:
        copy.start()
    for part in parts:
        far_turned[:first, part] = far_ref[part, :].T
    for part, copy in zip(parts, copies[0]):
        copy.wait()
        own_turned[:, part] = own_ref[part, :].T
    for part, copy in zip(parts, copies[1]):
        copy.wait()
        far_turned[first:, part] = last_ref[part, :].T


def pair_body(own_ref, got_ref, after_ref, *out_refs):
    tiles = ordered(lax.axis_index("tok"), own_ref[...], got_ref[...])
    count, wide = tiles.shape
    for out_ref in out_refs:
        out_ref[:, :wide] = tiles
        if out_ref.shape[1] > wide:
            out_ref[:, wide:] = jnp.zeros((count, out_ref.shape[1] - wide), bf16)


def far_pre_body(rows, count, *refs):
    *piece_refs, w_in_ref, w_last_ref, after_ref = refs[: count + 3]
    sent_ref, x_ref, dy_ref, sums_ref = refs[count + 3 :]
    wide = x_ref.shape[1]
    mixed = jnp.concatenate([ref[:, :wide] for ref in piece_refs], axis=0)
    x_cols, dy_cols = apart(mixed.astype(f32), rows)
    sums_ref[...] = jnp.sum(dy_cols, axis=0, keepdims=True)
    x_cols, dy_cols = x_cols.astype(bf16), dy_cols.astype(bf16)
    x_ref[...], dy_ref[...] = x_cols, dy_cols
    first = w_in_ref.shape[1]
    for at in tiles_of(first):
        sent_ref[:, at] = dot(x_cols, w_in_ref[:, at], 1, 0).astype(bf16)
    sent_ref[:, first:] = dot(x_cols, w_last_ref[...], 1, 0).astype(bf16)


def own_pre_body(x_ref, w_in_ref, dy_ref, w_out_ref, after_ref, own_ref, first_ref):
    x_cols = x_ref[...]
    for at in tiles_of(own_ref.shape[1]):
        own_ref[:, at] = dot(x_cols, w_in_ref[:, at], 1, 0)
    there = half_tiles(own_ref.shape[1], False)[0][1]
    first_ref[...] = dot(dy_ref[...], w_out_ref[there, :], 1, 1).astype(bf16)


def far_grad_body(dy_ref, w_out_ref, first_ref, after_ref, sent_ref):
    dy_cols = dy_ref[...]
    tiles = half_tiles(sent_ref.shape[1], False)
    sent_ref[:, tiles[0][0]] = first_ref[...]
    for at, there in tiles[1:]:
        sent_ref[:, at] = dot(dy_cols, w_out_ref[there, :], 1, 1).astype(bf16)


def own_grad_body(dy_ref, w_out_ref, own_ref):
    dy_cols = dy_ref[...]
    for at, there in half_tiles(own_ref.shape[1], True):
        own_ref[:, at] = dot(dy_cols, w_out_ref[there, :], 1, 1)


def add_body(own_ref, got_ref, out_ref):
    count, half = own_ref.shape
    out_ref[:, :half] = (own_ref[...] + got_ref[...].astype(f32)).astype(bf16)
    out_ref[:, half:] = jnp.zeros((count, out_ref.shape[1] - half), bf16)


def add_pre_body(own_ref, got_ref, sums_ref, out_ref):
    count, half = own_ref.shape
    out_ref[:, :half] = (own_ref[...] + got_ref[...].astype(f32)).astype(bf16)
    sums = [sums_ref[:, at] for at in tiles_of(sums_ref.shape[1], 128)]
    sums = jnp.concatenate(sums, axis=0)
    high = sums.astype(bf16).astype(f32)
    rest = jnp.zeros((count - 2 * sums.shape[0], 128), f32)
    out_ref[:, half:] = jnp.concatenate([high, sums - high, rest], axis=0).astype(bf16)


def gelu_body(bias_ref, own_ref, other_ref, after_ref, slopes_ref, act_ref):
    half = act_ref.shape[1]
    bias = bias_ref[:, half_of(half, True)]
    tile = tile_of(half, 512)
    for i in range(half // tile):
        at = pl.ds(i * tile, tile)
        pre_act = own_ref[:, at].astype(f32) + other_ref[:, at].astype(f32)
        activated, slopes = gelu_parts(pre_act + bias[:, i * tile : (i + 1) * tile])
        slopes_ref[:, at] = slopes
        act_ref[:, at] = activated.astype(bf16)


def grad_pre_body(slopes_ref, own_ref, other_ref, after_ref, later_ref, grad_ref):
    half = pl.ds(0, grad_ref.shape[1])
    grad_act = own_ref[:, half].astype(f32) + other_ref[:, half].astype(f32)
    grad_ref[...] = (grad_act * slopes_ref[...]).astype(bf16)


def far_forward_body(far_ref, w_out_ref, terms_ref, out_ref):
    act = far_ref[...]
    part = half_of(act.shape[1], False)
    for at in tiles_of(out_ref.shape[1]):
        out_ref[:, at] = terms_ref[:, at] + dot(act, w_out_ref[part, at], 1, 0)


def own_backward_body(grad_ref, turned_ref, out_ref):
    grad = grad_ref[...]
    for at in tiles_of(out_ref.shape[1]):
        out_ref[:, at] = dot(grad, turned_ref[:, at], 1, 0)


def blocks_body(rows, own_ref, far_ref, forward_ref, backward_ref, turned_ref, grad_ref, *out_refs):
    grad = far_ref[...]
    grad_ref[...] = ordered(lax.axis_index("kin"), own_ref[...], grad, 1)
    size = out_refs[0].shape[0]
    for at in tiles_of(forward_ref.shape[1]):
        backward = backward_ref[:, at] + dot(grad, turned_ref[:, at], 1, 0)
        terms = together(forward_ref[:, at], backward, rows).astype(bf16)
        for i, out_ref in enumerate(out_refs):
            out_ref[:, at] = terms[i * size : (i + 1) * size]


def outer_body(most, first_of, left_ref, right_ref, *refs):
    copies = start_outer(most, first_of, left_ref, right_ref, *refs[-3:])
    for copy in copies:
        copy.wait()


def start_outer(most, first_of, left_ref, right_ref, out_hbm, block_ref, sems):
    first = first_of(left_ref.shape[1])
    copies = []
    for i, at in enumerate(tiles_of(left_ref.shape[1], most)):
        left = left_ref[:, at].T
        for part in tiles_of(out_hbm.shape[1], 512):
            block_ref[at, part] = dot(left, right_ref[:, part], 1, 0).astype(bf16)
        there = pl.ds(pl.multiple_of(first + at.start, at.size), at.size)
        copies.append(
            pltpu.make_async_copy(block_ref.at[at, :], out_hbm.at[there, :], sems.at[i])
        )
        copies[-1].start()
    return copies


def own_forward_body(act_ref, dy_ref, w_out_ref, terms_ref, out_hbm, block_ref, sems):
    copies = start_outer(128, own_rows, act_ref, dy_ref, out_hbm, block_ref, sems)
    act = act_ref[...]
    part = half_of(act.shape[1], True)
    for at in tiles_of(terms_ref.shape[1]):
        terms_ref[:, at] = dot(act, w_out_ref[part, at], 1, 0)
    for copy in copies:
        copy.wait()


def own_forward(act, dy_cols, weight_out):
    count, half = act.shape
    hid, wide = weight_out.shape
    return pl.pallas_call(
        own_forward_body,
        out_shape=[pltpu.VMEM((count, wide), f32), like((hid, wide), bf16)],
        in_specs=[whole] * 3,
        out_specs=[whole, pl.BlockSpec(memory_space=pl.ANY)],
        scratch_shapes=[
            pltpu.VMEM((half, wide), bf16),
            pltpu.SemaphoreType.DMA((len(tiles_of(half, 128)),)),
        ],
        compiler_params=pltpu.CompilerParams(vmem_limit_bytes=16 * MIB),
        name="own_forward",
    )(kept(act), kept(dy_cols), kept(weight_out))


def outer(left, right, high, name, first_of, into=None, most=128):
    count, size = left.shape
    wide = right.shape[1]
    anywhere = pl.BlockSpec(memory_space=pl.ANY)
    return pl.pallas_call(
        functools.partial(outer_body, most, first_of),
        out_shape=like((high, wide), bf16),
        in_specs=[whole] * 2 + ([] if into is None else [anywhere]),
        out_specs=anywhere,
        scratch_shapes=[
            pltpu.VMEM((size, wide), bf16),
            pltpu.SemaphoreType.DMA((len(tiles_of(size, most)),)),
        ],
        input_output_aliases={} if into is None else {2: 0},
        compiler_params=pltpu.CompilerParams(vmem_limit_bytes=16 * MIB),
        name=name,
    )(kept(left), kept(right), *([] if into is None else [into]))


def sum_body(rows, bias_ref, *refs):
    *term_refs, after_ref, own_ref, sent_ref = refs
    wide = own_ref.shape[1]
    me = lax.axis_index("tok")
    summed = sum(ref[...].astype(f32) for ref in term_refs)
    bias = jnp.where(me == 0, bias_ref[:, :wide], bias_ref[:, wide:])
    row = lax.broadcasted_iota(jnp.int32, summed.shape, 0)
    summed = summed + jnp.where(lax.rem(row, 2 * rows) < rows, bias, 0.0)
    low, high = summed[: 2 * rows], summed[2 * rows :]
    own_ref[...] = jnp.where(me == 0, low, high).astype(bf16)
    sent_ref[...] = jnp.where(me == 0, high, low).astype(bf16)


def final_body(
    rows, own_ref, got_ref, sums_ref, other_ref, hidden_ref, rows_ref, grad_ref, out_sums_ref, bias_ref
):
    wide = own_ref.shape[1]
    me = lax.axis_index("tok")
    own, got = own_ref[...].astype(f32), got_ref[...].astype(f32)
    extra = other_ref[:, other_ref.shape[1] - 128 :].astype(f32)
    steps = wide // 128
    got_sums = extra[:steps] + extra[steps : 2 * steps]
    got_sums = jnp.concatenate([got_sums[i : i + 1] for i in range(steps)], axis=1)
    for i in range(2):
        at = pl.ds(i * wide, wide)
        part = jnp.where(me == i, own, got)
        rows_ref[:, at] = part[:rows].astype(bf16)
        grad_ref[:, at] = part[rows:].astype(bf16)
        out_sums_ref[:, at] = jnp.where(me == i, sums_ref[...], got_sums)
    bias_ref[...] = jnp.sum(hidden_ref[...].astype(f32), axis=0, keepdims=True)


def make_small(nn):
    def across(array, shift):
        return lax.ppermute(array, "nout", [(i, i ^ shift) for i in range(nn)])

    def on_device(tokens, weight_in, bias_in, weight_out, bias_out, grad_out):
        rows, cols = tokens.shape
        wide, hid = weight_in.shape
        half = hid // 2
        pair = 2 * rows
        count = 2 * nn * rows
        sem = pltpu.SemaphoreType.DMA

        mine = jnp.concatenate([tokens, grad_out], axis=0)
        me = lax.axis_index("tok")
        own = lax.dynamic_slice_in_dim(mine, me * wide, wide, 1)
        sent = lax.dynamic_slice_in_dim(mine, (1 - me) * wide, wide, 1)
        got = lax.ppermute(sent, "tok", swap)

        last = tile_of(half, 512)
        (in_far,) = call(
            load_body,
            "load_far",
            [like((wide, half - last), bf16)],
            grant=MIB,
            scratch=[sem((4,))],
            specs=[hbm, pl.BlockSpec(memory_space=pl.ANY)],
        )(in_hbm(weight_in), sent)
        tiles, farthest = call(
            pair_body, "pair_tiles", [like((2 * pair, wide + more), bf16) for more in (0, 128)]
        )(
            kept(own), kept(got), kept(in_far)
        )
        pieces = [across(tiles, shift) for shift in range(1, nn - 1)]
        pieces = [across(farthest, nn - 1)] + pieces + [tiles]
        in_own, in_last, own_turned, far_turned = call(
            load_and_turn_body,
            "load_own",
            [like((wide, half), bf16), like((wide, last), bf16)] + [like((half, wide), bf16)] * 2,
            grant=8 * MIB,
            scratch=[sem((2, 4))],
            specs=[hbm, pl.BlockSpec(memory_space=pl.ANY), whole, whole],
        )(in_hbm(weight_in), tiles, kept(in_far), kept(weight_out))

        def product(body, name, outs, *args):
            return call(body, name, outs, grant=8 * MIB)(*map(kept, args))

        crossing = like((count, half + 128), bf16)
        side, ends = like((count, half), bf16), like((count, wide), f32)
        sent, x_cols, dy_cols, sums = product(
            functools.partial(far_pre_body, rows, nn),
            "far_pre",
            [side] + [like((count, wide), bf16)] * 2 + [like((1, wide), f32)],
            *pieces,
            in_far,
            in_last,
            in_own,
        )
        got = lax.ppermute(sent, "kin", swap)
        own, first = product(
            own_pre_body,
            "own_pre",
            [like((count, half), f32), like((count, tile_of(half, 512)), bf16)],
            x_cols,
            in_own,
            dy_cols,
            weight_out,
            sent,
        )
        (own_pre,) = product(add_pre_body, "add_pre", [crossing], own, got, sums)
        other_pre = lax.ppermute(own_pre, "tok", swap)
        (sent,) = product(
            far_grad_body, "far_grad", [side], dy_cols, weight_out, first, own_pre
        )
        got = lax.ppermute(sent, "kin", swap)
        (own,) = product(own_grad_body, "own_grad", [like((count, half), f32)], dy_cols, weight_out)
        (own_grad,) = product(add_body, "add_grad", [crossing], own, got)
        other_grad = lax.ppermute(own_grad, "tok", swap)
        slopes, act_own = call(gelu_body, "gelu", [like((count, half), f32), side])(
            bias_in.reshape(1, hid), kept(own_pre), kept(other_pre), kept(own_grad)
        )
        act_far = lax.ppermute(act_own, "kin", swap)
        forward, weight_out_grad = own_forward(act_own, dy_cols, weight_out)
        (forward,) = product(
            far_forward_body, "far_forward", [ends], act_far, weight_out, forward
        )
        (grad_own,) = call(
            grad_pre_body, "grad_pre", [side], specs=[whole] * 4 + [hbm]
        )(
            kept(slopes),
            kept(own_grad),
            kept(other_grad),
            kept(forward),
            in_hbm(weight_out_grad),
        )
        grad_far = lax.ppermute(grad_own, "kin", swap)
        (backward,) = product(own_backward_body, "own_backward", [ends], grad_own, own_turned)
        grad, *blocks = product(
            functools.partial(blocks_body, rows),
            "output_blocks",
            [like((count, hid), bf16)] + [like((2 * pair, wide), bf16)] * nn,
            grad_own,
            grad_far,
            forward,
            backward,
            far_turned,
        )

        weight_in_grad = outer(x_cols, grad, wide, "weight_in_grad", lambda size: 0)
        weight_out_grad = outer(
            act_far, dy_cols, hid, "weight_out_grad_far", far_rows, into=weight_out_grad
        )

        terms = [across(blocks[0], nn - 1)]
        terms += [across(blocks[shift], shift) for shift in reversed(range(1, nn - 1))] + [blocks[-1]]
        own, sent = call(
            functools.partial(sum_body, rows),
            "sum_blocks",
            [like((pair, wide), bf16)] * 2,
            specs=[whole] * (nn + 1) + [hbm],
        )(
            bias_out.reshape(1, cols),
            *[kept(term) for term in terms],
            in_hbm(weight_in_grad),
        )
        got = lax.ppermute(sent, "tok", swap)
        output_rows, grad_tokens, bias_out_grad, bias_in_grad = call(
            functools.partial(final_body, rows),
            "final_rows",
            [like((rows, cols), bf16)] * 2 + [like((1, cols), f32), like((1, hid), f32)],
            resident=False,
        )(kept(own), kept(got), kept(sums), kept(other_pre), kept(grad))
        return (
            output_rows,
            grad_tokens,
            weight_in_grad,
            weight_out_grad,
            bias_in_grad.reshape(hid),
            bias_out_grad.reshape(cols),
        )

    return on_device


def make_plain(nt, nk, nn):
    spread, square = nt * nn, nk * nt

    def on_device(tokens, weight_in, bias_in, weight_out, bias_out, grad_out):
        rows, cols = tokens.shape
        wide, hid = weight_in.shape
        part = hid // square
        pair = 2 * rows
        total = pair * spread

        mine = jnp.concatenate([tokens, grad_out], axis=0)
        by_owner = mine.reshape(pair, nt, wide).transpose(1, 0, 2)
        chunks = jnp.broadcast_to(by_owner[:, None], (nt, nn, pair, wide))
        mixed = exchange(chunks.reshape(spread, pair, wide), ("tok", "nout")).reshape(total, wide)
        is_fwd = (lax.broadcasted_iota(jnp.int32, (total, 1), 0) % pair) < rows

        col_sums = jnp.sum(jnp.where(is_fwd, 0.0, mixed.astype(jnp.float32)), axis=0)
        bias_out_grad = lax.all_gather(col_sums, "tok", axis=0, tiled=True)

        partial = jnp.where(is_fwd, dot(mixed, weight_in, 1, 0), dot(mixed, weight_out, 1, 1))
        partial = partial.astype(jnp.bfloat16).reshape(total, square, part).transpose(1, 0, 2)
        got = exchange(partial, ("kin", "tok"))
        summed = jnp.sum(got.astype(jnp.float32), axis=0).reshape(spread, 2, rows, part)
        at = lax.axis_index(("kin", "tok"))
        pre_act = summed[:, 0] + lax.dynamic_slice_in_dim(bias_in, at * part, part)
        activated, slopes = gelu_parts(pre_act)
        grad_pre = summed[:, 1] * slopes
        both = jnp.stack([activated, grad_pre], axis=1).astype(jnp.bfloat16).reshape(total, part)
        both = exchange(jnp.broadcast_to(both[None], (square, total, part)), ("kin", "tok"))
        both = both.transpose(1, 0, 2).reshape(total, hid)

        split = both.reshape(spread, 2, rows, hid)
        act = split[:, 0].reshape(spread * rows, hid)
        grad_half = split[:, 1].reshape(spread * rows, hid)
        split = mixed.reshape(spread, 2, rows, wide)
        x_cols = split[:, 0].reshape(spread * rows, wide)
        dy_cols = split[:, 1].reshape(spread * rows, wide)
        bias_in_grad = jnp.sum(grad_half.astype(jnp.float32), axis=0)

        block = jnp.stack(
            [
                dot(act, weight_out, 1, 0).reshape(spread, rows, wide),
                dot(grad_half, weight_in, 1, 1).reshape(spread, rows, wide),
            ],
            axis=1,
        )
        block = block.astype(jnp.bfloat16).reshape(spread, pair, wide)
        back = exchange(block, ("tok", "nout")).reshape(nt, nn, pair, wide)
        weight_in_grad = dot(x_cols, grad_half, 0, 0).astype(jnp.bfloat16)
        weight_out_grad = dot(act, dy_cols, 0, 0).astype(jnp.bfloat16)
        final = jnp.sum(back.astype(jnp.float32), axis=1).transpose(1, 0, 2).reshape(pair, cols)
        output_rows = (final[:rows] + bias_out).astype(jnp.bfloat16)
        grad_tokens = final[rows:].astype(jnp.bfloat16)
        return (output_rows, grad_tokens, weight_in_grad, weight_out_grad, bias_in_grad, bias_out_grad)

    return on_device


def solution(mesh):
    nt, nk, nn = mesh.shape["tok"], mesh.shape["kin"], mesh.shape["nout"]
    return jax.shard_map(
        make_small(nn) if (nt, nk) == (2, 2) and nn in (2, 4) else make_plain(nt, nk, nn),
        mesh=mesh,
        in_specs=(
            P(("groups", "tok", "nout"), "kin"),
            P(("kin", "tok"), "nout"),
            P("nout"),
            P("nout", ("kin", "tok")),
            P("kin"),
            P(("groups", "tok", "nout"), "kin"),
        ),
        out_specs=(
            P(("groups", "tok", "nout"), "kin"),
            P(("groups", "tok", "nout"), "kin"),
            P(("groups", "kin", "tok"), "nout"),
            P(("groups", "nout"), ("kin", "tok")),
            P(("groups", "nout")),
            P(("groups", "kin")),
        ),
        check_vma=False,
    )
```

```python
import functools

import jax
import jax.numpy as jnp
from jax import lax
from jax.experimental import pallas as pl
from jax.experimental.pallas import tpu as pltpu
from jax.sharding import PartitionSpec as P

inv_root_two = 0.7071067811865476
inv_root_two_pi = 0.3989422804014327

MIB = 1 << 20
bf16, f32 = jnp.bfloat16, jnp.float32
like = jax.ShapeDtypeStruct
whole = pl.BlockSpec(memory_space=pltpu.VMEM)
hbm = pl.BlockSpec(memory_space=pltpu.HBM)
swap = [(0, 1), (1, 0)]


def gelu_parts(hidden):
    normal_cdf = 0.5 * (1.0 + lax.erf(hidden * inv_root_two))
    density = jnp.exp(-0.5 * hidden * hidden) * inv_root_two_pi
    return (hidden * normal_cdf, normal_cdf + hidden * density)


def dot(left, right, left_dim, right_dim):
    return lax.dot_general(
        left, right, (((left_dim,), (right_dim,)), ((), ())), preferred_element_type=jnp.float32
    )


def exchange(chunks, axes):
    return lax.all_to_all(chunks, axes, split_axis=0, concat_axis=0, tiled=True)


def dot_turned(rows, weight):
    return dot(weight, rows, 1, 1).T


def tile_of(size, most):
    return max(t for t in range(128, most + 1, 128) if size % t == 0)


def tiles_of(size, most=512):
    tile = tile_of(size, most)
    return [pl.ds(i * tile, tile) for i in range(size // tile)]


def call(body, name, outs, grant=4 * MIB, flops=0, moved=0, scratch=(), resident=True, specs=None):
    shapes = [pltpu.VMEM(o.shape, o.dtype) if resident else o for o in outs]

    def run(*args):
        cost = pl.CostEstimate(flops=flops, bytes_accessed=moved, transcendentals=0)
        return pl.pallas_call(
            body,
            out_shape=shapes,
            in_specs=specs or [whole] * len(args),
            out_specs=[whole] * len(outs),
            scratch_shapes=list(scratch),
            cost_estimate=cost,
            compiler_params=pltpu.CompilerParams(vmem_limit_bytes=grant),
            name=name,
        )(*args)

    return run


def kept(array):
    return pltpu.with_memory_space_constraint(array, pltpu.VMEM)


def in_hbm(array):
    return pltpu.with_memory_space_constraint(array, pltpu.HBM)


def apart(mixed, rows):
    total, wide = mixed.shape
    tiles = mixed.reshape(total // (4 * rows), 2, 2 * rows, wide)
    even, odd = tiles[:, 0], tiles[:, 1]
    is_low = lax.broadcasted_iota(jnp.int32, even.shape, 1) < rows
    first = jnp.where(is_low, even, pltpu.roll(odd, rows, 1))
    second = jnp.where(is_low, pltpu.roll(even, rows, 1), odd)
    return first.reshape(total // 2, wide), second.reshape(total // 2, wide)


def together(first, second, rows):
    total, wide = first.shape
    first = first.reshape(total // (2 * rows), 2 * rows, wide)
    second = second.reshape(total // (2 * rows), 2 * rows, wide)
    is_low = lax.broadcasted_iota(jnp.int32, first.shape, 1) < rows
    even = jnp.where(is_low, first, pltpu.roll(second, rows, 1))
    odd = jnp.where(is_low, pltpu.roll(first, rows, 1), second)
    return jnp.stack([even, odd], axis=1).reshape(2 * total, wide)


def ordered(me, own, far, axis=0):
    low, high = jnp.where(me == 0, own, far), jnp.where(me == 0, far, own)
    return jnp.concatenate([low, high], axis=axis)


def half_of(size, mine):
    core = lax.axis_index("kin")
    at = core if mine else 1 - core
    return pl.ds(pl.multiple_of(at * size, size), size)


def own_rows(half):
    return lax.axis_index("kin") * half


def far_rows(half):
    return (1 - lax.axis_index("kin")) * half


def half_tiles(half, mine, most):
    first = own_rows(half) if mine else far_rows(half)
    tile = tile_of(half, most)
    return [
        (pl.ds(i * tile, tile), pl.ds(pl.multiple_of(first + i * tile, tile), tile))
        for i in range(half // tile)
    ]


def load_body(hbm_ref, after_ref, out_ref, sems):
    size, wide = out_ref.shape
    half = hbm_ref.shape[1] // 2
    source = pl.ds(pl.multiple_of(far_rows(half), 128), wide)
    copies = []
    for j in range(4):
        part = pl.ds(j * (size // 4), size // 4)
        copies.append(
            pltpu.make_async_copy(hbm_ref.at[part, source], out_ref.at[part, :], sems.at[j])
        )
    for copy in copies:
        copy.start()
    for copy in copies:
        copy.wait()


def load_and_turn_body(hbm_ref, after_ref, far_ref, own_ref, last_ref, own_turned, far_turned, sems):
    wide, half = own_ref.shape
    first, last = far_ref.shape[1], last_ref.shape[1]
    size = wide // 4
    parts = [pl.ds(j * size, size) for j in range(4)]
    from_own = pl.ds(pl.multiple_of(own_rows(half), 128), half)
    from_last = pl.ds(pl.multiple_of(far_rows(half) + first, 128), last)
    copies = [
        [
            pltpu.make_async_copy(hbm_ref.at[part, source], ref.at[part, :], sems.at[i, j])
            for j, part in enumerate(parts)
        ]
        for i, (source, ref) in enumerate(((from_own, own_ref), (from_last, last_ref)))
    ]
    for copy in copies[0] + copies[1]:
        copy.start()
    for part in parts:
        far_turned[:first, part] = far_ref[part, :].T
    for part, copy in zip(parts, copies[0]):
        copy.wait()
        own_turned[:, part] = own_ref[part, :].T
    for part, copy in zip(parts, copies[1]):
        copy.wait()
        far_turned[first:, part] = last_ref[part, :].T


def cut_body(tokens_hbm, grad_hbm, own_ref, sent_ref, tokens_ref, grad_ref, sems):
    me = lax.axis_index("tok")
    first = pltpu.make_async_copy(tokens_hbm, tokens_ref, sems.at[0])
    second = pltpu.make_async_copy(grad_hbm, grad_ref, sems.at[1])
    first.start()
    second.start()
    first.wait()
    second.wait()
    mine = jnp.concatenate([tokens_ref[...].astype(f32), grad_ref[...].astype(f32)], axis=0)
    wide = own_ref.shape[1]
    low, high = mine[:, :wide], mine[:, wide:]
    own_ref[...] = jnp.where(me == 0, low, high).astype(bf16)
    sent_ref[...] = jnp.where(me == 0, high, low).astype(bf16)


def pair_body(own_ref, got_ref, after_ref, *out_refs):
    tiles = ordered(lax.axis_index("tok"), own_ref[...], got_ref[...])
    count, wide = tiles.shape
    for out_ref in out_refs:
        out_ref[:, :wide] = tiles
        if out_ref.shape[1] > wide:
            out_ref[:, wide:] = jnp.zeros((count, out_ref.shape[1] - wide), bf16)


def far_pre_body(rows, count, *refs):
    *piece_refs, w_in_ref, w_last_ref, after_ref = refs[: count + 3]
    sent_ref, x_ref, dy_ref, sums_ref = refs[count + 3 :]
    wide = x_ref.shape[1]
    mixed = jnp.concatenate([ref[:, :wide] for ref in piece_refs], axis=0)
    x_cols, dy_cols = apart(mixed.astype(f32), rows)
    sums_ref[...] = jnp.sum(dy_cols, axis=0, keepdims=True)
    x_cols, dy_cols = x_cols.astype(bf16), dy_cols.astype(bf16)
    x_ref[...], dy_ref[...] = x_cols, dy_cols
    first = w_in_ref.shape[1]
    for at in tiles_of(first):
        sent_ref[:, at] = dot(x_cols, w_in_ref[:, at], 1, 0).astype(bf16)
    sent_ref[:, first:] = dot(x_cols, w_last_ref[...], 1, 0).astype(bf16)


def own_pre_body(x_ref, w_in_ref, after_ref, own_ref):
    x_cols = x_ref[...]
    for at in tiles_of(own_ref.shape[1]):
        own_ref[:, at] = dot(x_cols, w_in_ref[:, at], 1, 0)


def far_grad_body(dy_ref, w_out_ref, after_ref, sent_ref):
    dy_cols = dy_ref[...]
    for at, there in half_tiles(sent_ref.shape[1], False, 1536):
        sent_ref[:, at] = dot_turned(dy_cols, w_out_ref[there, :]).astype(bf16)


def own_grad_body(dy_ref, w_out_ref, own_ref):
    dy_cols = dy_ref[...]
    for at, there in half_tiles(own_ref.shape[1], True, 1536):
        own_ref[:, at] = dot(dy_cols, w_out_ref[there, :], 1, 1)


def add_body(own_ref, got_ref, out_ref):
    count, half = own_ref.shape
    out_ref[:, :half] = (own_ref[...] + got_ref[...].astype(f32)).astype(bf16)
    out_ref[:, half:] = jnp.zeros((count, out_ref.shape[1] - half), bf16)


def add_pre_body(own_ref, got_ref, sums_ref, out_ref):
    count, half = own_ref.shape
    out_ref[:, :half] = (own_ref[...] + got_ref[...].astype(f32)).astype(bf16)
    sums = [sums_ref[:, at] for at in tiles_of(sums_ref.shape[1], 128)]
    sums = jnp.concatenate(sums, axis=0)
    high = sums.astype(bf16).astype(f32)
    rest = jnp.zeros((count - 2 * sums.shape[0], 128), f32)
    out_ref[:, half:] = jnp.concatenate([high, sums - high, rest], axis=0).astype(bf16)


def gelu_body(bias_ref, own_ref, other_ref, after_ref, slopes_ref, act_ref):
    half = act_ref.shape[1]
    bias = bias_ref[:, half_of(half, True)]
    tile = tile_of(half, 512)
    for i in range(half // tile):
        at = pl.ds(i * tile, tile)
        pre_act = own_ref[:, at].astype(f32) + other_ref[:, at].astype(f32)
        activated, slopes = gelu_parts(pre_act + bias[:, i * tile : (i + 1) * tile])
        slopes_ref[:, at] = slopes
        act_ref[:, at] = activated.astype(bf16)


def grad_pre_body(slopes_ref, own_ref, other_ref, after_ref, later_ref, grad_ref):
    half = pl.ds(0, grad_ref.shape[1])
    grad_act = own_ref[:, half].astype(f32) + other_ref[:, half].astype(f32)
    grad_ref[...] = (grad_act * slopes_ref[...]).astype(bf16)


def far_forward_body(far_ref, w_out_ref, terms_ref, out_ref):
    act = far_ref[...]
    part = half_of(act.shape[1], False)
    for at in tiles_of(out_ref.shape[1], 1536):
        out_ref[:, at] = terms_ref[:, at] + dot(act, w_out_ref[part, at], 1, 0)


def own_backward_body(grad_ref, turned_ref, out_ref):
    grad = grad_ref[...]
    for at in tiles_of(out_ref.shape[1]):
        out_ref[:, at] = dot(grad, turned_ref[:, at], 1, 0)


def blocks_body(rows, own_ref, far_ref, forward_ref, backward_ref, turned_ref, grad_ref, *out_refs):
    grad = far_ref[...]
    grad_ref[...] = ordered(lax.axis_index("kin"), own_ref[...], grad, 1)
    size = out_refs[0].shape[0]
    for at in tiles_of(forward_ref.shape[1]):
        backward = backward_ref[:, at] + dot(grad, turned_ref[:, at], 1, 0)
        terms = together(forward_ref[:, at], backward, rows).astype(bf16)
        for i, out_ref in enumerate(out_refs):
            out_ref[:, at] = terms[i * size : (i + 1) * size]


def outer_body(most, first_of, left_ref, right_ref, *refs):
    copies = start_outer(most, first_of, left_ref, right_ref, *refs[-3:])
    for copy in copies:
        copy.wait()


def start_outer(most, first_of, left_ref, right_ref, out_hbm, block_ref, sems):
    first = first_of(left_ref.shape[1])
    copies = []
    for i, at in enumerate(tiles_of(left_ref.shape[1], most)):
        left = left_ref[:, at].T
        for part in tiles_of(out_hbm.shape[1], 512):
            block_ref[at, part] = dot(left, right_ref[:, part], 1, 0).astype(bf16)
        there = pl.ds(pl.multiple_of(first + at.start, at.size), at.size)
        copies.append(
            pltpu.make_async_copy(block_ref.at[at, :], out_hbm.at[there, :], sems.at[i])
        )
        copies[-1].start()
    return copies


def own_forward_body(act_ref, dy_ref, w_out_ref, terms_ref, out_hbm, block_ref, sems):
    copies = start_outer(128, own_rows, act_ref, dy_ref, out_hbm, block_ref, sems)
    act = act_ref[...]
    part = half_of(act.shape[1], True)
    for at in tiles_of(terms_ref.shape[1]):
        terms_ref[:, at] = dot(act, w_out_ref[part, at], 1, 0)
    for copy in copies:
        copy.wait()


def own_forward(act, dy_cols, weight_out):
    count, half = act.shape
    hid, wide = weight_out.shape
    return pl.pallas_call(
        own_forward_body,
        out_shape=[pltpu.VMEM((count, wide), f32), like((hid, wide), bf16)],
        in_specs=[whole] * 3,
        out_specs=[whole, pl.BlockSpec(memory_space=pl.ANY)],
        scratch_shapes=[
            pltpu.VMEM((half, wide), bf16),
            pltpu.SemaphoreType.DMA((len(tiles_of(half, 128)),)),
        ],
        compiler_params=pltpu.CompilerParams(vmem_limit_bytes=16 * MIB),
        name="own_forward",
    )(kept(act), kept(dy_cols), kept(weight_out))


def outer(left, right, high, name, first_of, into=None, most=128):
    count, size = left.shape
    wide = right.shape[1]
    anywhere = pl.BlockSpec(memory_space=pl.ANY)
    return pl.pallas_call(
        functools.partial(outer_body, most, first_of),
        out_shape=like((high, wide), bf16),
        in_specs=[whole] * 2 + ([] if into is None else [anywhere]),
        out_specs=anywhere,
        scratch_shapes=[
            pltpu.VMEM((size, wide), bf16),
            pltpu.SemaphoreType.DMA((len(tiles_of(size, most)),)),
        ],
        input_output_aliases={} if into is None else {2: 0},
        compiler_params=pltpu.CompilerParams(vmem_limit_bytes=16 * MIB),
        name=name,
    )(kept(left), kept(right), *([] if into is None else [into]))


def sum_body(rows, bias_ref, *refs):
    *term_refs, after_ref, own_ref, sent_ref = refs
    wide = own_ref.shape[1]
    me = lax.axis_index("tok")
    summed = sum(ref[...].astype(f32) for ref in term_refs)
    bias = jnp.where(me == 0, bias_ref[:, :wide], bias_ref[:, wide:])
    row = lax.broadcasted_iota(jnp.int32, summed.shape, 0)
    summed = summed + jnp.where(lax.rem(row, 2 * rows) < rows, bias, 0.0)
    low, high = summed[: 2 * rows], summed[2 * rows :]
    own_ref[...] = jnp.where(me == 0, low, high).astype(bf16)
    sent_ref[...] = jnp.where(me == 0, high, low).astype(bf16)


def final_body(
    rows, own_ref, got_ref, sums_ref, other_ref, hidden_ref, rows_ref, grad_ref, out_sums_ref, bias_ref
):
    wide = own_ref.shape[1]
    me = lax.axis_index("tok")
    own, got = own_ref[...].astype(f32), got_ref[...].astype(f32)
    extra = other_ref[:, other_ref.shape[1] - 128 :].astype(f32)
    steps = wide // 128
    got_sums = extra[:steps] + extra[steps : 2 * steps]
    got_sums = jnp.concatenate([got_sums[i : i + 1] for i in range(steps)], axis=1)
    for i in range(2):
        at = pl.ds(i * wide, wide)
        part = jnp.where(me == i, own, got)
        rows_ref[:, at] = part[:rows].astype(bf16)
        grad_ref[:, at] = part[rows:].astype(bf16)
        out_sums_ref[:, at] = jnp.where(me == i, sums_ref[...], got_sums)
    bias_ref[...] = jnp.sum(hidden_ref[...].astype(f32), axis=0, keepdims=True)


def make_small(nn):
    def across(array, shift):
        return lax.ppermute(array, "nout", [(i, i ^ shift) for i in range(nn)])

    def on_device(tokens, weight_in, bias_in, weight_out, bias_out, grad_out):
        rows, cols = tokens.shape
        wide, hid = weight_in.shape
        half = hid // 2
        pair = 2 * rows
        count = 2 * nn * rows
        sem = pltpu.SemaphoreType.DMA

        own, sent = call(
            cut_body,
            "cut_tiles",
            [like((pair, wide), bf16)] * 2,
            scratch=[pltpu.VMEM((rows, cols), bf16)] * 2 + [pltpu.SemaphoreType.DMA((2,))],
            specs=[hbm] * 2,
        )(in_hbm(tokens), in_hbm(grad_out))
        got = lax.ppermute(sent, "tok", swap)

        last = tile_of(half, 512)
        (in_far,) = call(
            load_body,
            "load_far",
            [like((wide, half - last), bf16)],
            grant=MIB,
            scratch=[sem((4,))],
            specs=[hbm, pl.BlockSpec(memory_space=pl.ANY)],
        )(in_hbm(weight_in), sent)
        tiles, farthest = call(
            pair_body, "pair_tiles", [like((2 * pair, wide + more), bf16) for more in (0, 128)]
        )(
            kept(own), kept(got), kept(in_far)
        )
        pieces = [across(tiles, shift) for shift in range(1, nn - 1)]
        pieces = [across(farthest, nn - 1)] + pieces + [tiles]
        in_own, in_last, own_turned, far_turned = call(
            load_and_turn_body,
            "load_own",
            [like((wide, half), bf16), like((wide, last), bf16)] + [like((half, wide), bf16)] * 2,
            grant=8 * MIB,
            scratch=[sem((2, 4))],
            specs=[hbm, pl.BlockSpec(memory_space=pl.ANY), whole],
        )(in_hbm(weight_in), tiles, kept(in_far))

        def product(body, name, outs, *args):
            return call(body, name, outs, grant=8 * MIB)(*map(kept, args))

        crossing = like((count, half + 128), bf16)
        side, ends = like((count, half), bf16), like((count, wide), f32)
        sent, x_cols, dy_cols, sums = product(
            functools.partial(far_pre_body, rows, nn),
            "far_pre",
            [side] + [like((count, wide), bf16)] * 2 + [like((1, wide), f32)],
            *pieces,
            in_far,
            in_last,
            in_own,
        )
        got = lax.ppermute(sent, "kin", swap)
        (own,) = product(own_pre_body, "own_pre", [like((count, half), f32)], x_cols, in_own, sent)
        (own_pre,) = product(add_pre_body, "add_pre", [crossing], own, got, sums)
        other_pre = lax.ppermute(own_pre, "tok", swap)
        (sent,) = product(far_grad_body, "far_grad", [side], dy_cols, weight_out, own_pre)
        got = lax.ppermute(sent, "kin", swap)
        (own,) = product(own_grad_body, "own_grad", [like((count, half), f32)], dy_cols, weight_out)
        (own_grad,) = product(add_body, "add_grad", [crossing], own, got)
        other_grad = lax.ppermute(own_grad, "tok", swap)
        slopes, act_own = call(gelu_body, "gelu", [like((count, half), f32), side])(
            bias_in.reshape(1, hid), kept(own_pre), kept(other_pre), kept(own_grad)
        )
        act_far = lax.ppermute(act_own, "kin", swap)
        forward, weight_out_grad = own_forward(act_own, dy_cols, weight_out)
        (forward,) = product(
            far_forward_body, "far_forward", [ends], act_far, weight_out, forward
        )
        (grad_own,) = call(
            grad_pre_body, "grad_pre", [side], specs=[whole] * 4 + [hbm]
        )(
            kept(slopes),
            kept(own_grad),
            kept(other_grad),
            kept(forward),
            in_hbm(weight_out_grad),
        )
        grad_far = lax.ppermute(grad_own, "kin", swap)
        (backward,) = product(own_backward_body, "own_backward", [ends], grad_own, own_turned)
        grad, *blocks = product(
            functools.partial(blocks_body, rows),
            "output_blocks",
            [like((count, hid), bf16)] + [like((2 * pair, wide), bf16)] * nn,
            grad_own,
            grad_far,
            forward,
            backward,
            far_turned,
        )

        weight_in_grad = outer(x_cols, grad, wide, "weight_in_grad", lambda size: 0)
        weight_out_grad = outer(
            act_far, dy_cols, hid, "weight_out_grad_far", far_rows, into=weight_out_grad
        )

        terms = [across(blocks[0], nn - 1)]
        terms += [across(blocks[shift], shift) for shift in reversed(range(1, nn - 1))] + [blocks[-1]]
        own, sent = call(
            functools.partial(sum_body, rows),
            "sum_blocks",
            [like((pair, wide), bf16)] * 2,
            specs=[whole] * (nn + 1) + [hbm],
        )(
            bias_out.reshape(1, cols),
            *[kept(term) for term in terms],
            in_hbm(weight_in_grad),
        )
        got = lax.ppermute(sent, "tok", swap)
        output_rows, grad_tokens, bias_out_grad, bias_in_grad = call(
            functools.partial(final_body, rows),
            "final_rows",
            [like((rows, cols), bf16)] * 2 + [like((1, cols), f32), like((1, hid), f32)],
            resident=False,
        )(kept(own), kept(got), kept(sums), kept(other_pre), kept(grad))
        return (
            output_rows,
            grad_tokens,
            weight_in_grad,
            weight_out_grad,
            bias_in_grad.reshape(hid),
            bias_out_grad.reshape(cols),
        )

    return on_device


def make_plain(nt, nk, nn):
    spread, square = nt * nn, nk * nt

    def on_device(tokens, weight_in, bias_in, weight_out, bias_out, grad_out):
        rows, cols = tokens.shape
        wide, hid = weight_in.shape
        part = hid // square
        pair = 2 * rows
        total = pair * spread

        mine = jnp.concatenate([tokens, grad_out], axis=0)
        by_owner = mine.reshape(pair, nt, wide).transpose(1, 0, 2)
        chunks = jnp.broadcast_to(by_owner[:, None], (nt, nn, pair, wide))
        mixed = exchange(chunks.reshape(spread, pair, wide), ("tok", "nout")).reshape(total, wide)
        is_fwd = (lax.broadcasted_iota(jnp.int32, (total, 1), 0) % pair) < rows

        col_sums = jnp.sum(jnp.where(is_fwd, 0.0, mixed.astype(jnp.float32)), axis=0)
        bias_out_grad = lax.all_gather(col_sums, "tok", axis=0, tiled=True)

        partial = jnp.where(is_fwd, dot(mixed, weight_in, 1, 0), dot(mixed, weight_out, 1, 1))
        partial = partial.astype(jnp.bfloat16).reshape(total, square, part).transpose(1, 0, 2)
        got = exchange(partial, ("kin", "tok"))
        summed = jnp.sum(got.astype(jnp.float32), axis=0).reshape(spread, 2, rows, part)
        at = lax.axis_index(("kin", "tok"))
        pre_act = summed[:, 0] + lax.dynamic_slice_in_dim(bias_in, at * part, part)
        activated, slopes = gelu_parts(pre_act)
        grad_pre = summed[:, 1] * slopes
        both = jnp.stack([activated, grad_pre], axis=1).astype(jnp.bfloat16).reshape(total, part)
        both = exchange(jnp.broadcast_to(both[None], (square, total, part)), ("kin", "tok"))
        both = both.transpose(1, 0, 2).reshape(total, hid)

        split = both.reshape(spread, 2, rows, hid)
        act = split[:, 0].reshape(spread * rows, hid)
        grad_half = split[:, 1].reshape(spread * rows, hid)
        split = mixed.reshape(spread, 2, rows, wide)
        x_cols = split[:, 0].reshape(spread * rows, wide)
        dy_cols = split[:, 1].reshape(spread * rows, wide)
        bias_in_grad = jnp.sum(grad_half.astype(jnp.float32), axis=0)

        block = jnp.stack(
            [
                dot(act, weight_out, 1, 0).reshape(spread, rows, wide),
                dot(grad_half, weight_in, 1, 1).reshape(spread, rows, wide),
            ],
            axis=1,
        )
        block = block.astype(jnp.bfloat16).reshape(spread, pair, wide)
        back = exchange(block, ("tok", "nout")).reshape(nt, nn, pair, wide)
        weight_in_grad = dot(x_cols, grad_half, 0, 0).astype(jnp.bfloat16)
        weight_out_grad = dot(act, dy_cols, 0, 0).astype(jnp.bfloat16)
        final = jnp.sum(back.astype(jnp.float32), axis=1).transpose(1, 0, 2).reshape(pair, cols)
        output_rows = (final[:rows] + bias_out).astype(jnp.bfloat16)
        grad_tokens = final[rows:].astype(jnp.bfloat16)
        return (output_rows, grad_tokens, weight_in_grad, weight_out_grad, bias_in_grad, bias_out_grad)

    return on_device


def solution(mesh):
    nt, nk, nn = mesh.shape["tok"], mesh.shape["kin"], mesh.shape["nout"]
    return jax.shard_map(
        make_small(nn) if (nt, nk) == (2, 2) and nn in (2, 4) else make_plain(nt, nk, nn),
        mesh=mesh,
        in_specs=(
            P(("groups", "tok", "nout"), "kin"),
            P(("kin", "tok"), "nout"),
            P("nout"),
            P("nout", ("kin", "tok")),
            P("kin"),
            P(("groups", "tok", "nout"), "kin"),
        ),
        out_specs=(
            P(("groups", "tok", "nout"), "kin"),
            P(("groups", "tok", "nout"), "kin"),
            P(("groups", "kin", "tok"), "nout"),
            P(("groups", "nout"), ("kin", "tok")),
            P(("groups", "nout")),
            P(("groups", "kin")),
        ),
        check_vma=False,
    )
```

```python
import functools

import jax
import jax.numpy as jnp
from jax import lax
from jax.experimental import pallas as pl
from jax.experimental.pallas import tpu as pltpu
from jax.sharding import PartitionSpec as P

inv_root_two = 0.7071067811865476
inv_root_two_pi = 0.3989422804014327

MIB = 1 << 20
bf16, f32 = jnp.bfloat16, jnp.float32
like = jax.ShapeDtypeStruct
whole = pl.BlockSpec(memory_space=pltpu.VMEM)
hbm = pl.BlockSpec(memory_space=pltpu.HBM)
swap = [(0, 1), (1, 0)]


def gelu_parts(hidden):
    normal_cdf = 0.5 * (1.0 + lax.erf(hidden * inv_root_two))
    density = jnp.exp(-0.5 * hidden * hidden) * inv_root_two_pi
    return (hidden * normal_cdf, normal_cdf + hidden * density)


def dot(left, right, left_dim, right_dim):
    return lax.dot_general(
        left, right, (((left_dim,), (right_dim,)), ((), ())), preferred_element_type=jnp.float32
    )


def exchange(chunks, axes):
    return lax.all_to_all(chunks, axes, split_axis=0, concat_axis=0, tiled=True)


def dot_turned(rows, weight):
    return dot(weight, rows, 1, 1).T


def tile_of(size, most):
    return max(t for t in range(128, most + 1, 128) if size % t == 0)


def tiles_of(size, most=512):
    tile = tile_of(size, most)
    return [pl.ds(i * tile, tile) for i in range(size // tile)]


def call(body, name, outs, grant=4 * MIB, flops=0, moved=0, scratch=(), resident=True, specs=None):
    shapes = [pltpu.VMEM(o.shape, o.dtype) if resident else o for o in outs]

    def run(*args):
        cost = pl.CostEstimate(flops=flops, bytes_accessed=moved, transcendentals=0)
        return pl.pallas_call(
            body,
            out_shape=shapes,
            in_specs=specs or [whole] * len(args),
            out_specs=[whole] * len(outs),
            scratch_shapes=list(scratch),
            cost_estimate=cost,
            compiler_params=pltpu.CompilerParams(vmem_limit_bytes=grant),
            name=name,
        )(*args)

    return run


def kept(array):
    return pltpu.with_memory_space_constraint(array, pltpu.VMEM)


def in_hbm(array):
    return pltpu.with_memory_space_constraint(array, pltpu.HBM)


def apart(mixed, rows):
    total, wide = mixed.shape
    tiles = mixed.reshape(total // (4 * rows), 2, 2 * rows, wide)
    even, odd = tiles[:, 0], tiles[:, 1]
    is_low = lax.broadcasted_iota(jnp.int32, even.shape, 1) < rows
    first = jnp.where(is_low, even, pltpu.roll(odd, rows, 1))
    second = jnp.where(is_low, pltpu.roll(even, rows, 1), odd)
    return first.reshape(total // 2, wide), second.reshape(total // 2, wide)


def together(first, second, rows):
    total, wide = first.shape
    first = first.reshape(total // (2 * rows), 2 * rows, wide)
    second = second.reshape(total // (2 * rows), 2 * rows, wide)
    is_low = lax.broadcasted_iota(jnp.int32, first.shape, 1) < rows
    even = jnp.where(is_low, first, pltpu.roll(second, rows, 1))
    odd = jnp.where(is_low, pltpu.roll(first, rows, 1), second)
    return jnp.stack([even, odd], axis=1).reshape(2 * total, wide)


def ordered(me, own, far, axis=0):
    low, high = jnp.where(me == 0, own, far), jnp.where(me == 0, far, own)
    return jnp.concatenate([low, high], axis=axis)


def half_of(size, mine):
    core = lax.axis_index("kin")
    at = core if mine else 1 - core
    return pl.ds(pl.multiple_of(at * size, size), size)


def own_rows(half):
    return lax.axis_index("kin") * half


def far_rows(half):
    return (1 - lax.axis_index("kin")) * half


def half_tiles(half, mine, most):
    first = own_rows(half) if mine else far_rows(half)
    tile = tile_of(half, most)
    return [
        (pl.ds(i * tile, tile), pl.ds(pl.multiple_of(first + i * tile, tile), tile))
        for i in range(half // tile)
    ]


def load_body(hbm_ref, after_ref, out_ref, sems):
    size, wide = out_ref.shape
    half = hbm_ref.shape[1] // 2
    source = pl.ds(pl.multiple_of(far_rows(half), 128), wide)
    copies = []
    for j in range(4):
        part = pl.ds(j * (size // 4), size // 4)
        copies.append(
            pltpu.make_async_copy(hbm_ref.at[part, source], out_ref.at[part, :], sems.at[j])
        )
    for copy in copies:
        copy.start()
    for copy in copies:
        copy.wait()


def load_and_turn_body(hbm_ref, after_ref, far_ref, own_ref, last_ref, own_turned, far_turned, sems):
    wide, half = own_ref.shape
    first, last = far_ref.shape[1], last_ref.shape[1]
    size = wide // 4
    parts = [pl.ds(j * size, size) for j in range(4)]
    from_own = pl.ds(pl.multiple_of(own_rows(half), 128), half)
    from_last = pl.ds(pl.multiple_of(far_rows(half) + first, 128), last)
    copies = [
        [
            pltpu.make_async_copy(hbm_ref.at[part, source], ref.at[part, :], sems.at[i, j])
            for j, part in enumerate(parts)
        ]
        for i, (source, ref) in enumerate(((from_own, own_ref), (from_last, last_ref)))
    ]
    for copy in copies[0] + copies[1]:
        copy.start()
    for part in parts:
        far_turned[:first, part] = far_ref[part, :].T
    for part, copy in zip(parts, copies[0]):
        copy.wait()
        own_turned[:, part] = own_ref[part, :].T
    for part, copy in zip(parts, copies[1]):
        copy.wait()
        far_turned[first:, part] = last_ref[part, :].T


def cut_body(tokens_hbm, grad_hbm, own_ref, sent_ref, tokens_ref, grad_ref, sems):
    me = lax.axis_index("tok")
    first = pltpu.make_async_copy(tokens_hbm, tokens_ref, sems.at[0])
    second = pltpu.make_async_copy(grad_hbm, grad_ref, sems.at[1])
    first.start()
    second.start()
    first.wait()
    second.wait()
    mine = jnp.concatenate([tokens_ref[...].astype(f32), grad_ref[...].astype(f32)], axis=0)
    wide = own_ref.shape[1]
    low, high = mine[:, :wide], mine[:, wide:]
    own_ref[...] = jnp.where(me == 0, low, high).astype(bf16)
    sent_ref[...] = jnp.where(me == 0, high, low).astype(bf16)


def pair_body(own_ref, got_ref, after_ref, out_ref):
    out_ref[...] = ordered(lax.axis_index("tok"), own_ref[...], got_ref[...])


def far_pre_body(rows, count, *refs):
    *piece_refs, w_in_ref, w_last_ref, after_ref = refs[: count + 3]
    sent_ref, x_ref, dy_ref, sums_ref = refs[count + 3 :]
    wide = x_ref.shape[1]
    mixed = jnp.concatenate([ref[:, :wide] for ref in piece_refs], axis=0)
    x_cols, dy_cols = apart(mixed.astype(f32), rows)
    sums_ref[...] = jnp.sum(dy_cols, axis=0, keepdims=True)
    x_cols, dy_cols = x_cols.astype(bf16), dy_cols.astype(bf16)
    x_ref[...], dy_ref[...] = x_cols, dy_cols
    first = w_in_ref.shape[1]
    for at in tiles_of(first):
        sent_ref[:, at] = dot(x_cols, w_in_ref[:, at], 1, 0).astype(bf16)
    sent_ref[:, first:] = dot(x_cols, w_last_ref[...], 1, 0).astype(bf16)


def own_pre_body(x_ref, w_in_ref, after_ref, own_ref):
    x_cols = x_ref[...]
    for at in tiles_of(own_ref.shape[1]):
        own_ref[:, at] = dot(x_cols, w_in_ref[:, at], 1, 0)


def far_grad_body(dy_ref, w_out_ref, after_ref, sent_ref):
    dy_cols = dy_ref[...]
    for at, there in half_tiles(sent_ref.shape[1], False, 1536):
        sent_ref[:, at] = dot_turned(dy_cols, w_out_ref[there, :]).astype(bf16)


def own_grad_body(dy_ref, w_out_ref, own_ref):
    dy_cols = dy_ref[...]
    for at, there in half_tiles(own_ref.shape[1], True, 1536):
        own_ref[:, at] = dot(dy_cols, w_out_ref[there, :], 1, 1)


def add_body(own_ref, got_ref, out_ref):
    count, half = own_ref.shape
    out_ref[:, :half] = (own_ref[...] + got_ref[...].astype(f32)).astype(bf16)
    out_ref[:, half:] = jnp.zeros((count, out_ref.shape[1] - half), bf16)


def add_pre_body(own_ref, got_ref, sums_ref, out_ref):
    count, half = own_ref.shape
    out_ref[:, :half] = (own_ref[...] + got_ref[...].astype(f32)).astype(bf16)
    sums = [sums_ref[:, at] for at in tiles_of(sums_ref.shape[1], 128)]
    sums = jnp.concatenate(sums, axis=0)
    high = sums.astype(bf16).astype(f32)
    rest = jnp.zeros((count - 2 * sums.shape[0], 128), f32)
    out_ref[:, half:] = jnp.concatenate([high, sums - high, rest], axis=0).astype(bf16)


def gelu_body(bias_ref, own_ref, other_ref, after_ref, slopes_ref, act_ref):
    half = act_ref.shape[1]
    bias = bias_ref[:, half_of(half, True)]
    tile = tile_of(half, 512)
    for i in range(half // tile):
        at = pl.ds(i * tile, tile)
        pre_act = own_ref[:, at].astype(f32) + other_ref[:, at].astype(f32)
        activated, slopes = gelu_parts(pre_act + bias[:, i * tile : (i + 1) * tile])
        slopes_ref[:, at] = slopes
        act_ref[:, at] = activated.astype(bf16)


def grad_pre_body(slopes_ref, own_ref, other_ref, after_ref, later_ref, grad_ref):
    half = pl.ds(0, grad_ref.shape[1])
    grad_act = own_ref[:, half].astype(f32) + other_ref[:, half].astype(f32)
    grad_ref[...] = (grad_act * slopes_ref[...]).astype(bf16)


def far_forward_body(far_ref, w_out_ref, terms_ref, out_ref):
    act = far_ref[...]
    part = half_of(act.shape[1], False)
    for at in tiles_of(out_ref.shape[1], 1536):
        out_ref[:, at] = terms_ref[:, at] + dot(act, w_out_ref[part, at], 1, 0)


def own_backward_body(grad_ref, turned_ref, out_ref):
    grad = grad_ref[...]
    for at in tiles_of(out_ref.shape[1]):
        out_ref[:, at] = dot(grad, turned_ref[:, at], 1, 0)


def blocks_body(rows, own_ref, far_ref, forward_ref, backward_ref, turned_ref, grad_ref, *out_refs):
    grad = far_ref[...]
    grad_ref[...] = ordered(lax.axis_index("kin"), own_ref[...], grad, 1)
    size = out_refs[0].shape[0]
    for at in tiles_of(forward_ref.shape[1]):
        backward = backward_ref[:, at] + dot(grad, turned_ref[:, at], 1, 0)
        terms = together(forward_ref[:, at], backward, rows).astype(bf16)
        for i, out_ref in enumerate(out_refs):
            out_ref[:, at] = terms[i * size : (i + 1) * size]


def outer_body(most, first_of, left_ref, right_ref, *refs):
    copies = start_outer(most, first_of, left_ref, right_ref, *refs[-3:])
    for copy in copies:
        copy.wait()


def start_outer(most, first_of, left_ref, right_ref, out_hbm, block_ref, sems):
    first = first_of(left_ref.shape[1])
    copies = []
    for i, at in enumerate(tiles_of(left_ref.shape[1], most)):
        left = left_ref[:, at].T
        for part in tiles_of(out_hbm.shape[1], 512):
            block_ref[at, part] = dot(left, right_ref[:, part], 1, 0).astype(bf16)
        there = pl.ds(pl.multiple_of(first + at.start, at.size), at.size)
        copies.append(
            pltpu.make_async_copy(block_ref.at[at, :], out_hbm.at[there, :], sems.at[i])
        )
        copies[-1].start()
    return copies


def own_forward_body(act_ref, dy_ref, w_out_ref, terms_ref, out_hbm, block_ref, sems):
    copies = start_outer(128, own_rows, act_ref, dy_ref, out_hbm, block_ref, sems)
    act = act_ref[...]
    part = half_of(act.shape[1], True)
    for at in tiles_of(terms_ref.shape[1]):
        terms_ref[:, at] = dot(act, w_out_ref[part, at], 1, 0)
    for copy in copies:
        copy.wait()


def own_forward(act, dy_cols, weight_out):
    count, half = act.shape
    hid, wide = weight_out.shape
    return pl.pallas_call(
        own_forward_body,
        out_shape=[pltpu.VMEM((count, wide), f32), like((hid, wide), bf16)],
        in_specs=[whole] * 3,
        out_specs=[whole, pl.BlockSpec(memory_space=pl.ANY)],
        scratch_shapes=[
            pltpu.VMEM((half, wide), bf16),
            pltpu.SemaphoreType.DMA((len(tiles_of(half, 128)),)),
        ],
        compiler_params=pltpu.CompilerParams(vmem_limit_bytes=16 * MIB),
        name="own_forward",
    )(kept(act), kept(dy_cols), kept(weight_out))


def outer(left, right, high, name, first_of, into=None, most=128):
    count, size = left.shape
    wide = right.shape[1]
    anywhere = pl.BlockSpec(memory_space=pl.ANY)
    return pl.pallas_call(
        functools.partial(outer_body, most, first_of),
        out_shape=like((high, wide), bf16),
        in_specs=[whole] * 2 + ([] if into is None else [anywhere]),
        out_specs=anywhere,
        scratch_shapes=[
            pltpu.VMEM((size, wide), bf16),
            pltpu.SemaphoreType.DMA((len(tiles_of(size, most)),)),
        ],
        input_output_aliases={} if into is None else {2: 0},
        compiler_params=pltpu.CompilerParams(vmem_limit_bytes=16 * MIB),
        name=name,
    )(kept(left), kept(right), *([] if into is None else [into]))


def sum_body(rows, bias_ref, *refs):
    *term_refs, after_ref, own_ref, sent_ref = refs
    wide = own_ref.shape[1]
    me = lax.axis_index("tok")
    summed = sum(ref[...].astype(f32) for ref in term_refs)
    bias = jnp.where(me == 0, bias_ref[:, :wide], bias_ref[:, wide:])
    row = lax.broadcasted_iota(jnp.int32, summed.shape, 0)
    summed = summed + jnp.where(lax.rem(row, 2 * rows) < rows, bias, 0.0)
    low, high = summed[: 2 * rows], summed[2 * rows :]
    own_ref[...] = jnp.where(me == 0, low, high).astype(bf16)
    sent_ref[...] = jnp.where(me == 0, high, low).astype(bf16)


def final_body(
    rows, own_ref, got_ref, sums_ref, other_ref, hidden_ref, rows_ref, grad_ref, out_sums_ref, bias_ref
):
    wide = own_ref.shape[1]
    me = lax.axis_index("tok")
    own, got = own_ref[...].astype(f32), got_ref[...].astype(f32)
    extra = other_ref[:, other_ref.shape[1] - 128 :].astype(f32)
    steps = wide // 128
    got_sums = extra[:steps] + extra[steps : 2 * steps]
    got_sums = jnp.concatenate([got_sums[i : i + 1] for i in range(steps)], axis=1)
    for i in range(2):
        at = pl.ds(i * wide, wide)
        part = jnp.where(me == i, own, got)
        rows_ref[:, at] = part[:rows].astype(bf16)
        grad_ref[:, at] = part[rows:].astype(bf16)
        out_sums_ref[:, at] = jnp.where(me == i, sums_ref[...], got_sums)
    bias_ref[...] = jnp.sum(hidden_ref[...].astype(f32), axis=0, keepdims=True)


def make_small(nn):
    def across(array, shift):
        return lax.ppermute(array, "nout", [(i, i ^ shift) for i in range(nn)])

    def on_device(tokens, weight_in, bias_in, weight_out, bias_out, grad_out):
        rows, cols = tokens.shape
        wide, hid = weight_in.shape
        half = hid // 2
        pair = 2 * rows
        count = 2 * nn * rows
        sem = pltpu.SemaphoreType.DMA

        own, sent = call(
            cut_body,
            "cut_tiles",
            [like((pair, wide), bf16)] * 2,
            scratch=[pltpu.VMEM((rows, cols), bf16)] * 2 + [pltpu.SemaphoreType.DMA((2,))],
            specs=[hbm] * 2,
        )(in_hbm(tokens), in_hbm(grad_out))
        got = lax.ppermute(sent, "tok", swap)

        last = tile_of(half, 512)
        (in_far,) = call(
            load_body,
            "load_far",
            [like((wide, half - last), bf16)],
            grant=MIB,
            scratch=[sem((4,))],
            specs=[hbm, pl.BlockSpec(memory_space=pl.ANY)],
        )(in_hbm(weight_in), sent)
        (tiles,) = call(pair_body, "pair_tiles", [like((2 * pair, wide), bf16)])(
            kept(own), kept(got), kept(in_far)
        )
        pieces = [across(tiles, shift) for shift in range(1, nn)] + [tiles]
        in_own, in_last, own_turned, far_turned = call(
            load_and_turn_body,
            "load_own",
            [like((wide, half), bf16), like((wide, last), bf16)] + [like((half, wide), bf16)] * 2,
            grant=8 * MIB,
            scratch=[sem((2, 4))],
            specs=[hbm, pl.BlockSpec(memory_space=pl.ANY), whole],
        )(in_hbm(weight_in), tiles, kept(in_far))

        def product(body, name, outs, *args):
            return call(body, name, outs, grant=8 * MIB)(*map(kept, args))

        crossing = like((count, half + 128), bf16)
        side, ends = like((count, half), bf16), like((count, wide), f32)
        sent, x_cols, dy_cols, sums = product(
            functools.partial(far_pre_body, rows, nn),
            "far_pre",
            [side] + [like((count, wide), bf16)] * 2 + [like((1, wide), f32)],
            *pieces,
            in_far,
            in_last,
            in_own,
        )
        got = lax.ppermute(sent, "kin", swap)
        (own,) = product(own_pre_body, "own_pre", [like((count, half), f32)], x_cols, in_own, sent)
        (own_pre,) = product(add_pre_body, "add_pre", [crossing], own, got, sums)
        other_pre = lax.ppermute(own_pre, "tok", swap)
        (sent,) = product(far_grad_body, "far_grad", [side], dy_cols, weight_out, own_pre)
        got = lax.ppermute(sent, "kin", swap)
        (own,) = product(own_grad_body, "own_grad", [like((count, half), f32)], dy_cols, weight_out)
        (own_grad,) = product(add_body, "add_grad", [crossing], own, got)
        other_grad = lax.ppermute(own_grad, "tok", swap)
        slopes, act_own = call(gelu_body, "gelu", [like((count, half), f32), side])(
            bias_in.reshape(1, hid), kept(own_pre), kept(other_pre), kept(own_grad)
        )
        act_far = lax.ppermute(act_own, "kin", swap)
        forward, weight_out_grad = own_forward(act_own, dy_cols, weight_out)
        (forward,) = product(
            far_forward_body, "far_forward", [ends], act_far, weight_out, forward
        )
        (grad_own,) = call(
            grad_pre_body, "grad_pre", [side], specs=[whole] * 4 + [hbm]
        )(
            kept(slopes),
            kept(own_grad),
            kept(other_grad),
            kept(forward),
            in_hbm(weight_out_grad),
        )
        grad_far = lax.ppermute(grad_own, "kin", swap)
        (backward,) = product(own_backward_body, "own_backward", [ends], grad_own, own_turned)
        grad, *blocks = product(
            functools.partial(blocks_body, rows),
            "output_blocks",
            [like((count, hid), bf16)] + [like((2 * pair, wide), bf16)] * nn,
            grad_own,
            grad_far,
            forward,
            backward,
            far_turned,
        )

        weight_in_grad = outer(x_cols, grad, wide, "weight_in_grad", lambda size: 0)
        weight_out_grad = outer(
            act_far, dy_cols, hid, "weight_out_grad_far", far_rows, into=weight_out_grad
        )

        terms = [across(blocks[shift - 1], shift) for shift in reversed(range(1, nn))] + [blocks[-1]]
        own, sent = call(
            functools.partial(sum_body, rows),
            "sum_blocks",
            [like((pair, wide), bf16)] * 2,
            specs=[whole] * (nn + 1) + [hbm],
        )(
            bias_out.reshape(1, cols),
            *[kept(term) for term in terms],
            in_hbm(weight_in_grad),
        )
        got = lax.ppermute(sent, "tok", swap)
        output_rows, grad_tokens, bias_out_grad, bias_in_grad = call(
            functools.partial(final_body, rows),
            "final_rows",
            [like((rows, cols), bf16)] * 2 + [like((1, cols), f32), like((1, hid), f32)],
            resident=False,
        )(kept(own), kept(got), kept(sums), kept(other_pre), kept(grad))
        return (
            output_rows,
            grad_tokens,
            weight_in_grad,
            weight_out_grad,
            bias_in_grad.reshape(hid),
            bias_out_grad.reshape(cols),
        )

    return on_device


def make_plain(nt, nk, nn):
    spread, square = nt * nn, nk * nt

    def on_device(tokens, weight_in, bias_in, weight_out, bias_out, grad_out):
        rows, cols = tokens.shape
        wide, hid = weight_in.shape
        part = hid // square
        pair = 2 * rows
        total = pair * spread

        mine = jnp.concatenate([tokens, grad_out], axis=0)
        by_owner = mine.reshape(pair, nt, wide).transpose(1, 0, 2)
        chunks = jnp.broadcast_to(by_owner[:, None], (nt, nn, pair, wide))
        mixed = exchange(chunks.reshape(spread, pair, wide), ("tok", "nout")).reshape(total, wide)
        is_fwd = (lax.broadcasted_iota(jnp.int32, (total, 1), 0) % pair) < rows

        col_sums = jnp.sum(jnp.where(is_fwd, 0.0, mixed.astype(jnp.float32)), axis=0)
        bias_out_grad = lax.all_gather(col_sums, "tok", axis=0, tiled=True)

        partial = jnp.where(is_fwd, dot(mixed, weight_in, 1, 0), dot(mixed, weight_out, 1, 1))
        partial = partial.astype(jnp.bfloat16).reshape(total, square, part).transpose(1, 0, 2)
        got = exchange(partial, ("kin", "tok"))
        summed = jnp.sum(got.astype(jnp.float32), axis=0).reshape(spread, 2, rows, part)
        at = lax.axis_index(("kin", "tok"))
        pre_act = summed[:, 0] + lax.dynamic_slice_in_dim(bias_in, at * part, part)
        activated, slopes = gelu_parts(pre_act)
        grad_pre = summed[:, 1] * slopes
        both = jnp.stack([activated, grad_pre], axis=1).astype(jnp.bfloat16).reshape(total, part)
        both = exchange(jnp.broadcast_to(both[None], (square, total, part)), ("kin", "tok"))
        both = both.transpose(1, 0, 2).reshape(total, hid)

        split = both.reshape(spread, 2, rows, hid)
        act = split[:, 0].reshape(spread * rows, hid)
        grad_half = split[:, 1].reshape(spread * rows, hid)
        split = mixed.reshape(spread, 2, rows, wide)
        x_cols = split[:, 0].reshape(spread * rows, wide)
        dy_cols = split[:, 1].reshape(spread * rows, wide)
        bias_in_grad = jnp.sum(grad_half.astype(jnp.float32), axis=0)

        block = jnp.stack(
            [
                dot(act, weight_out, 1, 0).reshape(spread, rows, wide),
                dot(grad_half, weight_in, 1, 1).reshape(spread, rows, wide),
            ],
            axis=1,
        )
        block = block.astype(jnp.bfloat16).reshape(spread, pair, wide)
        back = exchange(block, ("tok", "nout")).reshape(nt, nn, pair, wide)
        weight_in_grad = dot(x_cols, grad_half, 0, 0).astype(jnp.bfloat16)
        weight_out_grad = dot(act, dy_cols, 0, 0).astype(jnp.bfloat16)
        final = jnp.sum(back.astype(jnp.float32), axis=1).transpose(1, 0, 2).reshape(pair, cols)
        output_rows = (final[:rows] + bias_out).astype(jnp.bfloat16)
        grad_tokens = final[rows:].astype(jnp.bfloat16)
        return (output_rows, grad_tokens, weight_in_grad, weight_out_grad, bias_in_grad, bias_out_grad)

    return on_device


def solution(mesh):
    nt, nk, nn = mesh.shape["tok"], mesh.shape["kin"], mesh.shape["nout"]
    return jax.shard_map(
        make_small(nn) if (nt, nk) == (2, 2) and nn in (2, 4) else make_plain(nt, nk, nn),
        mesh=mesh,
        in_specs=(
            P(("groups", "tok", "nout"), "kin"),
            P(("kin", "tok"), "nout"),
            P("nout"),
            P("nout", ("kin", "tok")),
            P("kin"),
            P(("groups", "tok", "nout"), "kin"),
        ),
        out_specs=(
            P(("groups", "tok", "nout"), "kin"),
            P(("groups", "tok", "nout"), "kin"),
            P(("groups", "kin", "tok"), "nout"),
            P(("groups", "nout"), ("kin", "tok")),
            P(("groups", "nout")),
            P(("groups", "kin")),
        ),
        check_vma=False,
    )
```

```python
import functools

import jax
import jax.numpy as jnp
from jax import lax
from jax.experimental import pallas as pl
from jax.experimental.pallas import tpu as pltpu
from jax.sharding import PartitionSpec as P

inv_root_two = 0.7071067811865476
inv_root_two_pi = 0.3989422804014327

MIB = 1 << 20
bf16, f32 = jnp.bfloat16, jnp.float32
like = jax.ShapeDtypeStruct
whole = pl.BlockSpec(memory_space=pltpu.VMEM)
hbm = pl.BlockSpec(memory_space=pltpu.HBM)
swap = [(0, 1), (1, 0)]


def gelu_parts(hidden):
    normal_cdf = 0.5 * (1.0 + lax.erf(hidden * inv_root_two))
    density = jnp.exp(-0.5 * hidden * hidden) * inv_root_two_pi
    return (hidden * normal_cdf, normal_cdf + hidden * density)


def dot(left, right, left_dim, right_dim):
    return lax.dot_general(
        left, right, (((left_dim,), (right_dim,)), ((), ())), preferred_element_type=jnp.float32
    )


def exchange(chunks, axes):
    return lax.all_to_all(chunks, axes, split_axis=0, concat_axis=0, tiled=True)


def dot_turned(rows, weight):
    return dot(weight, rows, 1, 1).T


def tile_of(size, most):
    return max(t for t in range(128, most + 1, 128) if size % t == 0)


def tiles_of(size, most=512):
    tile = tile_of(size, most)
    return [pl.ds(i * tile, tile) for i in range(size // tile)]


def call(body, name, outs, grant=4 * MIB, flops=0, moved=0, scratch=(), resident=True, specs=None):
    shapes = [pltpu.VMEM(o.shape, o.dtype) if resident else o for o in outs]

    def run(*args):
        cost = pl.CostEstimate(flops=flops, bytes_accessed=moved, transcendentals=0)
        return pl.pallas_call(
            body,
            out_shape=shapes,
            in_specs=specs or [whole] * len(args),
            out_specs=[whole] * len(outs),
            scratch_shapes=list(scratch),
            cost_estimate=cost,
            compiler_params=pltpu.CompilerParams(vmem_limit_bytes=grant),
            name=name,
        )(*args)

    return run


def kept(array):
    return pltpu.with_memory_space_constraint(array, pltpu.VMEM)


def in_hbm(array):
    return pltpu.with_memory_space_constraint(array, pltpu.HBM)


def apart(mixed, rows):
    total, wide = mixed.shape
    tiles = mixed.reshape(total // (4 * rows), 2, 2 * rows, wide)
    even, odd = tiles[:, 0], tiles[:, 1]
    is_low = lax.broadcasted_iota(jnp.int32, even.shape, 1) < rows
    first = jnp.where(is_low, even, pltpu.roll(odd, rows, 1))
    second = jnp.where(is_low, pltpu.roll(even, rows, 1), odd)
    return first.reshape(total // 2, wide), second.reshape(total // 2, wide)


def together(first, second, rows):
    total, wide = first.shape
    first = first.reshape(total // (2 * rows), 2 * rows, wide)
    second = second.reshape(total // (2 * rows), 2 * rows, wide)
    is_low = lax.broadcasted_iota(jnp.int32, first.shape, 1) < rows
    even = jnp.where(is_low, first, pltpu.roll(second, rows, 1))
    odd = jnp.where(is_low, pltpu.roll(first, rows, 1), second)
    return jnp.stack([even, odd], axis=1).reshape(2 * total, wide)


def ordered(me, own, far, axis=0):
    low, high = jnp.where(me == 0, own, far), jnp.where(me == 0, far, own)
    return jnp.concatenate([low, high], axis=axis)


def half_of(size, mine):
    core = lax.axis_index("kin")
    at = core if mine else 1 - core
    return pl.ds(pl.multiple_of(at * size, size), size)


def own_rows(half):
    return lax.axis_index("kin") * half


def far_rows(half):
    return (1 - lax.axis_index("kin")) * half


def half_tiles(half, mine, most):
    first = own_rows(half) if mine else far_rows(half)
    tile = tile_of(half, most)
    return [
        (pl.ds(i * tile, tile), pl.ds(pl.multiple_of(first + i * tile, tile), tile))
        for i in range(half // tile)
    ]


def load_body(hbm_ref, after_ref, out_ref, sems):
    size, wide = out_ref.shape
    half = hbm_ref.shape[1] // 2
    source = pl.ds(pl.multiple_of(far_rows(half), 128), wide)
    copies = []
    for j in range(4):
        part = pl.ds(j * (size // 4), size // 4)
        copies.append(
            pltpu.make_async_copy(hbm_ref.at[part, source], out_ref.at[part, :], sems.at[j])
        )
    for copy in copies:
        copy.start()
    for copy in copies:
        copy.wait()


def load_and_turn_body(hbm_ref, after_ref, far_ref, own_ref, last_ref, own_turned, far_turned, sems):
    wide, half = own_ref.shape
    first, last = far_ref.shape[1], last_ref.shape[1]
    size = wide // 4
    parts = [pl.ds(j * size, size) for j in range(4)]
    from_own = pl.ds(pl.multiple_of(own_rows(half), 128), half)
    from_last = pl.ds(pl.multiple_of(far_rows(half) + first, 128), last)
    copies = [
        [
            pltpu.make_async_copy(hbm_ref.at[part, source], ref.at[part, :], sems.at[i, j])
            for j, part in enumerate(parts)
        ]
        for i, (source, ref) in enumerate(((from_own, own_ref), (from_last, last_ref)))
    ]
    for copy in copies[0] + copies[1]:
        copy.start()
    for part in parts:
        far_turned[:first, part] = far_ref[part, :].T
    for part, copy in zip(parts, copies[0]):
        copy.wait()
        own_turned[:, part] = own_ref[part, :].T
    for part, copy in zip(parts, copies[1]):
        copy.wait()
        far_turned[first:, part] = last_ref[part, :].T


def pair_body(own_ref, got_ref, after_ref, *out_refs):
    tiles = ordered(lax.axis_index("tok"), own_ref[...], got_ref[...])
    count, wide = tiles.shape
    for out_ref in out_refs:
        out_ref[:, :wide] = tiles
        if out_ref.shape[1] > wide:
            out_ref[:, wide:] = jnp.zeros((count, out_ref.shape[1] - wide), bf16)


def far_pre_body(rows, count, *refs):
    *piece_refs, w_in_ref, w_last_ref, after_ref = refs[: count + 3]
    sent_ref, x_ref, dy_ref, sums_ref = refs[count + 3 :]
    wide = x_ref.shape[1]
    mixed = jnp.concatenate([ref[:, :wide] for ref in piece_refs], axis=0)
    x_cols, dy_cols = apart(mixed.astype(f32), rows)
    sums_ref[...] = jnp.sum(dy_cols, axis=0, keepdims=True)
    x_cols, dy_cols = x_cols.astype(bf16), dy_cols.astype(bf16)
    x_ref[...], dy_ref[...] = x_cols, dy_cols
    first = w_in_ref.shape[1]
    for at in tiles_of(first):
        sent_ref[:, at] = dot(x_cols, w_in_ref[:, at], 1, 0).astype(bf16)
    sent_ref[:, first:] = dot(x_cols, w_last_ref[...], 1, 0).astype(bf16)


def own_pre_body(x_ref, w_in_ref, after_ref, own_ref):
    x_cols = x_ref[...]
    for at in tiles_of(own_ref.shape[1]):
        own_ref[:, at] = dot(x_cols, w_in_ref[:, at], 1, 0)


def far_grad_body(dy_ref, w_out_ref, after_ref, sent_ref):
    dy_cols = dy_ref[...]
    for at, there in half_tiles(sent_ref.shape[1], False, 1536):
        sent_ref[:, at] = dot_turned(dy_cols, w_out_ref[there, :]).astype(bf16)


def own_grad_body(dy_ref, w_out_ref, own_ref):
    dy_cols = dy_ref[...]
    for at, there in half_tiles(own_ref.shape[1], True, 1536):
        own_ref[:, at] = dot(dy_cols, w_out_ref[there, :], 1, 1)


def add_body(own_ref, got_ref, out_ref):
    count, half = own_ref.shape
    out_ref[:, :half] = (own_ref[...] + got_ref[...].astype(f32)).astype(bf16)
    out_ref[:, half:] = jnp.zeros((count, out_ref.shape[1] - half), bf16)


def add_pre_body(own_ref, got_ref, sums_ref, out_ref):
    count, half = own_ref.shape
    out_ref[:, :half] = (own_ref[...] + got_ref[...].astype(f32)).astype(bf16)
    sums = [sums_ref[:, at] for at in tiles_of(sums_ref.shape[1], 128)]
    sums = jnp.concatenate(sums, axis=0)
    high = sums.astype(bf16).astype(f32)
    rest = jnp.zeros((count - 2 * sums.shape[0], 128), f32)
    out_ref[:, half:] = jnp.concatenate([high, sums - high, rest], axis=0).astype(bf16)


def gelu_body(bias_ref, own_ref, other_ref, after_ref, slopes_ref, act_ref):
    half = act_ref.shape[1]
    bias = bias_ref[:, half_of(half, True)]
    tile = tile_of(half, 512)
    for i in range(half // tile):
        at = pl.ds(i * tile, tile)
        pre_act = own_ref[:, at].astype(f32) + other_ref[:, at].astype(f32)
        activated, slopes = gelu_parts(pre_act + bias[:, i * tile : (i + 1) * tile])
        slopes_ref[:, at] = slopes
        act_ref[:, at] = activated.astype(bf16)


def grad_pre_body(slopes_ref, own_ref, other_ref, after_ref, later_ref, grad_ref):
    half = pl.ds(0, grad_ref.shape[1])
    grad_act = own_ref[:, half].astype(f32) + other_ref[:, half].astype(f32)
    grad_ref[...] = (grad_act * slopes_ref[...]).astype(bf16)


def far_forward_body(far_ref, w_out_ref, terms_ref, out_ref):
    act = far_ref[...]
    part = half_of(act.shape[1], False)
    for at in tiles_of(out_ref.shape[1], 1536):
        out_ref[:, at] = terms_ref[:, at] + dot(act, w_out_ref[part, at], 1, 0)


def own_backward_body(grad_ref, turned_ref, out_ref):
    grad = grad_ref[...]
    for at in tiles_of(out_ref.shape[1]):
        out_ref[:, at] = dot(grad, turned_ref[:, at], 1, 0)


def blocks_body(rows, own_ref, far_ref, forward_ref, backward_ref, turned_ref, grad_ref, *out_refs):
    grad = far_ref[...]
    grad_ref[...] = ordered(lax.axis_index("kin"), own_ref[...], grad, 1)
    size = out_refs[0].shape[0]
    for at in tiles_of(forward_ref.shape[1]):
        backward = backward_ref[:, at] + dot(grad, turned_ref[:, at], 1, 0)
        terms = together(forward_ref[:, at], backward, rows).astype(bf16)
        for i, out_ref in enumerate(out_refs):
            out_ref[:, at] = terms[i * size : (i + 1) * size]


def outer_body(most, first_of, left_ref, right_ref, *refs):
    copies = start_outer(most, first_of, left_ref, right_ref, *refs[-3:])
    for copy in copies:
        copy.wait()


def start_outer(most, first_of, left_ref, right_ref, out_hbm, block_ref, sems):
    first = first_of(left_ref.shape[1])
    copies = []
    for i, at in enumerate(tiles_of(left_ref.shape[1], most)):
        left = left_ref[:, at].T
        for part in tiles_of(out_hbm.shape[1], 1536):
            block_ref[at, part] = dot(left, right_ref[:, part], 1, 0).astype(bf16)
        there = pl.ds(pl.multiple_of(first + at.start, at.size), at.size)
        copies.append(
            pltpu.make_async_copy(block_ref.at[at, :], out_hbm.at[there, :], sems.at[i])
        )
        copies[-1].start()
    return copies


def own_forward_body(act_ref, dy_ref, w_out_ref, terms_ref, out_hbm, block_ref, sems):
    copies = start_outer(128, own_rows, act_ref, dy_ref, out_hbm, block_ref, sems)
    act = act_ref[...]
    part = half_of(act.shape[1], True)
    for at in tiles_of(terms_ref.shape[1]):
        terms_ref[:, at] = dot(act, w_out_ref[part, at], 1, 0)
    for copy in copies:
        copy.wait()


def own_forward(act, dy_cols, weight_out):
    count, half = act.shape
    hid, wide = weight_out.shape
    return pl.pallas_call(
        own_forward_body,
        out_shape=[pltpu.VMEM((count, wide), f32), like((hid, wide), bf16)],
        in_specs=[whole] * 3,
        out_specs=[whole, pl.BlockSpec(memory_space=pl.ANY)],
        scratch_shapes=[
            pltpu.VMEM((half, wide), bf16),
            pltpu.SemaphoreType.DMA((len(tiles_of(half, 128)),)),
        ],
        compiler_params=pltpu.CompilerParams(vmem_limit_bytes=16 * MIB),
        name="own_forward",
    )(kept(act), kept(dy_cols), kept(weight_out))


def outer(left, right, high, name, first_of, into=None, most=128):
    count, size = left.shape
    wide = right.shape[1]
    anywhere = pl.BlockSpec(memory_space=pl.ANY)
    return pl.pallas_call(
        functools.partial(outer_body, most, first_of),
        out_shape=like((high, wide), bf16),
        in_specs=[whole] * 2 + ([] if into is None else [anywhere]),
        out_specs=anywhere,
        scratch_shapes=[
            pltpu.VMEM((size, wide), bf16),
            pltpu.SemaphoreType.DMA((len(tiles_of(size, most)),)),
        ],
        input_output_aliases={} if into is None else {2: 0},
        compiler_params=pltpu.CompilerParams(vmem_limit_bytes=16 * MIB),
        name=name,
    )(kept(left), kept(right), *([] if into is None else [into]))


def sum_body(rows, bias_ref, *refs):
    *term_refs, after_ref, own_ref, sent_ref = refs
    wide = own_ref.shape[1]
    me = lax.axis_index("tok")
    summed = sum(ref[...].astype(f32) for ref in term_refs)
    bias = jnp.where(me == 0, bias_ref[:, :wide], bias_ref[:, wide:])
    row = lax.broadcasted_iota(jnp.int32, summed.shape, 0)
    summed = summed + jnp.where(lax.rem(row, 2 * rows) < rows, bias, 0.0)
    low, high = summed[: 2 * rows], summed[2 * rows :]
    own_ref[...] = jnp.where(me == 0, low, high).astype(bf16)
    sent_ref[...] = jnp.where(me == 0, high, low).astype(bf16)


def final_body(
    rows, own_ref, got_ref, sums_ref, other_ref, hidden_ref, rows_ref, grad_ref, out_sums_ref, bias_ref
):
    wide = own_ref.shape[1]
    me = lax.axis_index("tok")
    own, got = own_ref[...].astype(f32), got_ref[...].astype(f32)
    extra = other_ref[:, other_ref.shape[1] - 128 :].astype(f32)
    steps = wide // 128
    got_sums = extra[:steps] + extra[steps : 2 * steps]
    got_sums = jnp.concatenate([got_sums[i : i + 1] for i in range(steps)], axis=1)
    for i in range(2):
        at = pl.ds(i * wide, wide)
        part = jnp.where(me == i, own, got)
        rows_ref[:, at] = part[:rows].astype(bf16)
        grad_ref[:, at] = part[rows:].astype(bf16)
        out_sums_ref[:, at] = jnp.where(me == i, sums_ref[...], got_sums)
    bias_ref[...] = jnp.sum(hidden_ref[...].astype(f32), axis=0, keepdims=True)


def make_small(nn):
    def across(array, shift):
        return lax.ppermute(array, "nout", [(i, i ^ shift) for i in range(nn)])

    def on_device(tokens, weight_in, bias_in, weight_out, bias_out, grad_out):
        rows, cols = tokens.shape
        wide, hid = weight_in.shape
        half = hid // 2
        pair = 2 * rows
        count = 2 * nn * rows
        sem = pltpu.SemaphoreType.DMA

        mine = jnp.concatenate([tokens, grad_out], axis=0)
        me = lax.axis_index("tok")
        own = lax.dynamic_slice_in_dim(mine, me * wide, wide, 1)
        sent = lax.dynamic_slice_in_dim(mine, (1 - me) * wide, wide, 1)
        got = lax.ppermute(sent, "tok", swap)

        last = tile_of(half, 512)
        (in_far,) = call(
            load_body,
            "load_far",
            [like((wide, half - last), bf16)],
            grant=MIB,
            scratch=[sem((4,))],
            specs=[hbm, pl.BlockSpec(memory_space=pl.ANY)],
        )(in_hbm(weight_in), sent)
        tiles, farthest = call(
            pair_body, "pair_tiles", [like((2 * pair, wide + more), bf16) for more in (0, 128)]
        )(
            kept(own), kept(got), kept(in_far)
        )
        pieces = [across(tiles, shift) for shift in range(1, nn - 1)]
        pieces = [across(farthest, nn - 1)] + pieces[::-1] + [tiles]
        in_own, in_last, own_turned, far_turned = call(
            load_and_turn_body,
            "load_own",
            [like((wide, half), bf16), like((wide, last), bf16)] + [like((half, wide), bf16)] * 2,
            grant=8 * MIB,
            scratch=[sem((2, 4))],
            specs=[hbm, pl.BlockSpec(memory_space=pl.ANY), whole],
        )(in_hbm(weight_in), tiles, kept(in_far))

        def product(body, name, outs, *args):
            return call(body, name, outs, grant=8 * MIB)(*map(kept, args))

        crossing = like((count, half + 128), bf16)
        side, ends = like((count, half), bf16), like((count, wide), f32)
        sent, x_cols, dy_cols, sums = product(
            functools.partial(far_pre_body, rows, nn),
            "far_pre",
            [side] + [like((count, wide), bf16)] * 2 + [like((1, wide), f32)],
            *pieces,
            in_far,
            in_last,
            in_own,
        )
        got = lax.ppermute(sent, "kin", swap)
        (own,) = product(own_pre_body, "own_pre", [like((count, half), f32)], x_cols, in_own, sent)
        (own_pre,) = product(add_pre_body, "add_pre", [crossing], own, got, sums)
        other_pre = lax.ppermute(own_pre, "tok", swap)
        (sent,) = product(far_grad_body, "far_grad", [side], dy_cols, weight_out, own_pre)
        got = lax.ppermute(sent, "kin", swap)
        (own,) = product(own_grad_body, "own_grad", [like((count, half), f32)], dy_cols, weight_out)
        (own_grad,) = product(add_body, "add_grad", [crossing], own, got)
        other_grad = lax.ppermute(own_grad, "tok", swap)
        slopes, act_own = call(gelu_body, "gelu", [like((count, half), f32), side])(
            bias_in.reshape(1, hid), kept(own_pre), kept(other_pre), kept(own_grad)
        )
        act_far = lax.ppermute(act_own, "kin", swap)
        forward, weight_out_grad = own_forward(act_own, dy_cols, weight_out)
        (forward,) = product(
            far_forward_body, "far_forward", [ends], act_far, weight_out, forward
        )
        (grad_own,) = call(
            grad_pre_body, "grad_pre", [side], specs=[whole] * 4 + [hbm]
        )(
            kept(slopes),
            kept(own_grad),
            kept(other_grad),
            kept(forward),
            in_hbm(weight_out_grad),
        )
        grad_far = lax.ppermute(grad_own, "kin", swap)
        (backward,) = product(own_backward_body, "own_backward", [ends], grad_own, own_turned)
        grad, *blocks = product(
            functools.partial(blocks_body, rows),
            "output_blocks",
            [like((count, hid), bf16)] + [like((2 * pair, wide), bf16)] * nn,
            grad_own,
            grad_far,
            forward,
            backward,
            far_turned,
        )

        weight_in_grad = outer(x_cols, grad, wide, "weight_in_grad", lambda size: 0)
        weight_out_grad = outer(
            act_far, dy_cols, hid, "weight_out_grad_far", far_rows, into=weight_out_grad
        )

        terms = [across(blocks[i], nn - 1 - i) for i in range(nn - 1)] + [blocks[-1]]
        own, sent = call(
            functools.partial(sum_body, rows),
            "sum_blocks",
            [like((pair, wide), bf16)] * 2,
            specs=[whole] * (nn + 1) + [hbm],
        )(
            bias_out.reshape(1, cols),
            *[kept(term) for term in terms],
            in_hbm(weight_in_grad),
        )
        got = lax.ppermute(sent, "tok", swap)
        output_rows, grad_tokens, bias_out_grad, bias_in_grad = call(
            functools.partial(final_body, rows),
            "final_rows",
            [like((rows, cols), bf16)] * 2 + [like((1, cols), f32), like((1, hid), f32)],
            resident=False,
        )(kept(own), kept(got), kept(sums), kept(other_pre), kept(grad))
        return (
            output_rows,
            grad_tokens,
            weight_in_grad,
            weight_out_grad,
            bias_in_grad.reshape(hid),
            bias_out_grad.reshape(cols),
        )

    return on_device


def make_plain(nt, nk, nn):
    spread, square = nt * nn, nk * nt

    def on_device(tokens, weight_in, bias_in, weight_out, bias_out, grad_out):
        rows, cols = tokens.shape
        wide, hid = weight_in.shape
        part = hid // square
        pair = 2 * rows
        total = pair * spread

        mine = jnp.concatenate([tokens, grad_out], axis=0)
        by_owner = mine.reshape(pair, nt, wide).transpose(1, 0, 2)
        chunks = jnp.broadcast_to(by_owner[:, None], (nt, nn, pair, wide))
        mixed = exchange(chunks.reshape(spread, pair, wide), ("tok", "nout")).reshape(total, wide)
        is_fwd = (lax.broadcasted_iota(jnp.int32, (total, 1), 0) % pair) < rows

        col_sums = jnp.sum(jnp.where(is_fwd, 0.0, mixed.astype(jnp.float32)), axis=0)
        bias_out_grad = lax.all_gather(col_sums, "tok", axis=0, tiled=True)

        partial = jnp.where(is_fwd, dot(mixed, weight_in, 1, 0), dot(mixed, weight_out, 1, 1))
        partial = partial.astype(jnp.bfloat16).reshape(total, square, part).transpose(1, 0, 2)
        got = exchange(partial, ("kin", "tok"))
        summed = jnp.sum(got.astype(jnp.float32), axis=0).reshape(spread, 2, rows, part)
        at = lax.axis_index(("kin", "tok"))
        pre_act = summed[:, 0] + lax.dynamic_slice_in_dim(bias_in, at * part, part)
        activated, slopes = gelu_parts(pre_act)
        grad_pre = summed[:, 1] * slopes
        both = jnp.stack([activated, grad_pre], axis=1).astype(jnp.bfloat16).reshape(total, part)
        both = exchange(jnp.broadcast_to(both[None], (square, total, part)), ("kin", "tok"))
        both = both.transpose(1, 0, 2).reshape(total, hid)

        split = both.reshape(spread, 2, rows, hid)
        act = split[:, 0].reshape(spread * rows, hid)
        grad_half = split[:, 1].reshape(spread * rows, hid)
        split = mixed.reshape(spread, 2, rows, wide)
        x_cols = split[:, 0].reshape(spread * rows, wide)
        dy_cols = split[:, 1].reshape(spread * rows, wide)
        bias_in_grad = jnp.sum(grad_half.astype(jnp.float32), axis=0)

        block = jnp.stack(
            [
                dot(act, weight_out, 1, 0).reshape(spread, rows, wide),
                dot(grad_half, weight_in, 1, 1).reshape(spread, rows, wide),
            ],
            axis=1,
        )
        block = block.astype(jnp.bfloat16).reshape(spread, pair, wide)
        back = exchange(block, ("tok", "nout")).reshape(nt, nn, pair, wide)
        weight_in_grad = dot(x_cols, grad_half, 0, 0).astype(jnp.bfloat16)
        weight_out_grad = dot(act, dy_cols, 0, 0).astype(jnp.bfloat16)
        final = jnp.sum(back.astype(jnp.float32), axis=1).transpose(1, 0, 2).reshape(pair, cols)
        output_rows = (final[:rows] + bias_out).astype(jnp.bfloat16)
        grad_tokens = final[rows:].astype(jnp.bfloat16)
        return (output_rows, grad_tokens, weight_in_grad, weight_out_grad, bias_in_grad, bias_out_grad)

    return on_device


def solution(mesh):
    nt, nk, nn = mesh.shape["tok"], mesh.shape["kin"], mesh.shape["nout"]
    return jax.shard_map(
        make_small(nn) if (nt, nk) == (2, 2) and nn in (2, 4) else make_plain(nt, nk, nn),
        mesh=mesh,
        in_specs=(
            P(("groups", "tok", "nout"), "kin"),
            P(("kin", "tok"), "nout"),
            P("nout"),
            P("nout", ("kin", "tok")),
            P("kin"),
            P(("groups", "tok", "nout"), "kin"),
        ),
        out_specs=(
            P(("groups", "tok", "nout"), "kin"),
            P(("groups", "tok", "nout"), "kin"),
            P(("groups", "kin", "tok"), "nout"),
            P(("groups", "nout"), ("kin", "tok")),
            P(("groups", "nout")),
            P(("groups", "kin")),
        ),
        check_vma=False,
    )
```
